32 devices in a mesh: groups: 2 (over y), dp: 4 (over z), sub: 2 (over x), pair: 2 (over core).
Axes of the slice: x: 2, y: 2, z: 4, core: 2. Of those that a mesh axis runs over, the one named last changes fastest.
Arguments:
- inputs: bfloat16 [16384, 2048], P(('groups', 'dp', 'sub', 'pair')), parts along dimension 0, may hold values from -6 to 6
- cotangent: bfloat16 [16384, 256], P(('groups', 'dp', 'sub', 'pair')), parts along dimension 0, may hold values from -0.25 to 0.25
- error_prev: bfloat16 [32, 2048, 256], P(('groups', 'dp', 'sub', 'pair')), parts along dimension 0, may hold values from -16 to 16
- seed_q: float32 [32, 256], replicated, may hold values from -6 to 6
Outputs:
- error_next: bfloat16 [32, 2048, 256], P(('groups', 'dp', 'sub', 'pair')), parts along dimension 0
- basis: float32 [64, 2048], P('groups'), parts along dimension 0
- second: float32 [64, 256], P('groups'), parts along dimension 0
The draws below stay inside these ranges and needn't reach their ends.
There are 2 independent parts, one for each index of `groups`. The reference program is written for one: setup_inputs(seed, part) draws one part's arguments, and reference() takes and returns one part's arrays. A program takes and returns all parts, laid end to end along the dimension named above; an argument that names none is the same for every part. Nothing has to cross between parts.
All inputs are finite; a program needn't handle non-finite values.
Results may differ from the reference program's by a relative error of at most 0.001.
Values sent between devices are 32-bit elements; how exact they have to be, the bound alone decides.
No kernel may reach another device: no remote copies, remote signals or barrier semaphores. Data moves between devices by JAX's collectives and lax.ppermute only.
A program may use at most 64 MiB of HBM per device.

```python
import math
import jax
import jax.numpy as jnp
from jax import lax

IN = 2048
OUT = 256
RANK = 32
TOK_DEV = 512
WORKERS = 16
ROWS = 8192


def spread_scales(key, count, low, high):
    return low * jnp.exp(jax.random.uniform(key, (count,), jnp.float32) * math.log(high / low))


def draw_error_prev(key, part):
    key = jax.random.fold_in(key, 7)
    k_row, k_col, k_common, k_noise = jax.random.split(key, 4)
    row_scale = spread_scales(k_row, IN, 0.5, 2.0)
    col_scale = spread_scales(k_col, OUT, 0.5, 2.0)
    common = 0.6 * jnp.clip(jax.random.normal(k_common, (IN, OUT), jnp.float32), -4.0, 4.0)
    noise = jnp.clip(jax.random.normal(k_noise, (WORKERS, IN, OUT), jnp.float32), -4.0, 4.0)
    field = row_scale[:, None] * col_scale[None, :] * common
    return jnp.clip(field[None, :, :] + noise, -16.0, 16.0).astype(jnp.bfloat16)


def steps_of(own_key, shape, cuts, low, top_value):
    def one(dim, blocks):
        steps = jax.random.uniform(jax.random.fold_in(jax.random.fold_in(own_key, 6), dim), (blocks,), jnp.float32, low / len(cuts), top_value / len(cuts))
        return jnp.repeat(jnp.exp(steps), shape[dim] // blocks).reshape((-1,) + (1,) * (len(shape) - dim - 1))

    loudness = one(*cuts[0])
    for cut in cuts[1:]:
        loudness = loudness * one(*cut)
    return loudness


def centred(key, extent, spread, limit, cuts=(), held_as=jnp.bfloat16):
    result = jax.random.normal(key, extent, jnp.float32) * spread
    if len(cuts) > 0:
        result = steps_of(key, extent, cuts, -0.22, 0.18) * result
    return jnp.clip(result, min=-limit, max=limit).astype(held_as)


def setup_inputs(seed: int = 0, part: int = 0) -> dict:
    key_of = jax.random.split(jax.random.key(seed), 5)
    part_splits = jax.random.split(jax.random.fold_in(key_of[4], part), 5)
    return {
        "inputs": centred(part_splits[0], (ROWS, IN), 1.0, 6.0, ((0, 16),)),
        "cotangent": centred(part_splits[1], (ROWS, OUT), TOK_DEV ** -0.5, 0.25, ((0, 16),)),
        "error_prev": draw_error_prev(jax.random.fold_in(jax.random.fold_in(key_of[4], part), 71), part),
        "seed_q": centred(key_of[3], (RANK, OUT), 1.0, 6.0, (), jnp.float32),
    }


def reference(inputs, cotangent, error_prev, seed_q):
    workers = error_prev.shape[0]
    x_blocks = inputs.reshape(workers, TOK_DEV, IN)
    c_blocks = cotangent.reshape(workers, TOK_DEV, OUT)

    def local(args):
        x_block, c_block, e_block = args
        return jnp.dot(x_block.T.astype(jnp.float32), c_block.astype(jnp.float32), preferred_element_type=jnp.float32) + e_block.astype(jnp.float32)
    merged = lax.map(local, (x_blocks, c_blocks, error_prev))
    total = jnp.sum(merged, axis=0)
    first = jnp.dot(seed_q, total.T, precision=lax.Precision.HIGHEST)
    qmat, rmat = jnp.linalg.qr(first.T)
    signs = jnp.where(jnp.diagonal(rmat) < 0, -1.0, 1.0)
    basis = (qmat * signs[None, :]).T
    second = jnp.dot(basis, total, precision=lax.Precision.HIGHEST) / workers
    approx = jnp.dot(basis.T, second, precision=lax.Precision.HIGHEST)
    error_next = (merged - approx[None]).astype(jnp.bfloat16)
    return (error_next, basis, second)
```

```python
import jax
import jax.numpy as jnp
from jax import lax
from jax.sharding import PartitionSpec as P

AXES = ("dp", "sub", "pair")
HIGHEST = lax.Precision.HIGHEST


def split_axes(mesh):
    direct, count = (), 1
    for axis in AXES:
        if count * mesh.shape[axis] <= 16:
            direct, count = direct + (axis,), count * mesh.shape[axis]
    rest = tuple(axis for axis in AXES if axis not in direct)
    return direct, rest, count


def exchange(block, shift, direct, count):
    return lax.ppermute(block, direct, [(i, (i + shift) % count) for i in range(count)])


def local(direct, rest, count, workers, inputs, cotangent, error_prev, seed_q):
    merged = lax.dot_general(
        inputs, cotangent, (((0,), (0,)), ((), ())), preferred_element_type=jnp.float32
    )
    merged = merged + error_prev[0].astype(jnp.float32)
    term = lax.dot_general(seed_q, merged, (((1,), (1,)), ((), ())), precision=HIGHEST)
    if rest:
        term = lax.psum(term, rest)
    me = lax.axis_index(direct)
    rank, width = term.shape
    piece = width // count
    pieces = term.reshape(rank, count, piece).transpose(1, 0, 2)
    pieces = jnp.roll(pieces, -me, axis=0)
    chunk = pieces[0]
    for shift in range(1, count):
        chunk = chunk + exchange(pieces[shift], shift, direct, count)
    chunks = [chunk] + [exchange(chunk, shift, direct, count) for shift in range(1, count)]
    first = jnp.roll(jnp.stack(chunks[::-1]), me + 1, axis=0)
    first = first.transpose(1, 0, 2).reshape(rank, width)

    product = jnp.dot(first, merged, precision=HIGHEST)
    if rest:
        product = lax.psum(product, rest)
    slim = product.shape[0] // count
    rows = product.reshape(count, slim, product.shape[1])
    rows = jnp.roll(rows, -me, axis=0)
    own = rows[0]
    for shift in range(1, count):
        own = own + exchange(rows[shift], shift, direct, count)
    owns = [own] + [exchange(own, shift, direct, count) for shift in range(1, count)]
    product = jnp.roll(jnp.stack(owns[::-1]), me + 1, axis=0).reshape(product.shape)

    basis = first
    for sweep in range(2):
        gram = jnp.dot(basis, basis.T, precision=HIGHEST)
        lower = jnp.linalg.cholesky(gram)
        basis = jax.scipy.linalg.solve_triangular(lower, basis, lower=True)
        product = jax.scipy.linalg.solve_triangular(lower, product, lower=True)
    second = product / workers
    approx = lax.dot_general(basis, second, (((0,), (0,)), ((), ())), precision=HIGHEST)
    error_next = (merged - approx).astype(jnp.bfloat16)[None]
    return (error_next, basis, second)


def solution(mesh):
    direct, rest, count = split_axes(mesh)
    workers = 1
    for axis in AXES:
        workers *= mesh.shape[axis]
    everyone = ("groups",) + AXES

    def run(*args):
        return local(direct, rest, count, workers, *args)

    return jax.shard_map(
        run,
        mesh=mesh,
        in_specs=(P(everyone, None), P(everyone, None), P(everyone, None, None), P()),
        out_specs=(P(everyone, None, None), P("groups", None), P("groups", None)),
        check_vma=False,
    )
```

```python
import jax
import jax.numpy as jnp
from jax import lax
from jax.sharding import PartitionSpec as P

AXES = ("dp", "sub", "pair")
HIGHEST = lax.Precision.HIGHEST


def split_axes(mesh):
    direct, count = (), 1
    for axis in AXES:
        if count * mesh.shape[axis] <= 16:
            direct, count = direct + (axis,), count * mesh.shape[axis]
    rest = tuple(axis for axis in AXES if axis not in direct)
    return direct, rest, count


def swap(pieces, direct):
    return lax.all_to_all(pieces, direct, 0, 0, tiled=True)


def total_of(pieces, direct):
    own = jnp.sum(swap(pieces, direct), axis=0)
    return swap(jnp.broadcast_to(own[None], pieces.shape), direct)


def local(direct, rest, count, workers, inputs, cotangent, error_prev, seed_q):
    merged = lax.dot_general(
        inputs, cotangent, (((0,), (0,)), ((), ())), preferred_element_type=jnp.float32
    )
    merged = merged + error_prev[0].astype(jnp.float32)
    term = lax.dot_general(seed_q, merged, (((1,), (1,)), ((), ())), precision=HIGHEST)
    if rest:
        term = lax.psum(term, rest)
    rank, width = term.shape
    pieces = term.reshape(rank, count, width // count).transpose(1, 0, 2)
    first = total_of(pieces, direct).transpose(1, 0, 2).reshape(rank, width)

    product = jnp.dot(first, merged, precision=HIGHEST)
    if rest:
        product = lax.psum(product, rest)
    rows = product.reshape(count, -1, product.shape[1])
    product = total_of(rows, direct).reshape(product.shape)

    basis = first
    for sweep in range(2):
        gram = jnp.dot(basis, basis.T, precision=HIGHEST)
        lower = jnp.linalg.cholesky(gram)
        basis = jax.scipy.linalg.solve_triangular(lower, basis, lower=True)
        product = jax.scipy.linalg.solve_triangular(lower, product, lower=True)
    second = product / workers
    approx = lax.dot_general(basis, second, (((0,), (0,)), ((), ())), precision=HIGHEST)
    error_next = (merged - approx).astype(jnp.bfloat16)[None]
    return (error_next, basis, second)


def solution(mesh):
    direct, rest, count = split_axes(mesh)
    workers = 1
    for axis in AXES:
        workers *= mesh.shape[axis]
    everyone = ("groups",) + AXES

    def run(*args):
        return local(direct, rest, count, workers, *args)

    return jax.shard_map(
        run,
        mesh=mesh,
        in_specs=(P(everyone, None), P(everyone, None), P(everyone, None, None), P()),
        out_specs=(P(everyone, None, None), P("groups", None), P("groups", None)),
        check_vma=False,
    )
```

```python
import jax
import jax.numpy as jnp
from jax import lax
from jax.sharding import PartitionSpec as P

NEAR = ("sub", "pair")
FAR = ("dp",)
EVERYONE = ("groups",) + FAR + NEAR
HIGHEST = lax.Precision.HIGHEST


def swap(pieces, axes):
    return lax.all_to_all(pieces, axes, 0, 0, tiled=True)


def copies(block, axes, count):
    return swap(jnp.broadcast_to(block[None], (count,) + block.shape), axes)


def local(near, far, inputs, cotangent, error_prev, seed_q):
    merged = lax.dot_general(
        inputs, cotangent, (((0,), (0,)), ((), ())), preferred_element_type=jnp.float32
    )
    merged = merged + error_prev[0].astype(jnp.float32)
    term = lax.dot_general(seed_q, merged, (((1,), (1,)), ((), ())), precision=HIGHEST)
    rank, width = term.shape
    pieces = term.reshape(rank, near, width // near).transpose(1, 0, 2)
    part = jnp.sum(swap(pieces, NEAR), axis=0)
    chunk = jnp.sum(copies(part, FAR, far), axis=0)
    first = copies(chunk, NEAR, near).transpose(1, 0, 2).reshape(rank, width)

    product = jnp.dot(first, merged, precision=HIGHEST)
    product = jnp.sum(copies(product, NEAR, near), axis=0)
    product = jnp.sum(copies(product, FAR, far), axis=0)

    basis = first
    for sweep in range(2):
        gram = jnp.dot(basis, basis.T, precision=HIGHEST)
        lower = jnp.linalg.cholesky(gram)
        basis = jax.scipy.linalg.solve_triangular(lower, basis, lower=True)
        product = jax.scipy.linalg.solve_triangular(lower, product, lower=True)
    second = product / (near * far)
    approx = lax.dot_general(basis, second, (((0,), (0,)), ((), ())), precision=HIGHEST)
    error_next = (merged - approx).astype(jnp.bfloat16)[None]
    return (error_next, basis, second)


def solution(mesh):
    near = mesh.shape["sub"] * mesh.shape["pair"]
    far = mesh.shape["dp"]

    def run(*args):
        return local(near, far, *args)

    return jax.shard_map(
        run,
        mesh=mesh,
        in_specs=(P(EVERYONE, None), P(EVERYONE, None), P(EVERYONE, None, None), P()),
        out_specs=(P(EVERYONE, None, None), P("groups", None), P("groups", None)),
        check_vma=False,
    )
```

```python
import functools

import jax
import jax.numpy as jnp
from jax import lax
from jax.experimental import pallas as pl
from jax.experimental.pallas import tpu as pltpu
from jax.sharding import PartitionSpec as P

AXES = ("dp", "sub", "pair")
EVERYONE = ("groups",) + AXES
VMEM_BYTES = 24 * 1024 * 1024
BF16, F32 = jnp.bfloat16, jnp.float32


def split_axes(mesh):
    direct, count = (), 1
    for axis in AXES:
        if count * mesh.shape[axis] <= 16:
            direct, count = direct + (axis,), count * mesh.shape[axis]
    rest = tuple(axis for axis in AXES if axis not in direct)
    return direct, rest, count


def swap(pieces, direct):
    return lax.all_to_all(pieces, direct, 0, 0, tiled=True)


def parts_of(value, count):
    parts = []
    for _ in range(count):
        part = value.astype(BF16)
        parts.append(part)
        value = value - part.astype(F32)
    return parts


def dot(a, b, dims):
    return lax.dot_general(a, b, (dims, ((), ())), preferred_element_type=F32)


def params(semantics=None):
    return pltpu.CompilerParams(dimension_semantics=semantics, vmem_limit_bytes=VMEM_BYTES)


def cost(flops, nbytes):
    return pl.CostEstimate(flops=flops, bytes_accessed=nbytes, transcendentals=0)


def merge_kernel(x_ref, c_ref, e_ref, seed_ref, merged_ref, pieces_ref):
    merged = dot(x_ref[...], c_ref[...], ((0,), (0,))) + e_ref[0].astype(F32)
    merged_ref[...] = merged
    rank = seed_ref.shape[0]
    m_high, m_low = parts_of(merged, 2)
    s_high, s_low = parts_of(seed_ref[...], 2)
    both = dot(jnp.concatenate([s_high, s_low], axis=0), m_high, ((1,), (1,)))
    term = both[:rank] + both[rank:] + dot(s_high, m_low, ((1,), (1,)))
    piece = pieces_ref.shape[2]
    for i in range(pieces_ref.shape[0]):
        pieces_ref[i] = term[:, i * piece:(i + 1) * piece]


def merge(inputs, cotangent, error_prev, seed_q, count):
    tokens, width = inputs.shape
    out = cotangent.shape[1]
    rank = seed_q.shape[0]
    piece = width // count
    block = max(piece, 512)
    per = block // piece
    return pl.pallas_call(
        merge_kernel,
        grid=(width // block,),
        in_specs=[
            pl.BlockSpec((tokens, block), lambda i: (0, i)),
            pl.BlockSpec((tokens, out), lambda i: (0, 0)),
            pl.BlockSpec((1, block, out), lambda i: (0, i, 0)),
            pl.BlockSpec((rank, out), lambda i: (0, 0)),
        ],
        out_specs=[
            pl.BlockSpec((block, out), lambda i: (i, 0)),
            pl.BlockSpec((per, rank, piece), lambda i: (i, 0, 0)),
        ],
        out_shape=[
            jax.ShapeDtypeStruct((width, out), F32),
            jax.ShapeDtypeStruct((count, rank, piece), F32),
        ],
        compiler_params=params(("arbitrary",)),
        cost_estimate=cost(2 * tokens * width * out, 6 * width * out + 2 * tokens * width),
        name="merge",
    )(inputs, cotangent, error_prev, seed_q)


def rows_of(pieces_ref):
    return jnp.concatenate([pieces_ref[i] for i in range(pieces_ref.shape[0])], axis=1)


def product_kernel(pieces_ref, merged_ref, copies_ref):
    first = rows_of(pieces_ref)
    rank = first.shape[0]
    f_high, f_low = parts_of(first, 2)
    m_high, m_low = parts_of(merged_ref[...], 2)
    both = dot(jnp.concatenate([f_high, f_low], axis=0), m_high, ((1,), (0,)))
    product = both[:rank] + both[rank:] + dot(f_high, m_low, ((1,), (0,)))
    for i in range(copies_ref.shape[0]):
        copies_ref[i] = product


def product_copies(pieces, merged, copies):
    count, rank, piece = pieces.shape
    width, out = merged.shape
    return pl.pallas_call(
        product_kernel,
        out_shape=jax.ShapeDtypeStruct((copies, rank, out), F32),
        compiler_params=params(),
        cost_estimate=cost(2 * rank * width * out, 4 * width * out),
        name="product",
    )(pieces, merged)


def gram_of(rows):
    rank = rows.shape[0]
    stack = jnp.concatenate(parts_of(rows, 3), axis=0)
    full = dot(stack, stack, ((1,), (1,)))
    gram = None
    for i, j in ((2, 0), (0, 2), (1, 1), (1, 0), (0, 1), (0, 0)):
        term = full[i * rank:(i + 1) * rank, j * rank:(j + 1) * rank]
        gram = term if gram is None else gram + term
    return gram


def inverse_factor(gram):
    rank = gram.shape[0]
    row = lax.broadcasted_iota(jnp.int32, (rank, rank), 0)
    lane = lax.broadcasted_iota(jnp.int32, (rank, rank), 1)
    eye = jnp.where(row == lane, 1.0, 0.0).astype(F32)
    wide = jnp.concatenate([gram, eye], axis=1)
    index = lax.broadcasted_iota(jnp.int32, (rank, 1), 0)
    for k in range(rank - 1):
        pivot = wide[k:k + 1, :]
        scale = 1.0 / wide[k:k + 1, k:k + 1]
        factor = jnp.where(index > k, wide[:, k:k + 1] * scale, 0.0)
        wide = wide - factor * pivot
    diagonal = jnp.sum(jnp.where(row == lane, wide[:, :rank], 0.0), axis=1, keepdims=True)
    return wide[:, rank:] * lax.rsqrt(diagonal)


def short_dot(left, right):
    a, b, c = parts_of(left, 3)
    d, e, f = parts_of(right, 3)
    lefts = jnp.concatenate([c, a, b, b, a, a], axis=1)
    rights = jnp.concatenate([d, f, e, d, e, d], axis=0)
    return dot(lefts, rights, ((1,), (0,)))


def sweep_kernel(pieces_ref, basis_ref, inverse_ref):
    rows = rows_of(pieces_ref)
    inverse = None
    for sweep in range(2):
        step = inverse_factor(gram_of(rows))
        rows = short_dot(step, rows)
        inverse = step if inverse is None else short_dot(step, inverse)
    basis_ref[...] = rows
    inverse_ref[...] = inverse


def sweeps(pieces):
    count, rank, piece = pieces.shape
    width = count * piece
    return pl.pallas_call(
        sweep_kernel,
        out_shape=[
            jax.ShapeDtypeStruct((rank, width), F32),
            jax.ShapeDtypeStruct((rank, rank), F32),
        ],
        compiler_params=params(),
        cost_estimate=cost(10 ** 10, 10 ** 7),
        name="sweeps",
    )(pieces)


def error_kernel(workers, merged_ref, basis_ref, inverse_ref, products_ref, error_ref, second_ref, right_ref):
    rank = second_ref.shape[0]

    @pl.when(pl.program_id(0) == 0)
    def _():
        product = products_ref[0]
        for i in range(1, products_ref.shape[0]):
            product = product + products_ref[i]
        second = short_dot(inverse_ref[...], product) * (1.0 / workers)
        second_ref[...] = second
        high, low = parts_of(second, 2)
        right_ref[...] = jnp.concatenate([high, low, high], axis=0)

    b_high, b_low = parts_of(basis_ref[...], 2)
    lefts = jnp.concatenate([b_high, b_high, b_low], axis=0)
    approx = dot(lefts, right_ref[...], ((0,), (0,)))
    error_ref[0] = (merged_ref[...] - approx).astype(error_ref.dtype)


def error_of(merged, basis, inverse, products, workers):
    width, out = merged.shape
    rank = basis.shape[0]
    block = min(width, 512)
    return pl.pallas_call(
        functools.partial(error_kernel, workers),
        grid=(width // block,),
        in_specs=[
            pl.BlockSpec((block, out), lambda i: (i, 0)),
            pl.BlockSpec((rank, block), lambda i: (0, i)),
            pl.BlockSpec((rank, rank), lambda i: (0, 0)),
            pl.BlockSpec(products.shape, lambda i: (0, 0, 0)),
        ],
        out_specs=[
            pl.BlockSpec((1, block, out), lambda i: (0, i, 0)),
            pl.BlockSpec((rank, out), lambda i: (0, 0)),
        ],
        out_shape=[
            jax.ShapeDtypeStruct((1, width, out), BF16),
            jax.ShapeDtypeStruct((rank, out), F32),
        ],
        scratch_shapes=[pltpu.VMEM((3 * rank, out), BF16)],
        compiler_params=params(("arbitrary",)),
        cost_estimate=cost(2 * rank * width * out, 6 * width * out),
        name="error_next",
    )(merged, basis, inverse, products)


def local(direct, rest, count, workers, inputs, cotangent, error_prev, seed_q):
    merged, pieces = merge(inputs, cotangent, error_prev, seed_q, count)
    if rest:
        pieces = lax.psum(pieces, rest)
    chunk = jnp.sum(swap(pieces, direct), axis=0)
    pieces = swap(jnp.broadcast_to(chunk[None], pieces.shape), direct)
    copies = product_copies(pieces, merged, count)
    if rest:
        copies = lax.psum(copies, rest)
    products = swap(copies, direct)
    basis, inverse = sweeps(pieces)
    error_next, second = error_of(merged, basis, inverse, products, workers)
    return (error_next, basis, second)


def solution(mesh):
    direct, rest, count = split_axes(mesh)
    workers = 1
    for axis in AXES:
        workers *= mesh.shape[axis]

    def run(*args):
        return local(direct, rest, count, workers, *args)

    return jax.shard_map(
        run,
        mesh=mesh,
        in_specs=(P(EVERYONE, None), P(EVERYONE, None), P(EVERYONE, None, None), P()),
        out_specs=(P(EVERYONE, None, None), P("groups", None), P("groups", None)),
        check_vma=False,
    )
```

```python
import functools

import jax
import jax.numpy as jnp
from jax import lax
from jax.experimental import pallas as pl
from jax.experimental.pallas import tpu as pltpu
from jax.sharding import PartitionSpec as P

AXES = ("dp", "sub", "pair")
EVERYONE = ("groups",) + AXES
VMEM_BYTES = 24 * 1024 * 1024
BF16, F32 = jnp.bfloat16, jnp.float32
HBM = pl.BlockSpec(memory_space=pltpu.HBM)
VMEM = pl.BlockSpec(memory_space=pltpu.VMEM)


def split_axes(mesh):
    count, chips = mesh.shape["pair"], []
    for axis in ("dp", "sub"):
        if count * mesh.shape[axis] <= 16:
            chips.append(axis)
            count *= mesh.shape[axis]
    chips = tuple(chips)
    rest = tuple(axis for axis in AXES if axis not in chips + ("pair",))
    return chips, rest, count // mesh.shape["pair"]


def swap(pieces, axes):
    return lax.all_to_all(pieces, axes, 0, 0, tiled=True)


def across(value):
    return lax.ppermute(value, "pair", [(0, 1), (1, 0)])


def parts_of(value, count):
    parts = []
    for _ in range(count):
        part = value.astype(BF16)
        parts.append(part)
        value = value - part.astype(F32)
    return parts


def dot(a, b, dims):
    return lax.dot_general(a, b, (dims, ((), ())), preferred_element_type=F32)


def params():
    return pltpu.CompilerParams(vmem_limit_bytes=VMEM_BYTES)


def cost(flops, nbytes):
    return pl.CostEstimate(flops=flops, bytes_accessed=nbytes, transcendentals=0)


def merge_kernel(steps, x_hbm, c_hbm, e_hbm, seed_hbm, merged_ref, pieces_ref,
                 x_ref, c_ref, e_ref, seed_ref, x_sem, e_sem, small_sem):
    width, out = merged_ref.shape
    block = width // steps
    copies = [
        pltpu.make_async_copy(c_hbm, c_ref, small_sem.at[0]),
        pltpu.make_async_copy(seed_hbm, seed_ref, small_sem.at[1]),
    ]
    for i in range(steps):
        part = pl.ds(i * block, block)
        copies.append(pltpu.make_async_copy(x_hbm.at[:, part], x_ref.at[:, part], x_sem.at[i]))
        copies.append(pltpu.make_async_copy(e_hbm.at[0, part, :], e_ref.at[part, :], e_sem.at[i]))
    for copy in copies:
        copy.start()
    copies[0].wait()
    copies[1].wait()
    rank = seed_ref.shape[0]
    half, piece = pieces_ref.shape[1:]
    s_high, s_low = parts_of(seed_ref[...], 2)
    s_both = jnp.concatenate([s_high, s_low], axis=0)
    for i in range(steps):
        copies[2 + 2 * i].wait()
        copies[3 + 2 * i].wait()
        part = pl.ds(i * block, block)
        merged = dot(x_ref[:, part], c_ref[...], ((0,), (0,))) + e_ref[part, :].astype(F32)
        merged_ref[part, :] = merged
        m_high, m_low = parts_of(merged, 2)
        both = dot(s_both, m_high, ((1,), (1,)))
        term = both[:rank] + both[rank:] + dot(s_high, m_low, ((1,), (1,)))
        for j in range(block // piece):
            for k in range(rank // half):
                pieces_ref[(i * (block // piece) + j) * (rank // half) + k] = (
                    term[k * half:(k + 1) * half, j * piece:(j + 1) * piece])


def merge(inputs, cotangent, error_prev, seed_q, chips):
    tokens, width = inputs.shape
    out = cotangent.shape[1]
    rank = seed_q.shape[0]
    steps = 4
    return pl.pallas_call(
        functools.partial(merge_kernel, steps),
        in_specs=[HBM, HBM, HBM, HBM],
        out_specs=[VMEM, VMEM],
        out_shape=[
            jax.ShapeDtypeStruct((width, out), F32),
            jax.ShapeDtypeStruct((2 * chips, rank // 2, width // chips), F32),
        ],
        scratch_shapes=[
            pltpu.VMEM((tokens, width), BF16),
            pltpu.VMEM((tokens, out), BF16),
            pltpu.VMEM((width, out), BF16),
            pltpu.VMEM((rank, out), F32),
            pltpu.SemaphoreType.DMA((steps,)),
            pltpu.SemaphoreType.DMA((steps,)),
            pltpu.SemaphoreType.DMA((2,)),
        ],
        compiler_params=params(),
        cost_estimate=cost(2 * tokens * width * out, 6 * width * out + 2 * tokens * width),
        name="merge",
    )(inputs, cotangent, error_prev, seed_q)


def rows_of(pieces_ref):
    return jnp.concatenate([pieces_ref[i] for i in range(pieces_ref.shape[0])], axis=1)


def product_kernel(pieces_ref, mine_ref, other_ref, copies_ref):
    rows = rows_of(pieces_ref)
    half = rows.shape[0]
    f_high, f_low = parts_of(rows, 2)
    m_high, m_low = parts_of(mine_ref[...] + other_ref[...], 2)
    both = dot(jnp.concatenate([f_high, f_low], axis=0), m_high, ((1,), (0,)))
    product = both[:half] + both[half:] + dot(f_high, m_low, ((1,), (0,)))
    for i in range(copies_ref.shape[0]):
        copies_ref[i] = product


def product_copies(pieces, mine, other):
    chips, half, piece = pieces.shape
    width, out = mine.shape
    return pl.pallas_call(
        product_kernel,
        out_shape=jax.ShapeDtypeStruct((chips, half, out), F32),
        compiler_params=params(),
        cost_estimate=cost(2 * half * width * out, 8 * width * out),
        name="product",
    )(pieces, mine, other)


def both_halves(mine, other):
    low = lax.axis_index("pair") == 0
    return jnp.concatenate([jnp.where(low, mine, other), jnp.where(low, other, mine)], axis=0)


def gram_of(rows):
    rank = rows.shape[0]
    stack = jnp.concatenate(parts_of(rows, 3), axis=0)
    full = dot(stack, stack, ((1,), (1,)))
    gram = None
    for i, j in ((2, 0), (0, 2), (1, 1), (1, 0), (0, 1), (0, 0)):
        term = full[i * rank:(i + 1) * rank, j * rank:(j + 1) * rank]
        gram = term if gram is None else gram + term
    return gram


def inverse_factor(gram):
    rank = gram.shape[0]
    row = lax.broadcasted_iota(jnp.int32, (rank, rank), 0)
    lane = lax.broadcasted_iota(jnp.int32, (rank, rank), 1)
    eye = jnp.where(row == lane, 1.0, 0.0).astype(F32)
    wide = jnp.concatenate([gram, eye], axis=1)
    index = lax.broadcasted_iota(jnp.int32, (rank, 1), 0)
    for k in range(rank - 1):
        pivot = wide[k:k + 1, :]
        scale = 1.0 / wide[k:k + 1, k:k + 1]
        factor = jnp.where(index > k, wide[:, k:k + 1] * scale, 0.0)
        wide = wide - factor * pivot
    diagonal = jnp.sum(jnp.where(row == lane, wide[:, :rank], 0.0), axis=1, keepdims=True)
    return wide[:, rank:] * lax.rsqrt(diagonal)


def short_dot(left, right):
    a, b, c = parts_of(left, 3)
    d, e, f = parts_of(right, 3)
    lefts = jnp.concatenate([c, a, b, b, a, a], axis=1)
    rights = jnp.concatenate([d, f, e, d, e, d], axis=0)
    return dot(lefts, rights, ((1,), (0,)))


def sweep_kernel(mine_ref, other_ref, basis_ref, inverse_ref):
    rows = both_halves(rows_of(mine_ref), rows_of(other_ref))
    inverse = None
    for sweep in range(2):
        step = inverse_factor(gram_of(rows))
        rows = short_dot(step, rows)
        inverse = step if inverse is None else short_dot(step, inverse)
    basis_ref[...] = rows
    inverse_ref[...] = inverse


def sweeps(mine, other):
    chips, half, piece = mine.shape
    rank, width = 2 * half, chips * piece
    return pl.pallas_call(
        sweep_kernel,
        out_shape=[
            jax.ShapeDtypeStruct((rank, width), F32),
            jax.ShapeDtypeStruct((rank, rank), F32),
        ],
        compiler_params=params(),
        cost_estimate=cost(10 ** 10, 10 ** 7),
        name="sweeps",
    )(mine, other)


def error_kernel(workers, steps, merged_ref, basis_ref, inverse_ref, mine_ref, other_ref,
                 error_hbm, basis_hbm, second_ref, error_ref, error_sem, basis_sem):
    width = merged_ref.shape[0]
    block = width // steps
    keep = pltpu.make_async_copy(basis_ref, basis_hbm, basis_sem)
    keep.start()
    product = both_halves(mine_ref[...], other_ref[...])
    second = short_dot(inverse_ref[...], product) * (1.0 / workers)
    second_ref[...] = second
    s_high, s_low = parts_of(second, 2)
    rights = jnp.concatenate([s_high, s_low, s_high], axis=0)
    copies = []
    for i in range(steps):
        part = pl.ds(i * block, block)
        b_high, b_low = parts_of(basis_ref[:, part], 2)
        lefts = jnp.concatenate([b_high, b_high, b_low], axis=0)
        approx = dot(lefts, rights, ((0,), (0,)))
        error_ref[part, :] = (merged_ref[part, :] - approx).astype(BF16)
        copies.append(pltpu.make_async_copy(
            error_ref.at[part, :], error_hbm.at[0, part, :], error_sem.at[i]))
        copies[i].start()
    for copy in copies + [keep]:
        copy.wait()


def error_of(merged, basis, inverse, mine, other, workers):
    width, out = merged.shape
    rank = basis.shape[0]
    steps = 4
    return pl.pallas_call(
        functools.partial(error_kernel, workers, steps),
        in_specs=[VMEM] * 5,
        out_specs=[HBM, HBM, VMEM],
        out_shape=[
            jax.ShapeDtypeStruct((1, width, out), BF16),
            jax.ShapeDtypeStruct((rank, width), F32),
            jax.ShapeDtypeStruct((rank, out), F32),
        ],
        scratch_shapes=[
            pltpu.VMEM((width, out), BF16),
            pltpu.SemaphoreType.DMA((steps,)),
            pltpu.SemaphoreType.DMA,
        ],
        compiler_params=params(),
        cost_estimate=cost(2 * rank * width * out, 6 * width * out),
        name="error_next",
    )(merged, basis, inverse, mine, other)


def local(chips, rest, count, workers, inputs, cotangent, error_prev, seed_q):
    inputs, cotangent, error_prev, seed_q = (
        pltpu.with_memory_space_constraint(value, pltpu.HBM)
        for value in (inputs, cotangent, error_prev, seed_q))
    merged, pieces = merge(inputs, cotangent, error_prev, seed_q, count)
    merged_other = across(merged)
    if rest:
        pieces = lax.psum(pieces, rest)
    chunk = jnp.sum(swap(pieces, chips + ("pair",)), axis=0)
    half = swap(jnp.broadcast_to(chunk[None], (count,) + chunk.shape), chips)
    half_other = across(half)
    copies = product_copies(half, merged, merged_other)
    if rest:
        copies = lax.psum(copies, rest)
    product = jnp.sum(swap(copies, chips), axis=0)
    product_other = across(product)
    basis, inverse = sweeps(half, half_other)
    error_next, basis, second = error_of(merged, basis, inverse, product, product_other, workers)
    return (error_next, basis, second)


def solution(mesh):
    chips, rest, count = split_axes(mesh)
    workers = 1
    for axis in AXES:
        workers *= mesh.shape[axis]

    def run(*args):
        return local(chips, rest, count, workers, *args)

    return jax.shard_map(
        run,
        mesh=mesh,
        in_specs=(P(EVERYONE, None), P(EVERYONE, None), P(EVERYONE, None, None), P()),
        out_specs=(P(EVERYONE, None, None), P("groups", None), P("groups", None)),
        check_vma=False,
    )
```

```python
import functools

import jax
import jax.numpy as jnp
from jax import lax
from jax.experimental import pallas as pl
from jax.experimental.pallas import tpu as pltpu
from jax.sharding import PartitionSpec as P

AXES = ("dp", "sub", "pair")
EVERYONE = ("groups",) + AXES
VMEM_BYTES = 24 * 1024 * 1024
CHUNK = 256
GROUP = 4
BF16, F32 = jnp.bfloat16, jnp.float32
HBM = pl.BlockSpec(memory_space=pltpu.HBM)
VMEM = pl.BlockSpec(memory_space=pltpu.VMEM)


def split_axes(mesh):
    count, chips = mesh.shape["pair"], []
    for axis in ("dp", "sub"):
        if count * mesh.shape[axis] <= 16:
            chips.append(axis)
            count *= mesh.shape[axis]
    chips = tuple(chips)
    rest = tuple(axis for axis in AXES if axis not in chips + ("pair",))
    return chips, rest, count // mesh.shape["pair"]


def swap(pieces, axes):
    return lax.all_to_all(pieces, axes, 0, 0, tiled=True)


def across(value):
    return lax.ppermute(value, "pair", [(0, 1), (1, 0)])


def parts_of(value, count):
    parts = []
    for _ in range(count):
        part = value.astype(BF16)
        parts.append(part)
        value = value - part.astype(F32)
    return parts


def dot(a, b, dims):
    return lax.dot_general(a, b, (dims, ((), ())), preferred_element_type=F32)


def params():
    return pltpu.CompilerParams(vmem_limit_bytes=VMEM_BYTES)


def cost(flops, nbytes):
    return pl.CostEstimate(flops=flops, bytes_accessed=nbytes, transcendentals=0)


def split_copies(x_hbm, e_hbm, x_ref, e_ref, x_sem, e_sem, block):
    copies = []
    for i in range(x_hbm.shape[1] // block):
        part = pl.ds(i * block, block)
        copies.append((
            pltpu.make_async_copy(x_hbm.at[:, part], x_ref.at[:, part], x_sem.at[i]),
            pltpu.make_async_copy(e_hbm.at[0, part, :], e_ref.at[part, :], e_sem.at[i]),
        ))
    return copies


def term_kernel(block, x_hbm, c_hbm, e_hbm, seed_hbm, pieces_ref,
                x_ref, c_ref, e_ref, seed_ref, x_sem, e_sem, small_sem):
    small = [
        pltpu.make_async_copy(seed_hbm, seed_ref, small_sem.at[0]),
        pltpu.make_async_copy(c_hbm, c_ref, small_sem.at[1]),
    ]
    copies = split_copies(x_hbm, e_hbm, x_ref, e_ref, x_sem, e_sem, block)
    for copy in small + [copy for pair in copies for copy in pair]:
        copy.start()
    small[0].wait()
    small[1].wait()
    rank = seed_ref.shape[0]
    half, piece = pieces_ref.shape[1:]
    seed = jnp.concatenate(parts_of(seed_ref[...], 3), axis=0)
    mixed = added(dot(seed, c_ref[...], ((1,), (1,))), rank)
    mixed = jnp.concatenate(parts_of(mixed, 3), axis=0)
    for i, pair in enumerate(copies):
        part = pl.ds(i * block, block)
        pair[0].wait()
        pair[1].wait()
        term = added(dot(mixed, x_ref[:, part], ((1,), (0,)))
                     + dot(seed, e_ref[part, :], ((1,), (1,))), rank)
        for j in range(block // piece):
            for k in range(rank // half):
                pieces_ref[(i * (block // piece) + j) * (rank // half) + k] = (
                    term[k * half:(k + 1) * half, j * piece:(j + 1) * piece])


def added(stack, rank):
    total = stack[stack.shape[0] - rank:]
    for i in range(stack.shape[0] // rank - 2, -1, -1):
        total = total + stack[i * rank:(i + 1) * rank]
    return total


def term_pieces(inputs, cotangent, error_prev, seed_q, chips):
    tokens, width = inputs.shape
    out = cotangent.shape[1]
    rank = seed_q.shape[0]
    block = max(CHUNK, width // chips)
    return pl.pallas_call(
        functools.partial(term_kernel, block),
        in_specs=[HBM] * 4,
        out_specs=VMEM,
        out_shape=jax.ShapeDtypeStruct((2 * chips, rank // 2, width // chips), F32),
        scratch_shapes=[
            pltpu.VMEM((tokens, width), BF16),
            pltpu.VMEM((tokens, out), BF16),
            pltpu.VMEM((width, out), BF16),
            pltpu.VMEM((rank, out), F32),
            pltpu.SemaphoreType.DMA((width // block,)),
            pltpu.SemaphoreType.DMA((width // block,)),
            pltpu.SemaphoreType.DMA((2,)),
        ],
        compiler_params=params(),
        cost_estimate=cost(6 * tokens * rank * width, 2 * tokens * width + 2 * width * out),
        name="term",
    )(inputs, cotangent, error_prev, seed_q)


def merge_kernel(x_hbm, c_hbm, e_hbm, merged_ref, x_ref, c_ref, e_ref, x_sem, e_sem, c_sem):
    small = pltpu.make_async_copy(c_hbm, c_ref, c_sem)
    copies = split_copies(x_hbm, e_hbm, x_ref, e_ref, x_sem, e_sem, CHUNK)
    for copy in [small] + [copy for pair in copies for copy in pair]:
        copy.start()
    small.wait()
    for i, pair in enumerate(copies):
        part = pl.ds(i * CHUNK, CHUNK)
        pair[0].wait()
        pair[1].wait()
        merged_ref[part, :] = (
            dot(x_ref[:, part], c_ref[...], ((0,), (0,))) + e_ref[part, :].astype(F32))


def merge(inputs, cotangent, error_prev):
    tokens, width = inputs.shape
    out = cotangent.shape[1]
    return pl.pallas_call(
        merge_kernel,
        in_specs=[HBM] * 3,
        out_specs=VMEM,
        out_shape=jax.ShapeDtypeStruct((width, out), F32),
        scratch_shapes=[
            pltpu.VMEM((tokens, width), BF16),
            pltpu.VMEM((tokens, out), BF16),
            pltpu.VMEM((width, out), BF16),
            pltpu.SemaphoreType.DMA((width // CHUNK,)),
            pltpu.SemaphoreType.DMA((width // CHUNK,)),
            pltpu.SemaphoreType.DMA,
        ],
        compiler_params=params(),
        cost_estimate=cost(10 ** 9, 10 ** 7),
        name="merge",
    )(inputs, cotangent, error_prev)


def product_kernel(pieces_ref, mine_ref, other_ref, copies_ref):
    chips, half, piece = pieces_ref.shape
    product = None
    for i in range(chips):
        part = pl.ds(i * piece, piece)
        m_high, m_low = parts_of(mine_ref[part, :] + other_ref[part, :], 2)
        f_high, f_low = parts_of(pieces_ref[i], 2)
        both = jnp.concatenate([f_high, f_low], axis=0)
        term = added(dot(both, m_high, ((1,), (0,))), half) + dot(f_high, m_low, ((1,), (0,)))
        product = term if product is None else product + term
    for i in range(chips):
        copies_ref[i] = product


def product_copies(pieces, mine, other):
    chips, half, piece = pieces.shape
    width, out = mine.shape
    return pl.pallas_call(
        product_kernel,
        out_shape=jax.ShapeDtypeStruct((chips, half, out), F32),
        compiler_params=params(),
        cost_estimate=cost(2 * half * width * out, 8 * width * out),
        name="product",
    )(pieces, mine, other)


def both_halves(mine, other):
    low = lax.axis_index("pair") == 0
    return jnp.concatenate([jnp.where(low, mine, other), jnp.where(low, other, mine)], axis=0)


def gram_blocks(rows):
    stack = jnp.concatenate(parts_of(rows, 3), axis=0)
    return dot(stack, stack, ((1,), (1,)))


def gram_of(blocks, rank):
    gram = None
    for i, j in ((2, 0), (0, 2), (1, 1), (1, 0), (0, 1), (0, 0)):
        term = blocks[i * rank:(i + 1) * rank, j * rank:(j + 1) * rank]
        gram = term if gram is None else gram + term
    return gram


def inverse_factor(gram):
    rank = gram.shape[0]
    row = lax.broadcasted_iota(jnp.int32, (rank, rank), 0)
    lane = lax.broadcasted_iota(jnp.int32, (rank, rank), 1)
    eye = jnp.where(row == lane, 1.0, 0.0).astype(F32)
    wide = jnp.concatenate([gram, eye], axis=1)
    index = lax.broadcasted_iota(jnp.int32, wide.shape, 0)
    scale = jnp.ones_like(wide)
    for base in range(0, rank, GROUP):
        columns = [
            jnp.broadcast_to(wide[:, k:k + 1], wide.shape) for k in range(base, base + GROUP)
        ]
        for j in range(GROUP):
            k = base + j
            pivot = columns[j][k:k + 1, :]
            factor = jnp.where(index > k, columns[j] * (1.0 / pivot), 0.0)
            for i in range(j + 1, GROUP):
                columns[i] = columns[i] - factor * columns[i][k:k + 1, :]
            wide = wide - factor * wide[k:k + 1, :]
            scale = jnp.where(index == k, lax.rsqrt(pivot), scale)
    return (wide * scale)[:, rank:]


def short_dot(left, right):
    a, b, c = parts_of(left, 3)
    d, e, f = parts_of(right, 3)
    lefts = jnp.concatenate([c, a, b, b, a, a], axis=1)
    rights = jnp.concatenate([d, f, e, d, e, d], axis=0)
    return dot(lefts, rights, ((1,), (0,)))


def sweep_kernel(mine_ref, other_ref, basis_ref, inverse_ref):
    chips, half, piece = mine_ref.shape
    rank = 2 * half
    blocks = None
    for i in range(chips):
        rows = both_halves(mine_ref[i], other_ref[i])
        basis_ref[:, i * piece:(i + 1) * piece] = rows
        term = gram_blocks(rows)
        blocks = term if blocks is None else blocks + term
    step = inverse_factor(gram_of(blocks, rank))
    blocks = None
    for i in range(chips):
        rows = short_dot(step, basis_ref[:, i * piece:(i + 1) * piece])
        basis_ref[:, i * piece:(i + 1) * piece] = rows
        term = gram_blocks(rows)
        blocks = term if blocks is None else blocks + term
    last = inverse_factor(gram_of(blocks, rank))
    for i in range(chips):
        part = slice(i * piece, (i + 1) * piece)
        basis_ref[:, part] = short_dot(last, basis_ref[:, part])
    inverse_ref[...] = short_dot(last, step)


def sweeps(mine, other):
    chips, half, piece = mine.shape
    rank, width = 2 * half, chips * piece
    return pl.pallas_call(
        sweep_kernel,
        out_shape=[
            jax.ShapeDtypeStruct((rank, width), F32),
            jax.ShapeDtypeStruct((rank, rank), F32),
        ],
        compiler_params=params(),
        cost_estimate=cost(10 ** 10, 10 ** 7),
        name="sweeps",
    )(mine, other)


def error_kernel(workers, steps, merged_ref, basis_ref, inverse_ref, mine_ref, other_ref,
                 error_hbm, basis_hbm, second_ref, error_ref, error_sem, basis_sem):
    width = merged_ref.shape[0]
    block = width // steps
    keep = pltpu.make_async_copy(basis_ref, basis_hbm, basis_sem)
    keep.start()
    product = both_halves(mine_ref[...], other_ref[...])
    second = short_dot(inverse_ref[...], product) * (1.0 / workers)
    second_ref[...] = second
    s_high, s_low = parts_of(second, 2)
    rights = jnp.concatenate([s_high, s_low, s_high], axis=0)
    copies = []
    for i in range(steps):
        part = pl.ds(i * block, block)
        b_high, b_low = parts_of(basis_ref[:, part], 2)
        lefts = jnp.concatenate([b_high, b_high, b_low], axis=0)
        approx = dot(lefts, rights, ((0,), (0,)))
        error_ref[part, :] = (merged_ref[part, :] - approx).astype(BF16)
        copies.append(pltpu.make_async_copy(
            error_ref.at[part, :], error_hbm.at[0, part, :], error_sem.at[i]))
        copies[i].start()
    for copy in copies + [keep]:
        copy.wait()


def error_of(merged, basis, inverse, mine, other, workers):
    width, out = merged.shape
    rank = basis.shape[0]
    steps = width // CHUNK
    return pl.pallas_call(
        functools.partial(error_kernel, workers, steps),
        in_specs=[VMEM] * 5,
        out_specs=[HBM, HBM, VMEM],
        out_shape=[
            jax.ShapeDtypeStruct((1, width, out), BF16),
            jax.ShapeDtypeStruct((rank, width), F32),
            jax.ShapeDtypeStruct((rank, out), F32),
        ],
        scratch_shapes=[
            pltpu.VMEM((width, out), BF16),
            pltpu.SemaphoreType.DMA((steps,)),
            pltpu.SemaphoreType.DMA,
        ],
        compiler_params=params(),
        cost_estimate=cost(2 * rank * width * out, 6 * width * out),
        name="error_next",
    )(merged, basis, inverse, mine, other)


def local(chips, rest, count, workers, *arguments):
    inputs, cotangent, error_prev, seed_q = (
        pltpu.with_memory_space_constraint(value, pltpu.HBM) for value in arguments)
    pieces = term_pieces(inputs, cotangent, error_prev, seed_q, count)
    merged = merge(inputs, cotangent, error_prev)
    merged_other = across(merged)
    if rest:
        pieces = lax.psum(pieces, rest)
    chunk = jnp.sum(swap(pieces, chips + ("pair",)), axis=0)
    half = swap(jnp.broadcast_to(chunk[None], (count,) + chunk.shape), chips)
    half_other = across(half)
    copies = product_copies(half, merged, merged_other)
    if rest:
        copies = lax.psum(copies, rest)
    basis, inverse = sweeps(half, half_other)
    product = jnp.sum(swap(copies, chips), axis=0)
    product, basis, inverse = lax.optimization_barrier((product, basis, inverse))
    product_other = across(product)
    error_next, basis, second = error_of(merged, basis, inverse, product, product_other, workers)
    return (error_next, basis, second)


def solution(mesh):
    chips, rest, count = split_axes(mesh)
    workers = 1
    for axis in AXES:
        workers *= mesh.shape[axis]

    def run(*args):
        return local(chips, rest, count, workers, *args)

    return jax.shard_map(
        run,
        mesh=mesh,
        in_specs=(P(EVERYONE, None), P(EVERYONE, None), P(EVERYONE, None, None), P()),
        out_specs=(P(EVERYONE, None, None), P("groups", None), P("groups", None)),
        check_vma=False,
    )
```

```python
import functools

import jax
import jax.numpy as jnp
from jax import lax
from jax.experimental import pallas as pl
from jax.experimental.pallas import tpu as pltpu
from jax.sharding import PartitionSpec as P

AXES = ("dp", "sub", "pair")
EVERYONE = ("groups",) + AXES
VMEM_BYTES = 24 * 1024 * 1024
CHUNK = 256
GROUP = 4
BF16, F32 = jnp.bfloat16, jnp.float32
HBM = pl.BlockSpec(memory_space=pltpu.HBM)
ANY = pl.BlockSpec(memory_space=pl.ANY)
VMEM = pl.BlockSpec(memory_space=pltpu.VMEM)


def split_axes(mesh):
    count, chips = mesh.shape["pair"], []
    for axis in ("dp", "sub"):
        if count * mesh.shape[axis] <= 16:
            chips.append(axis)
            count *= mesh.shape[axis]
    chips = tuple(chips)
    rest = tuple(axis for axis in AXES if axis not in chips + ("pair",))
    return chips, rest, tuple(mesh.shape[axis] for axis in chips)


def swap(pieces, axes):
    return lax.all_to_all(pieces, axes, 0, 0, tiled=True)


def across(value):
    return lax.ppermute(value, "pair", [(0, 1), (1, 0)])


def parts_of(value, count):
    parts = []
    for _ in range(count):
        part = value.astype(BF16)
        parts.append(part)
        value = value - part.astype(F32)
    return parts


def dot(a, b, dims):
    return lax.dot_general(a, b, (dims, ((), ())), preferred_element_type=F32)


def params():
    return pltpu.CompilerParams(vmem_limit_bytes=VMEM_BYTES)


def cost(flops, nbytes):
    return pl.CostEstimate(flops=flops, bytes_accessed=nbytes, transcendentals=0)


def whole_copies(pairs, sems):
    return [pltpu.make_async_copy(pair[0], pair[1], sems.at[i]) for i, pair in enumerate(pairs)]


def row_parts(source, target, parts):
    block = target.shape[0] // parts
    rows = [pl.ds(i * block, block) for i in range(parts)]
    return [(source.at[part, :], target.at[part, :]) for part in rows]


def term_kernel(x_hbm, c_hbm, e_hbm, seed_hbm, pieces_ref,
                x_ref, c_ref, e_ref, seed_ref, term_ref, sems):
    copies = whole_copies(
        [(seed_hbm, seed_ref), (c_hbm, c_ref)] + row_parts(e_hbm.at[0], e_ref, 2)
        + row_parts(x_hbm, x_ref, 2), sems)
    for copy in copies:
        copy.start()
    rank = seed_ref.shape[0]
    tokens, width = x_ref.shape
    half, piece = pieces_ref.shape[1:]
    copies[0].wait()
    copies[1].wait()
    seed = jnp.concatenate(parts_of(seed_ref[...], 3), axis=0)
    mixed = added(dot(seed, c_ref[...], ((1,), (1,))), rank)
    mixed = jnp.concatenate(parts_of(mixed, 3), axis=0)
    blocks = width // CHUNK
    for i in range(blocks):
        if i % (blocks // 2) == 0:
            copies[2 + i // (blocks // 2)].wait()
        part = pl.ds(i * CHUNK, CHUNK)
        term_ref[:, part] = added(dot(seed, e_ref[part, :], ((1,), (1,))), rank)
    for t in range(2):
        copies[4 + t].wait()
        own = mixed[:, t * (tokens // 2):(t + 1) * (tokens // 2)]
        rows = pl.ds(t * (tokens // 2), tokens // 2)
        for i in range(blocks):
            part = pl.ds(i * CHUNK, CHUNK)
            term_ref[:, part] += added(dot(own, x_ref[rows, part], ((1,), (0,))), rank)
    for j in range(width // piece):
        for k in range(rank // half):
            pieces_ref[j * (rank // half) + k] = (
                term_ref[k * half:(k + 1) * half, j * piece:(j + 1) * piece])


def added(stack, rank):
    total = stack[stack.shape[0] - rank:]
    for i in range(stack.shape[0] // rank - 2, -1, -1):
        total = total + stack[i * rank:(i + 1) * rank]
    return total


def term_pieces(inputs, cotangent, error_prev, seed_q, chips):
    tokens, width = inputs.shape
    out = cotangent.shape[1]
    rank = seed_q.shape[0]
    return pl.pallas_call(
        term_kernel,
        in_specs=[HBM] * 4,
        out_specs=VMEM,
        out_shape=jax.ShapeDtypeStruct((2 * chips, rank // 2, width // chips), F32),
        scratch_shapes=[
            pltpu.VMEM((tokens, width), BF16),
            pltpu.VMEM((tokens, out), BF16),
            pltpu.VMEM((width, out), BF16),
            pltpu.VMEM((rank, out), F32),
            pltpu.VMEM((rank, width), F32),
            pltpu.SemaphoreType.DMA((6,)),
        ],
        compiler_params=params(),
        cost_estimate=cost(6 * tokens * rank * width, 2 * tokens * width + 2 * width * out),
        name="term",
    )(inputs, cotangent, error_prev, seed_q)


def merge_kernel(x_hbm, c_hbm, e_hbm, after_hbm, merged_ref, x_ref, c_ref, e_ref, sems):
    copies = whole_copies([(c_hbm, c_ref), (x_hbm, x_ref), (e_hbm.at[0], e_ref)], sems)
    for copy in copies:
        copy.start()
    for copy in copies:
        copy.wait()
    for i in range(merged_ref.shape[0] // CHUNK):
        part = pl.ds(i * CHUNK, CHUNK)
        merged_ref[part, :] = (
            dot(x_ref[:, part], c_ref[...], ((0,), (0,))) + e_ref[part, :].astype(F32))


def merge(inputs, cotangent, error_prev, after):
    tokens, width = inputs.shape
    out = cotangent.shape[1]
    return pl.pallas_call(
        merge_kernel,
        in_specs=[HBM] * 3 + [ANY],
        out_specs=VMEM,
        out_shape=jax.ShapeDtypeStruct((width, out), F32),
        scratch_shapes=[
            pltpu.VMEM((tokens, width), BF16),
            pltpu.VMEM((tokens, out), BF16),
            pltpu.VMEM((width, out), BF16),
            pltpu.SemaphoreType.DMA((3,)),
        ],
        compiler_params=params(),
        cost_estimate=cost(10 ** 9, 10 ** 7),
        name="merge",
    )(inputs, cotangent, error_prev, after)


def gathered(block, rounds):
    blocks = block[None]
    for axis, size, bit, mask in rounds:
        other = lax.ppermute(blocks, axis, [(i, i ^ bit) for i in range(size)])
        blocks = jnp.concatenate([blocks, other], axis=0)
    return blocks


def masks_of(rounds):
    masks = [0]
    for axis, size, bit, mask in rounds:
        masks = masks + [old ^ mask for old in masks]
    return masks


def chip_index(chips, sizes):
    index = 0
    for axis, size in zip(chips, sizes):
        index = index * size + lax.axis_index(axis)
    return index


def place(chip, mask, piece):
    return pl.ds(pl.multiple_of((chip ^ mask) * piece, piece), piece)


def product_kernel(layout, pieces_ref, mine_ref, other_hbm, copies_ref, other_ref, sems):
    chips, sizes, masks = layout
    count, half, piece = pieces_ref.shape
    chip = chip_index(chips, sizes)
    parts = [place(chip, mask, piece) for mask in masks]
    copies = whole_copies([(other_hbm.at[part, :], other_ref.at[part, :]) for part in parts], sems)
    for copy in copies:
        copy.start()
    product = None
    for i, part in enumerate(parts):
        f_high, f_low = parts_of(pieces_ref[i], 2)
        both = jnp.concatenate([f_high, f_low], axis=0)
        copies[i].wait()
        m_high, m_low = parts_of(mine_ref[part, :] + other_ref[part, :], 2)
        term = added(dot(both, m_high, ((1,), (0,))), half) + dot(f_high, m_low, ((1,), (0,)))
        product = term if product is None else product + term
    for i in range(count):
        copies_ref[i] = product


def product_copies(layout, pieces, mine, other):
    count, half, piece = pieces.shape
    width, out = mine.shape
    return pl.pallas_call(
        functools.partial(product_kernel, layout),
        in_specs=[VMEM, VMEM, ANY],
        out_shape=jax.ShapeDtypeStruct((count, half, out), F32),
        scratch_shapes=[pltpu.VMEM((width, out), F32), pltpu.SemaphoreType.DMA((count,))],
        compiler_params=params(),
        cost_estimate=cost(2 * half * width * out, 8 * width * out),
        name="product",
    )(pieces, mine, other)


def both_halves(mine, other):
    low = lax.axis_index("pair") == 0
    return jnp.concatenate([jnp.where(low, mine, other), jnp.where(low, other, mine)], axis=0)


def gram_blocks(rows):
    stack = jnp.concatenate(parts_of(rows, 3), axis=0)
    return dot(stack, stack, ((1,), (1,)))


def gram_of(blocks, rank):
    gram = None
    for i, j in ((2, 0), (0, 2), (1, 1), (1, 0), (0, 1), (0, 0)):
        term = blocks[i * rank:(i + 1) * rank, j * rank:(j + 1) * rank]
        gram = term if gram is None else gram + term
    return gram


def inverse_factor(gram):
    rank = gram.shape[0]
    row = lax.broadcasted_iota(jnp.int32, (rank, rank), 0)
    lane = lax.broadcasted_iota(jnp.int32, (rank, rank), 1)
    eye = jnp.where(row == lane, 1.0, 0.0).astype(F32)
    wide = jnp.concatenate([gram, eye], axis=1)
    index = lax.broadcasted_iota(jnp.int32, wide.shape, 0)
    scale = jnp.ones_like(wide)
    for base in range(0, rank, GROUP):
        columns = [
            jnp.broadcast_to(wide[:, k:k + 1], wide.shape) for k in range(base, base + GROUP)
        ]
        for j in range(GROUP):
            k = base + j
            pivot = columns[j][k:k + 1, :]
            factor = jnp.where(index > k, columns[j] * (1.0 / pivot), 0.0)
            for i in range(j + 1, GROUP):
                columns[i] = columns[i] - factor * columns[i][k:k + 1, :]
            wide = wide - factor * wide[k:k + 1, :]
            scale = jnp.where(index == k, lax.rsqrt(pivot), scale)
    return (wide * scale)[:, rank:]


def short_dot(left, right):
    a, b, c = parts_of(left, 3)
    d, e, f = parts_of(right, 3)
    lefts = jnp.concatenate([c, a, b, b, a, a], axis=1)
    rights = jnp.concatenate([d, f, e, d, e, d], axis=0)
    return dot(lefts, rights, ((1,), (0,)))


def sweep_kernel(layout, mine_ref, other_ref, basis_ref, inverse_ref):
    chips, sizes, masks = layout
    count, half, piece = mine_ref.shape
    rank = 2 * half
    chip = chip_index(chips, sizes)
    blocks = None
    for i, mask in enumerate(masks):
        rows = both_halves(mine_ref[i], other_ref[i])
        basis_ref[:, place(chip, mask, piece)] = rows
        term = gram_blocks(rows)
        blocks = term if blocks is None else blocks + term
    step = inverse_factor(gram_of(blocks, rank))
    blocks = None
    for i in range(count):
        part = slice(i * piece, (i + 1) * piece)
        rows = short_dot(step, basis_ref[:, part])
        basis_ref[:, part] = rows
        term = gram_blocks(rows)
        blocks = term if blocks is None else blocks + term
    last = inverse_factor(gram_of(blocks, rank))
    for i in range(count):
        part = slice(i * piece, (i + 1) * piece)
        basis_ref[:, part] = short_dot(last, basis_ref[:, part])
    inverse_ref[...] = short_dot(last, step)


def sweeps(layout, mine, other):
    count, half, piece = mine.shape
    rank, width = 2 * half, count * piece
    return pl.pallas_call(
        functools.partial(sweep_kernel, layout),
        out_shape=[
            jax.ShapeDtypeStruct((rank, width), F32),
            jax.ShapeDtypeStruct((rank, rank), F32),
        ],
        compiler_params=params(),
        cost_estimate=cost(10 ** 10, 10 ** 7),
        name="sweeps",
    )(mine, other)


def error_kernel(workers, steps, merged_ref, basis_ref, inverse_ref, mine_ref, other_ref,
                 error_hbm, basis_hbm, second_ref, error_ref, error_sem, basis_sem):
    width = merged_ref.shape[0]
    block = width // steps
    keep = pltpu.make_async_copy(basis_ref, basis_hbm, basis_sem)
    keep.start()
    product = both_halves(mine_ref[...], other_ref[...])
    second = short_dot(inverse_ref[...], product) * (1.0 / workers)
    second_ref[...] = second
    s_high, s_low = parts_of(second, 2)
    rights = jnp.concatenate([s_high, s_low, s_high], axis=0)
    copies = []
    for i in range(steps):
        part = pl.ds(i * block, block)
        b_high, b_low = parts_of(basis_ref[:, part], 2)
        lefts = jnp.concatenate([b_high, b_high, b_low], axis=0)
        approx = dot(lefts, rights, ((0,), (0,)))
        error_ref[part, :] = (merged_ref[part, :] - approx).astype(BF16)
        copies.append(pltpu.make_async_copy(
            error_ref.at[part, :], error_hbm.at[0, part, :], error_sem.at[i]))
        copies[i].start()
    for copy in copies + [keep]:
        copy.wait()


def error_of(merged, basis, inverse, mine, other, workers):
    width, out = merged.shape
    rank = basis.shape[0]
    steps = width // CHUNK
    return pl.pallas_call(
        functools.partial(error_kernel, workers, steps),
        in_specs=[VMEM] * 5,
        out_specs=[HBM, HBM, VMEM],
        out_shape=[
            jax.ShapeDtypeStruct((1, width, out), BF16),
            jax.ShapeDtypeStruct((rank, width), F32),
            jax.ShapeDtypeStruct((rank, out), F32),
        ],
        scratch_shapes=[
            pltpu.VMEM((width, out), BF16),
            pltpu.SemaphoreType.DMA((steps,)),
            pltpu.SemaphoreType.DMA,
        ],
        compiler_params=params(),
        cost_estimate=cost(2 * rank * width * out, 6 * width * out),
        name="error_next",
    )(merged, basis, inverse, mine, other)


def local(chips, rest, sizes, workers, *arguments):
    inputs, cotangent, error_prev, seed_q = (
        pltpu.with_memory_space_constraint(value, pltpu.HBM) for value in arguments)
    count, rounds, stride = 1, [], 1
    for axis, size in zip(chips[::-1], sizes[::-1]):
        bits = [1 << i for i in range(size.bit_length() - 1)]
        rounds = [(axis, size, bit, bit * stride) for bit in bits[::-1]] + rounds
        stride *= size
    count = stride
    layout = (chips, sizes, masks_of(rounds))
    pieces = term_pieces(inputs, cotangent, error_prev, seed_q, count)
    merged = merge(inputs, cotangent, error_prev, pieces)
    merged_other = across(merged)
    if rest:
        pieces = lax.psum(pieces, rest)
    chunk = jnp.sum(swap(pieces, chips + ("pair",)), axis=0)
    chunk, merged = lax.optimization_barrier((chunk, merged))
    half = gathered(chunk, rounds)
    half_other = across(half)
    copies = product_copies(layout, half, merged, merged_other)
    if rest:
        copies = lax.psum(copies, rest)
    basis, inverse = sweeps(layout, half, half_other)
    product = jnp.sum(swap(copies, chips), axis=0)
    product, basis, inverse = lax.optimization_barrier((product, basis, inverse))
    product_other = across(product)
    error_next, basis, second = error_of(merged, basis, inverse, product, product_other, workers)
    return (error_next, basis, second)


def solution(mesh):
    chips, rest, sizes = split_axes(mesh)
    workers = 1
    for axis in AXES:
        workers *= mesh.shape[axis]

    def run(*args):
        return local(chips, rest, sizes, workers, *args)

    return jax.shard_map(
        run,
        mesh=mesh,
        in_specs=(P(EVERYONE, None), P(EVERYONE, None), P(EVERYONE, None, None), P()),
        out_specs=(P(EVERYONE, None, None), P("groups", None), P("groups", None)),
        check_vma=False,
    )
```

```python
import functools

import jax
import jax.numpy as jnp
from jax import lax
from jax.experimental import pallas as pl
from jax.experimental.pallas import tpu as pltpu
from jax.sharding import PartitionSpec as P

AXES = ("dp", "sub", "pair")
EVERYONE = ("groups",) + AXES
VMEM_BYTES = 24 * 1024 * 1024
CHUNK = 256
GROUP = 4
BF16, F32 = jnp.bfloat16, jnp.float32
HBM = pl.BlockSpec(memory_space=pltpu.HBM)
ANY = pl.BlockSpec(memory_space=pl.ANY)
VMEM = pl.BlockSpec(memory_space=pltpu.VMEM)


def swapped(value, axis, size, bit):
    return lax.ppermute(value, axis, [(i, i ^ bit) for i in range(size)])


def across(value):
    return swapped(value, "pair", 2, 1)


def bits_of(axis, size):
    assert size & (size - 1) == 0
    return [(axis, size, 1 << i) for i in range(size.bit_length() - 1)]


def parts_of(value, count):
    parts = []
    for _ in range(count):
        part = value.astype(BF16)
        parts.append(part)
        value = value - part.astype(F32)
    return parts


def dot(a, b, dims):
    return lax.dot_general(a, b, (dims, ((), ())), preferred_element_type=F32)


def params():
    return pltpu.CompilerParams(vmem_limit_bytes=VMEM_BYTES)


def cost(flops, nbytes):
    return pl.CostEstimate(flops=flops, bytes_accessed=nbytes, transcendentals=0)


def whole_copies(pairs, sems):
    return [pltpu.make_async_copy(pair[0], pair[1], sems.at[i]) for i, pair in enumerate(pairs)]


def row_parts(source, target, parts):
    block = target.shape[0] // parts
    rows = [pl.ds(i * block, block) for i in range(parts)]
    return [(source.at[part, :], target.at[part, :]) for part in rows]


def term_kernel(x_hbm, c_hbm, e_hbm, seed_hbm, keep_ref, send_ref,
                x_ref, c_ref, e_ref, seed_ref, term_ref, sems):
    copies = whole_copies(
        [(seed_hbm, seed_ref), (c_hbm, c_ref)] + row_parts(e_hbm.at[0], e_ref, 2)
        + row_parts(x_hbm, x_ref, 2), sems)
    for copy in copies:
        copy.start()
    rank = seed_ref.shape[0]
    tokens, width = x_ref.shape
    half, piece = keep_ref.shape[1:]
    copies[0].wait()
    copies[1].wait()
    seed = jnp.concatenate(parts_of(seed_ref[...], 3), axis=0)
    mixed = added(dot(seed, c_ref[...], ((1,), (1,))), rank)
    mixed = jnp.concatenate(parts_of(mixed, 3), axis=0)
    blocks = width // CHUNK
    for i in range(blocks):
        if i % (blocks // 2) == 0:
            copies[2 + i // (blocks // 2)].wait()
        part = pl.ds(i * CHUNK, CHUNK)
        term_ref[:, part] = added(dot(seed, e_ref[part, :], ((1,), (1,))), rank)
    for t in range(2):
        copies[4 + t].wait()
        own = mixed[:, t * (tokens // 2):(t + 1) * (tokens // 2)]
        rows = pl.ds(t * (tokens // 2), tokens // 2)
        for i in range(blocks):
            part = pl.ds(i * CHUNK, CHUNK)
            term_ref[:, part] += added(dot(own, x_ref[rows, part], ((1,), (0,))), rank)
    low = lax.axis_index("pair") == 0
    for i in range(2):
        part = side(i, piece)
        top, bottom = term_ref[:half, part], term_ref[half:, part]
        keep_ref[i] = jnp.where(low, top, bottom)
        send_ref[i] = jnp.where(low, bottom, top)


def side(i, piece, start=0, size=None):
    chosen = (lax.axis_index("sub") & 1) ^ i
    return pl.ds(pl.multiple_of(chosen * piece + start, CHUNK), size or piece)


def added(stack, rank):
    total = stack[stack.shape[0] - rank:]
    for i in range(stack.shape[0] // rank - 2, -1, -1):
        total = total + stack[i * rank:(i + 1) * rank]
    return total


def term_halves(inputs, cotangent, error_prev, seed_q):
    tokens, width = inputs.shape
    out = cotangent.shape[1]
    rank = seed_q.shape[0]
    return pl.pallas_call(
        term_kernel,
        in_specs=[HBM] * 4,
        out_specs=[VMEM] * 2,
        out_shape=[jax.ShapeDtypeStruct((2, rank // 2, width // 2), F32)] * 2,
        scratch_shapes=[
            pltpu.VMEM((tokens, width), BF16),
            pltpu.VMEM((tokens, out), BF16),
            pltpu.VMEM((width, out), BF16),
            pltpu.VMEM((rank, out), F32),
            pltpu.VMEM((rank, width), F32),
            pltpu.SemaphoreType.DMA((6,)),
        ],
        compiler_params=params(),
        cost_estimate=cost(6 * tokens * rank * width, 2 * tokens * width + 2 * width * out),
        name="term",
    )(inputs, cotangent, error_prev, seed_q)


def merge_kernel(x_hbm, c_hbm, e_hbm, after_hbm, merged_ref, x_ref, c_ref, e_ref, sems):
    copies = whole_copies([(c_hbm, c_ref), (x_hbm, x_ref), (e_hbm.at[0], e_ref)], sems)
    for copy in copies:
        copy.start()
    for copy in copies:
        copy.wait()
    for i in range(merged_ref.shape[0] // CHUNK):
        part = pl.ds(i * CHUNK, CHUNK)
        merged_ref[part, :] = (
            dot(x_ref[:, part], c_ref[...], ((0,), (0,))) + e_ref[part, :].astype(F32))


def merge(inputs, cotangent, error_prev, after):
    tokens, width = inputs.shape
    out = cotangent.shape[1]
    return pl.pallas_call(
        merge_kernel,
        in_specs=[HBM] * 3 + [ANY],
        out_specs=VMEM,
        out_shape=jax.ShapeDtypeStruct((width, out), F32),
        scratch_shapes=[
            pltpu.VMEM((tokens, width), BF16),
            pltpu.VMEM((tokens, out), BF16),
            pltpu.VMEM((width, out), BF16),
            pltpu.SemaphoreType.DMA((3,)),
        ],
        compiler_params=params(),
        cost_estimate=cost(10 ** 9, 10 ** 7),
        name="merge",
    )(inputs, cotangent, error_prev, after)


def product_kernel(near_ref, far_ref, mine_ref, other_hbm, product_ref, other_ref, sems):
    half, piece = near_ref.shape
    per = piece // CHUNK
    parts = [side(i, piece, j * CHUNK, CHUNK) for i in range(2) for j in range(per)]
    copies = whole_copies([(other_hbm.at[part, :], other_ref.at[part, :]) for part in parts], sems)
    for copy in copies:
        copy.start()
    product = None
    for i, part in enumerate(parts):
        rows_ref = near_ref if i < per else far_ref
        rows = rows_ref[:, (i % per) * CHUNK:(i % per + 1) * CHUNK]
        f_high, f_low = parts_of(rows, 2)
        both = jnp.concatenate([f_high, f_low], axis=0)
        copies[i].wait()
        m_high, m_low = parts_of(mine_ref[part, :] + other_ref[part, :], 2)
        term = added(dot(both, m_high, ((1,), (0,))), half) + dot(f_high, m_low, ((1,), (0,)))
        product = term if product is None else product + term
    product_ref[...] = product


def product_of(near, far, mine, other):
    half = near.shape[0]
    width, out = mine.shape
    return pl.pallas_call(
        product_kernel,
        in_specs=[VMEM, VMEM, VMEM, ANY],
        out_shape=jax.ShapeDtypeStruct((half, out), F32),
        scratch_shapes=[
            pltpu.VMEM((width, out), F32), pltpu.SemaphoreType.DMA((width // CHUNK,))],
        compiler_params=params(),
        cost_estimate=cost(2 * half * width * out, 8 * width * out),
        name="product",
    )(near, far, mine, other)


def both_halves(mine, other):
    low = lax.axis_index("pair") == 0
    return jnp.concatenate([jnp.where(low, mine, other), jnp.where(low, other, mine)], axis=0)


def gram_blocks(rows):
    stack = jnp.concatenate(parts_of(rows, 3), axis=0)
    return dot(stack, stack, ((1,), (1,)))


def gram_of(blocks, rank):
    gram = None
    for i, j in ((2, 0), (0, 2), (1, 1), (1, 0), (0, 1), (0, 0)):
        term = blocks[i * rank:(i + 1) * rank, j * rank:(j + 1) * rank]
        gram = term if gram is None else gram + term
    return gram


def inverse_factor(gram):
    rank = gram.shape[0]
    row = lax.broadcasted_iota(jnp.int32, (rank, rank), 0)
    lane = lax.broadcasted_iota(jnp.int32, (rank, rank), 1)
    eye = jnp.where(row == lane, 1.0, 0.0).astype(F32)
    wide = jnp.concatenate([gram, eye], axis=1)
    index = lax.broadcasted_iota(jnp.int32, wide.shape, 0)
    scale = jnp.ones_like(wide)
    for base in range(0, rank, GROUP):
        columns = [
            jnp.broadcast_to(wide[:, k:k + 1], wide.shape) for k in range(base, base + GROUP)
        ]
        for j in range(GROUP):
            k = base + j
            pivot = columns[j][k:k + 1, :]
            factor = jnp.where(index > k, columns[j] * (1.0 / pivot), 0.0)
            for i in range(j + 1, GROUP):
                columns[i] = columns[i] - factor * columns[i][k:k + 1, :]
            wide = wide - factor * wide[k:k + 1, :]
            scale = jnp.where(index == k, lax.rsqrt(pivot), scale)
    return (wide * scale)[:, rank:]


def short_dot(left, right):
    a, b, c = parts_of(left, 3)
    d, e, f = parts_of(right, 3)
    lefts = jnp.concatenate([c, a, b, b, a, a], axis=1)
    rights = jnp.concatenate([d, f, e, d, e, d], axis=0)
    return dot(lefts, rights, ((1,), (0,)))


def first_sweep_kernel(mine_ref, other_ref, rows_ref, step_ref, gram_ref):
    half, piece = mine_ref.shape[1:]
    rank = 2 * half
    blocks = None
    for i in range(2):
        for j in range(piece // CHUNK):
            part = slice(j * CHUNK, (j + 1) * CHUNK)
            rows = both_halves(mine_ref[i, :, part], other_ref[i, :, part])
            rows_ref[:, side(i, piece, j * CHUNK, CHUNK)] = rows
            term = gram_blocks(rows)
            blocks = term if blocks is None else blocks + term
    step = inverse_factor(gram_of(blocks, rank))
    step_ref[...] = step
    blocks = None
    for i in range(rows_ref.shape[1] // CHUNK):
        part = slice(i * CHUNK, (i + 1) * CHUNK)
        rows = short_dot(step, rows_ref[:, part])
        rows_ref[:, part] = rows
        term = gram_blocks(rows)
        blocks = term if blocks is None else blocks + term
    gram_ref[...] = gram_of(blocks, rank)


def first_sweep(mine, other):
    _, half, piece = mine.shape
    rank, width = 2 * half, 2 * piece
    return pl.pallas_call(
        first_sweep_kernel,
        out_shape=[
            jax.ShapeDtypeStruct((rank, width), F32),
            jax.ShapeDtypeStruct((rank, rank), F32),
            jax.ShapeDtypeStruct((rank, rank), F32),
        ],
        compiler_params=params(),
        cost_estimate=cost(10 ** 9, 7 * 10 ** 6),
        name="first_sweep",
    )(mine, other)


def second_sweep_kernel(rows_ref, step_ref, gram_ref, basis_ref, inverse_ref):
    last = inverse_factor(gram_ref[...])
    for i in range(rows_ref.shape[1] // CHUNK):
        part = slice(i * CHUNK, (i + 1) * CHUNK)
        basis_ref[:, part] = short_dot(last, rows_ref[:, part])
    inverse_ref[...] = short_dot(last, step_ref[...])


def second_sweep(rows, step, gram):
    return pl.pallas_call(
        second_sweep_kernel,
        out_shape=[
            jax.ShapeDtypeStruct(rows.shape, F32),
            jax.ShapeDtypeStruct(step.shape, F32),
        ],
        compiler_params=params(),
        cost_estimate=cost(10 ** 9, 7 * 10 ** 6),
        name="second_sweep",
    )(rows, step, gram)


def error_kernel(workers, steps, merged_ref, basis_ref, inverse_ref, mine_ref, other_ref,
                 error_hbm, basis_hbm, second_ref, error_ref, error_sem, basis_sem):
    width = merged_ref.shape[0]
    block = width // steps
    keep = pltpu.make_async_copy(basis_ref, basis_hbm, basis_sem)
    keep.start()
    product = both_halves(mine_ref[...], other_ref[...])
    second = short_dot(inverse_ref[...], product) * (1.0 / workers)
    second_ref[...] = second
    s_high, s_low = parts_of(second, 2)
    rights = jnp.concatenate([s_high, s_low, s_high], axis=0)
    copies = []
    for i in range(steps):
        part = pl.ds(i * block, block)
        b_high, b_low = parts_of(basis_ref[:, part], 2)
        lefts = jnp.concatenate([b_high, b_high, b_low], axis=0)
        approx = dot(lefts, rights, ((0,), (0,)))
        error_ref[part, :] = (merged_ref[part, :] - approx).astype(BF16)
        copies.append(pltpu.make_async_copy(
            error_ref.at[part, :], error_hbm.at[0, part, :], error_sem.at[i]))
        copies[i].start()
    for copy in copies + [keep]:
        copy.wait()


def error_of(merged, basis, inverse, mine, other, workers):
    width, out = merged.shape
    rank = basis.shape[0]
    steps = width // CHUNK
    return pl.pallas_call(
        functools.partial(error_kernel, workers, steps),
        in_specs=[VMEM] * 5,
        out_specs=[HBM, HBM, VMEM],
        out_shape=[
            jax.ShapeDtypeStruct((1, width, out), BF16),
            jax.ShapeDtypeStruct((rank, width), F32),
            jax.ShapeDtypeStruct((rank, out), F32),
        ],
        scratch_shapes=[
            pltpu.VMEM((width, out), BF16),
            pltpu.SemaphoreType.DMA((steps,)),
            pltpu.SemaphoreType.DMA,
        ],
        compiler_params=params(),
        cost_estimate=cost(2 * rank * width * out, 6 * width * out),
        name="error_next",
    )(merged, basis, inverse, mine, other)


def local(sizes, *arguments):
    inputs, cotangent, error_prev, seed_q = (
        pltpu.with_memory_space_constraint(value, pltpu.HBM) for value in arguments)
    beside = ("sub", sizes["sub"], 1)
    rounds = bits_of("sub", sizes["sub"]) + bits_of("dp", sizes["dp"])
    workers = 2 * sizes["sub"] * sizes["dp"]

    keep, send = term_halves(inputs, cotangent, error_prev, seed_q)
    part = keep + across(send)
    merged = merge(inputs, cotangent, error_prev, part)
    merged_other = across(merged)
    near = part[0] + swapped(part[1], *beside)
    for axis_bit in rounds[1:]:
        near = near + swapped(near, *axis_bit)
    far = swapped(near, *beside)
    mine = jnp.stack([near, far])
    other = across(mine)

    product = product_of(near, far, merged, merged_other)
    rows, step, gram = first_sweep(mine, other)
    product = product + swapped(product, *rounds[0])
    product, rows, step, gram = lax.optimization_barrier((product, rows, step, gram))
    basis, inverse = second_sweep(rows, step, gram)
    for i, axis_bit in enumerate(rounds[1:]):
        product = product + swapped(product, *axis_bit)
        if i == 0:
            product, basis, inverse = lax.optimization_barrier((product, basis, inverse))
    product_other = across(product)
    error_next, basis, second = error_of(merged, basis, inverse, product, product_other, workers)
    return (error_next, basis, second)


def solution(mesh):
    sizes = {axis: mesh.shape[axis] for axis in AXES}
    assert sizes["pair"] == 2 and sizes["sub"] > 1

    def run(*args):
        return local(sizes, *args)

    return jax.shard_map(
        run,
        mesh=mesh,
        in_specs=(P(EVERYONE, None), P(EVERYONE, None), P(EVERYONE, None, None), P()),
        out_specs=(P(EVERYONE, None, None), P("groups", None), P("groups", None)),
        check_vma=False,
    )
```

```python
import functools

import jax
import jax.numpy as jnp
from jax import lax
from jax.experimental import pallas as pl
from jax.experimental.pallas import tpu as pltpu
from jax.sharding import PartitionSpec as P

AXES = ("dp", "sub", "pair")
EVERYONE = ("groups",) + AXES
VMEM_BYTES = 24 * 1024 * 1024
CHUNK = 256
GROUP = 4
PARTS = 4
BF16, F32 = jnp.bfloat16, jnp.float32
HBM = pl.BlockSpec(memory_space=pltpu.HBM)
ANY = pl.BlockSpec(memory_space=pl.ANY)
VMEM = pl.BlockSpec(memory_space=pltpu.VMEM)


def bits_of(axis, size):
    assert size > 1 and size & (size - 1) == 0
    return [(axis, 1 << i) for i in range(size.bit_length() - 1)]


def swapped(value, sizes, ways):
    pairs = []
    for dp in range(sizes["dp"]):
        for sub in range(sizes["sub"]):
            for pair in range(2):
                here = {"dp": dp, "sub": sub, "pair": pair}
                axis, bit = ways[pair]
                there = {**here, axis: here[axis] ^ bit}
                pairs.append(tuple(
                    (c["dp"] * sizes["sub"] + c["sub"]) * 2 + c["pair"] for c in (here, there)))
    return lax.ppermute(value, AXES, pairs)


def across(value):
    return lax.ppermute(value, "pair", [(0, 1), (1, 0)])


def sides():
    sub, dp = lax.axis_index("sub") & 1, lax.axis_index("dp") & 1
    pair = lax.axis_index("pair")
    return sub + pair * (dp - sub), dp + pair * (sub - dp)


def half_of(chosen, piece, start=0, size=None):
    return pl.ds(pl.multiple_of(chosen * piece + start, CHUNK), size or piece)


def parts_of(value, count):
    parts = []
    for _ in range(count):
        part = value.astype(BF16)
        parts.append(part)
        value = value - part.astype(F32)
    return parts


def dot(a, b, dims):
    return lax.dot_general(a, b, (dims, ((), ())), preferred_element_type=F32)


def params():
    return pltpu.CompilerParams(vmem_limit_bytes=VMEM_BYTES)


def cost(flops, nbytes):
    return pl.CostEstimate(flops=flops, bytes_accessed=nbytes, transcendentals=0)


def whole_copies(pairs, sems):
    return [pltpu.make_async_copy(pair[0], pair[1], sems.at[i]) for i, pair in enumerate(pairs)]


def row_parts(source, target, parts):
    block = target.shape[0] // parts
    rows = [pl.ds(i * block, block) for i in range(parts)]
    return [(source.at[part, :], target.at[part, :]) for part in rows]


def term_kernel(x_hbm, c_hbm, e_hbm, seed_hbm, keep_ref, send_ref,
                x_ref, c_ref, e_ref, seed_ref, term_ref, sems):
    copies = whole_copies(
        [(seed_hbm, seed_ref), (c_hbm, c_ref)] + row_parts(e_hbm.at[0], e_ref, 2)
        + row_parts(x_hbm, x_ref, 2), sems)
    for copy in copies:
        copy.start()
    rank = seed_ref.shape[0]
    tokens, width = x_ref.shape
    half, piece = keep_ref.shape[1:]
    copies[0].wait()
    copies[1].wait()
    seed = jnp.concatenate(parts_of(seed_ref[...], 3), axis=0)
    mixed = added(dot(seed, c_ref[...], ((1,), (1,))), rank)
    mixed = jnp.concatenate(parts_of(mixed, 3), axis=0)
    blocks = width // CHUNK
    for i in range(blocks):
        if i % (blocks // 2) == 0:
            copies[2 + i // (blocks // 2)].wait()
        part = pl.ds(i * CHUNK, CHUNK)
        term_ref[:, part] = added(dot(seed, e_ref[part, :], ((1,), (1,))), rank)
    for t in range(2):
        copies[4 + t].wait()
        own = mixed[:, t * (tokens // 2):(t + 1) * (tokens // 2)]
        rows = pl.ds(t * (tokens // 2), tokens // 2)
        for i in range(blocks):
            part = pl.ds(i * CHUNK, CHUNK)
            term_ref[:, part] += added(dot(own, x_ref[rows, part], ((1,), (0,))), rank)
    low = lax.axis_index("pair") == 0
    mine, other = sides()
    for i in range(2):
        part = half_of(mine ^ i, piece)
        keep_ref[i] = jnp.where(low, term_ref[:half, part], term_ref[half:, part])
        part = half_of(other ^ i, piece)
        send_ref[i] = jnp.where(low, term_ref[half:, part], term_ref[:half, part])


def added(stack, rank):
    total = stack[stack.shape[0] - rank:]
    for i in range(stack.shape[0] // rank - 2, -1, -1):
        total = total + stack[i * rank:(i + 1) * rank]
    return total


def term_halves(inputs, cotangent, error_prev, seed_q):
    tokens, width = inputs.shape
    out = cotangent.shape[1]
    rank = seed_q.shape[0]
    return pl.pallas_call(
        term_kernel,
        in_specs=[HBM] * 4,
        out_specs=[VMEM] * 2,
        out_shape=[jax.ShapeDtypeStruct((2, rank // 2, width // 2), F32)] * 2,
        scratch_shapes=[
            pltpu.VMEM((tokens, width), BF16),
            pltpu.VMEM((tokens, out), BF16),
            pltpu.VMEM((width, out), BF16),
            pltpu.VMEM((rank, out), F32),
            pltpu.VMEM((rank, width), F32),
            pltpu.SemaphoreType.DMA((6,)),
        ],
        compiler_params=params(),
        cost_estimate=cost(6 * tokens * rank * width, 2 * tokens * width + 2 * width * out),
        name="term",
    )(inputs, cotangent, error_prev, seed_q)


def merge_kernel(index, x_hbm, c_hbm, e_hbm, after_hbm, merged_ref, x_ref, c_ref, e_ref, sems):
    size = merged_ref.shape[0]
    rows = pl.ds(index * size, size)
    copies = whole_copies(
        [(c_hbm, c_ref), (x_hbm.at[:, rows], x_ref), (e_hbm.at[0, rows, :], e_ref)], sems)
    for copy in copies:
        copy.start()
    for copy in copies:
        copy.wait()
    for i in range(size // CHUNK):
        part = pl.ds(i * CHUNK, CHUNK)
        merged_ref[part, :] = (
            dot(x_ref[:, part], c_ref[...], ((0,), (0,))) + e_ref[part, :].astype(F32))


def merge(inputs, cotangent, error_prev, after, index):
    tokens, width = inputs.shape
    size, out = width // PARTS, cotangent.shape[1]
    return pl.pallas_call(
        functools.partial(merge_kernel, index),
        in_specs=[HBM] * 3 + [ANY],
        out_specs=VMEM,
        out_shape=jax.ShapeDtypeStruct((size, out), F32),
        scratch_shapes=[
            pltpu.VMEM((tokens, size), BF16),
            pltpu.VMEM((tokens, out), BF16),
            pltpu.VMEM((size, out), BF16),
            pltpu.SemaphoreType.DMA((3,)),
        ],
        compiler_params=params(),
        cost_estimate=cost(10 ** 8 // PARTS, 10 ** 6 // PARTS),
        name="merge",
    )(inputs, cotangent, error_prev, after)


def product_kernel(near_ref, far_ref, *refs):
    mine_refs, other_hbms = refs[:PARTS], refs[PARTS:2 * PARTS]
    product_ref, other_ref, sems = refs[2 * PARTS:]
    half, piece = near_ref.shape
    size = mine_refs[0].shape[0]
    copies = whole_copies(
        [(other, other_ref.at[pl.ds(i * size, size), :]) for i, other in enumerate(other_hbms)],
        sems)
    for copy in copies:
        copy.start()
    straight = sides()[0] == 0
    product = None
    for i in range(2 * piece // CHUNK):
        start = i * CHUNK
        part = slice(start % piece, start % piece + CHUNK)
        near, far = near_ref[:, part], far_ref[:, part]
        rows = jnp.where(straight, near, far) if start < piece else jnp.where(straight, far, near)
        f_high, f_low = parts_of(rows, 2)
        both = jnp.concatenate([f_high, f_low], axis=0)
        if start % size == 0:
            copies[start // size].wait()
        merged = (mine_refs[start // size][start % size:start % size + CHUNK, :]
                  + other_ref[start:start + CHUNK, :])
        m_high, m_low = parts_of(merged, 2)
        term = added(dot(both, m_high, ((1,), (0,))), half) + dot(f_high, m_low, ((1,), (0,)))
        product = term if product is None else product + term
    product_ref[...] = product


def product_of(near, far, mine, other):
    half, piece = near.shape
    out = mine[0].shape[1]
    width = 2 * piece
    return pl.pallas_call(
        product_kernel,
        in_specs=[VMEM] * (2 + PARTS) + [ANY] * PARTS,
        out_shape=jax.ShapeDtypeStruct((half, out), F32),
        scratch_shapes=[pltpu.VMEM((width, out), F32), pltpu.SemaphoreType.DMA((PARTS,))],
        compiler_params=params(),
        cost_estimate=cost(2 * half * width * out, 8 * width * out),
        name="product",
    )(near, far, *mine, *other)


def both_halves(mine, other):
    low = lax.axis_index("pair") == 0
    return jnp.concatenate([jnp.where(low, mine, other), jnp.where(low, other, mine)], axis=0)


def gram_blocks(rows):
    stack = jnp.concatenate(parts_of(rows, 3), axis=0)
    return dot(stack, stack, ((1,), (1,)))


def gram_of(blocks, rank):
    gram = None
    for i, j in ((2, 0), (0, 2), (1, 1), (1, 0), (0, 1), (0, 0)):
        term = blocks[i * rank:(i + 1) * rank, j * rank:(j + 1) * rank]
        gram = term if gram is None else gram + term
    return gram


def inverse_factor(gram):
    rank = gram.shape[0]
    row = lax.broadcasted_iota(jnp.int32, (rank, rank), 0)
    lane = lax.broadcasted_iota(jnp.int32, (rank, rank), 1)
    eye = jnp.where(row == lane, 1.0, 0.0).astype(F32)
    wide = jnp.concatenate([gram, eye], axis=1)
    index = lax.broadcasted_iota(jnp.int32, wide.shape, 0)
    scale = jnp.ones_like(wide)
    for base in range(0, rank, GROUP):
        columns = [
            jnp.broadcast_to(wide[:, k:k + 1], wide.shape) for k in range(base, base + GROUP)
        ]
        for j in range(GROUP):
            k = base + j
            pivot = columns[j][k:k + 1, :]
            factor = jnp.where(index > k, columns[j] * (1.0 / pivot), 0.0)
            for i in range(j + 1, GROUP):
                columns[i] = columns[i] - factor * columns[i][k:k + 1, :]
            wide = wide - factor * wide[k:k + 1, :]
            scale = jnp.where(index == k, lax.rsqrt(pivot), scale)
    return (wide * scale)[:, rank:]


def short_dot(left, right):
    a, b, c = parts_of(left, 3)
    d, e, f = parts_of(right, 3)
    lefts = jnp.concatenate([c, a, b, b, a, a], axis=1)
    rights = jnp.concatenate([d, f, e, d, e, d], axis=0)
    return dot(lefts, rights, ((1,), (0,)))


def first_sweep_kernel(mine_ref, other_ref, rows_ref, step_ref, gram_ref):
    half, piece = mine_ref.shape[1:]
    rank = 2 * half
    blocks = None
    mine, other = sides()
    for i in range(2):
        for j in range(piece // CHUNK):
            part = slice(j * CHUNK, (j + 1) * CHUNK)
            rows = both_halves(mine_ref[i, :, part], other_ref[i ^ mine ^ other, :, part])
            rows_ref[:, half_of(mine ^ i, piece, j * CHUNK, CHUNK)] = rows
            term = gram_blocks(rows)
            blocks = term if blocks is None else blocks + term
    step = inverse_factor(gram_of(blocks, rank))
    step_ref[...] = step
    blocks = None
    for i in range(rows_ref.shape[1] // CHUNK):
        part = slice(i * CHUNK, (i + 1) * CHUNK)
        rows = short_dot(step, rows_ref[:, part])
        rows_ref[:, part] = rows
        term = gram_blocks(rows)
        blocks = term if blocks is None else blocks + term
    gram_ref[...] = gram_of(blocks, rank)


def first_sweep(mine, other):
    _, half, piece = mine.shape
    rank, width = 2 * half, 2 * piece
    return pl.pallas_call(
        first_sweep_kernel,
        out_shape=[
            jax.ShapeDtypeStruct((rank, width), F32),
            jax.ShapeDtypeStruct((rank, rank), F32),
            jax.ShapeDtypeStruct((rank, rank), F32),
        ],
        compiler_params=params(),
        cost_estimate=cost(10 ** 9, 7 * 10 ** 6),
        name="first_sweep",
    )(mine, other)


def second_sweep_kernel(rows_ref, step_ref, gram_ref, basis_ref, inverse_ref, lefts_ref):
    last = inverse_factor(gram_ref[...])
    rank = last.shape[0]
    for i in range(rows_ref.shape[1] // CHUNK):
        part = slice(i * CHUNK, (i + 1) * CHUNK)
        basis = short_dot(last, rows_ref[:, part])
        basis_ref[:, part] = basis
        high, low = parts_of(basis, 2)
        zeros = jnp.zeros((lefts_ref.shape[1] - 3 * rank, CHUNK), BF16)
        lefts_ref[part, :] = jnp.concatenate([high, high, low, zeros], axis=0).T
    inverse_ref[...] = short_dot(last, step_ref[...])


def second_sweep(rows, step, gram):
    return pl.pallas_call(
        second_sweep_kernel,
        out_shape=[
            jax.ShapeDtypeStruct(rows.shape, F32),
            jax.ShapeDtypeStruct(step.shape, F32),
            jax.ShapeDtypeStruct((rows.shape[1], 128), BF16),
        ],
        compiler_params=params(),
        cost_estimate=cost(10 ** 9, 7 * 10 ** 6),
        name="second_sweep",
    )(rows, step, gram)


def error_kernel(workers, basis_ref, lefts_ref, inverse_ref, mine_ref, other_ref, *refs):
    merged_refs = refs[:PARTS]
    error_hbm, basis_hbm, second_ref, error_ref, error_sem, basis_sem = refs[PARTS:]
    size = merged_refs[0].shape[0]
    keep = pltpu.make_async_copy(basis_ref, basis_hbm, basis_sem)
    keep.start()
    product = both_halves(mine_ref[...], other_ref[...])
    second = short_dot(inverse_ref[...], product) * (1.0 / workers)
    second_ref[...] = second
    high, low = parts_of(second, 2)
    zeros = jnp.zeros((lefts_ref.shape[1] - 3 * high.shape[0], high.shape[1]), BF16)
    rights = jnp.concatenate([high, low, high, zeros], axis=0)
    copies = []
    for i in range(lefts_ref.shape[0] // CHUNK):
        start = i * CHUNK
        part = pl.ds(start, CHUNK)
        approx = dot(lefts_ref[part, :], rights, ((1,), (0,)))
        merged = merged_refs[start // size][start % size:start % size + CHUNK, :]
        error_ref[part, :] = (merged - approx).astype(BF16)
        copies.append(pltpu.make_async_copy(
            error_ref.at[part, :], error_hbm.at[0, part, :], error_sem.at[i]))
        copies[i].start()
    for copy in copies + [keep]:
        copy.wait()


def error_of(merged, basis, lefts, inverse, mine, other, workers):
    rank, width = basis.shape
    out = mine.shape[1]
    return pl.pallas_call(
        functools.partial(error_kernel, workers),
        in_specs=[VMEM] * (5 + PARTS),
        out_specs=[HBM, HBM, VMEM],
        out_shape=[
            jax.ShapeDtypeStruct((1, width, out), BF16),
            jax.ShapeDtypeStruct((rank, width), F32),
            jax.ShapeDtypeStruct((rank, out), F32),
        ],
        scratch_shapes=[
            pltpu.VMEM((width, out), BF16),
            pltpu.SemaphoreType.DMA((width // CHUNK,)),
            pltpu.SemaphoreType.DMA,
        ],
        compiler_params=params(),
        cost_estimate=cost(2 * rank * width * out, 6 * width * out),
        name="error_next",
    )(basis, lefts, inverse, mine, other, *merged)


def local(sizes, *arguments):
    inputs, cotangent, error_prev, seed_q = (
        pltpu.with_memory_space_constraint(value, pltpu.HBM) for value in arguments)
    sub, dp = bits_of("sub", sizes["sub"]), bits_of("dp", sizes["dp"])
    rounds = list(zip(sub[:1] + dp + sub[1:], dp + sub))
    workers = 2 * sizes["sub"] * sizes["dp"]

    keep, send = term_halves(inputs, cotangent, error_prev, seed_q)
    part = keep + across(send)
    near = part[0] + swapped(part[1], sizes, rounds[0])
    merged = [
        merge(inputs, cotangent, error_prev, part if i < PARTS // 2 else near, i)
        for i in range(PARTS)]
    merged_other = [across(rows) for rows in merged]
    for ways in rounds[1:]:
        near = near + swapped(near, sizes, ways)
    far = swapped(near, sizes, rounds[0])
    mine = jnp.stack([near, far])
    other = across(mine)

    product = product_of(near, far, merged, merged_other)
    rows, step, gram = first_sweep(mine, other)
    product = product + swapped(product, sizes, rounds[0])
    product, rows, step, gram = lax.optimization_barrier((product, rows, step, gram))
    basis, inverse, lefts = second_sweep(rows, step, gram)
    for i, ways in enumerate(rounds[1:]):
        product = product + swapped(product, sizes, ways)
        if i == 0:
            product, basis, inverse, lefts = lax.optimization_barrier(
                (product, basis, inverse, lefts))
    product_other = across(product)
    return error_of(merged, basis, lefts, inverse, product, product_other, workers)


def solution(mesh):
    sizes = {axis: mesh.shape[axis] for axis in AXES}
    assert sizes["pair"] == 2

    def run(*args):
        return tuple(local(sizes, *args))

    return jax.shard_map(
        run,
        mesh=mesh,
        in_specs=(P(EVERYONE, None), P(EVERYONE, None), P(EVERYONE, None, None), P()),
        out_specs=(P(EVERYONE, None, None), P("groups", None), P("groups", None)),
        check_vma=False,
    )
```

```python
import functools

import jax
import jax.numpy as jnp
from jax import lax
from jax.experimental import pallas as pl
from jax.experimental.pallas import tpu as pltpu
from jax.sharding import PartitionSpec as P

AXES = ("dp", "sub", "pair")
EVERYONE = ("groups",) + AXES
VMEM_BYTES = 24 * 1024 * 1024
CHUNK = 256
GROUP = 4
PARTS = 4
BF16, F32 = jnp.bfloat16, jnp.float32
HBM = pl.BlockSpec(memory_space=pltpu.HBM)
ANY = pl.BlockSpec(memory_space=pl.ANY)
VMEM = pl.BlockSpec(memory_space=pltpu.VMEM)


def bits_of(axis, size):
    assert size > 1 and size & (size - 1) == 0
    return [(axis, 1 << i) for i in range(size.bit_length() - 1)]


def swapped(value, sizes, way):
    axis, bit = way
    pairs = []
    for dp in range(sizes["dp"]):
        for sub in range(sizes["sub"]):
            here = {"dp": dp, "sub": sub}
            there = {**here, axis: here[axis] ^ bit}
            pairs.append(tuple((c["dp"] * sizes["sub"] + c["sub"]) * 2 + 1 for c in (here, there)))
    return lax.ppermute(value, AXES, pairs)


def to_first(value):
    return lax.ppermute(value, "pair", [(1, 0)])


def to_second(value):
    return lax.ppermute(value, "pair", [(0, 1)])


def of_second(mine, got):
    return jnp.where(lax.axis_index("pair") == 1, mine, got)


def side():
    return lax.axis_index("sub") & 1


def half_of(chosen, piece, start=0, size=None):
    return pl.ds(pl.multiple_of(chosen * piece + start, CHUNK), size or piece)


def parts_of(value, count):
    parts = []
    for _ in range(count):
        part = value.astype(BF16)
        parts.append(part)
        value = value - part.astype(F32)
    return parts


def dot(a, b, dims):
    return lax.dot_general(a, b, (dims, ((), ())), preferred_element_type=F32)


def params():
    return pltpu.CompilerParams(vmem_limit_bytes=VMEM_BYTES)


def cost(flops, nbytes):
    return pl.CostEstimate(flops=flops, bytes_accessed=nbytes, transcendentals=0)


def whole_copies(pairs, sems):
    return [pltpu.make_async_copy(pair[0], pair[1], sems.at[i]) for i, pair in enumerate(pairs)]


def row_parts(source, target, parts):
    block = target.shape[0] // parts
    rows = [pl.ds(i * block, block) for i in range(parts)]
    return [(source.at[part, :], target.at[part, :]) for part in rows]


def term_kernel(x_hbm, c_hbm, e_hbm, seed_hbm, halves_ref,
                x_ref, c_ref, e_ref, seed_ref, term_ref, sems):
    copies = whole_copies(
        [(seed_hbm, seed_ref), (c_hbm, c_ref)] + row_parts(e_hbm.at[0], e_ref, 2)
        + row_parts(x_hbm, x_ref, 2), sems)
    for copy in copies:
        copy.start()
    rank = seed_ref.shape[0]
    tokens, width = x_ref.shape
    piece = halves_ref.shape[2]
    copies[0].wait()
    copies[1].wait()
    seed = jnp.concatenate(parts_of(seed_ref[...], 3), axis=0)
    mixed = added(dot(seed, c_ref[...], ((1,), (1,))), rank)
    mixed = jnp.concatenate(parts_of(mixed, 3), axis=0)
    blocks = width // CHUNK
    for i in range(blocks):
        if i % (blocks // 2) == 0:
            copies[2 + i // (blocks // 2)].wait()
        part = pl.ds(i * CHUNK, CHUNK)
        term_ref[:, part] = added(dot(seed, e_ref[part, :], ((1,), (1,))), rank)
    for t in range(2):
        copies[4 + t].wait()
        own = mixed[:, t * (tokens // 2):(t + 1) * (tokens // 2)]
        rows = pl.ds(t * (tokens // 2), tokens // 2)
        for i in range(blocks):
            part = pl.ds(i * CHUNK, CHUNK)
            term_ref[:, part] += added(dot(own, x_ref[rows, part], ((1,), (0,))), rank)
    for i in range(2):
        halves_ref[i] = term_ref[:, half_of(side() ^ i, piece)]


def added(stack, rank):
    total = stack[stack.shape[0] - rank:]
    for i in range(stack.shape[0] // rank - 2, -1, -1):
        total = total + stack[i * rank:(i + 1) * rank]
    return total


def term_halves(inputs, cotangent, error_prev, seed_q):
    tokens, width = inputs.shape
    out = cotangent.shape[1]
    rank = seed_q.shape[0]
    return pl.pallas_call(
        term_kernel,
        in_specs=[HBM] * 4,
        out_specs=VMEM,
        out_shape=jax.ShapeDtypeStruct((2, rank, width // 2), F32),
        scratch_shapes=[
            pltpu.VMEM((tokens, width), BF16),
            pltpu.VMEM((tokens, out), BF16),
            pltpu.VMEM((width, out), BF16),
            pltpu.VMEM((rank, out), F32),
            pltpu.VMEM((rank, width), F32),
            pltpu.SemaphoreType.DMA((6,)),
        ],
        compiler_params=params(),
        cost_estimate=cost(6 * tokens * rank * width, 2 * tokens * width + 2 * width * out),
        name="term",
    )(inputs, cotangent, error_prev, seed_q)


def merge_kernel(x_hbm, c_hbm, e_hbm, after_hbm, *refs):
    merged_refs = refs[:PARTS]
    x_ref, c_ref, e_ref, sems = refs[PARTS:]
    size = merged_refs[0].shape[0]
    copies = whole_copies([(c_hbm, c_ref), (x_hbm, x_ref), (e_hbm.at[0], e_ref)], sems)
    for copy in copies:
        copy.start()
    for copy in copies:
        copy.wait()
    for i in range(e_ref.shape[0] // CHUNK):
        start = i * CHUNK
        part = pl.ds(start, CHUNK)
        merged_refs[start // size][start % size:start % size + CHUNK, :] = (
            dot(x_ref[:, part], c_ref[...], ((0,), (0,))) + e_ref[part, :].astype(F32))


def merge(inputs, cotangent, error_prev, after):
    tokens, width = inputs.shape
    out = cotangent.shape[1]
    return pl.pallas_call(
        merge_kernel,
        in_specs=[HBM] * 3 + [ANY],
        out_specs=[VMEM] * PARTS,
        out_shape=[jax.ShapeDtypeStruct((width // PARTS, out), F32)] * PARTS,
        scratch_shapes=[
            pltpu.VMEM((tokens, width), BF16),
            pltpu.VMEM((tokens, out), BF16),
            pltpu.VMEM((width, out), BF16),
            pltpu.SemaphoreType.DMA((3,)),
        ],
        compiler_params=params(),
        cost_estimate=cost(10 ** 8, 10 ** 6),
        name="merge",
    )(inputs, cotangent, error_prev, after)


def product_kernel(near_ref, far_ref, *refs):
    mine_refs, other_hbms = refs[:PARTS], refs[PARTS:2 * PARTS]
    product_ref, other_ref, sems = refs[2 * PARTS:]
    rank, piece = near_ref.shape
    size = mine_refs[0].shape[0]
    copies = whole_copies(
        [(other, other_ref.at[pl.ds(i * size, size), :]) for i, other in enumerate(other_hbms)],
        sems)
    for copy in copies:
        copy.start()
    straight = side() == 0
    product = None
    for i in range(2 * piece // CHUNK):
        start = i * CHUNK
        part = slice(start % piece, start % piece + CHUNK)
        near, far = near_ref[:, part], far_ref[:, part]
        rows = jnp.where(straight, near, far) if start < piece else jnp.where(straight, far, near)
        f_high, f_low = parts_of(rows, 2)
        both = jnp.concatenate([f_high, f_low], axis=0)
        if start % size == 0:
            copies[start // size].wait()
        merged = (mine_refs[start // size][start % size:start % size + CHUNK, :]
                  + other_ref[start:start + CHUNK, :])
        m_high, m_low = parts_of(merged, 2)
        term = added(dot(both, m_high, ((1,), (0,))), rank) + dot(f_high, m_low, ((1,), (0,)))
        product = term if product is None else product + term
    product_ref[...] = product


def product_of(near, far, mine, other):
    rank, piece = near.shape
    out = mine[0].shape[1]
    width = 2 * piece
    return pl.pallas_call(
        product_kernel,
        in_specs=[VMEM] * (2 + PARTS) + [ANY] * PARTS,
        out_shape=jax.ShapeDtypeStruct((rank, out), F32),
        scratch_shapes=[pltpu.VMEM((width, out), F32), pltpu.SemaphoreType.DMA((PARTS,))],
        compiler_params=params(),
        cost_estimate=cost(2 * rank * width * out, 8 * width * out),
        name="product",
    )(near, far, *mine, *other)


def gram_blocks(rows):
    stack = jnp.concatenate(parts_of(rows, 3), axis=0)
    return dot(stack, stack, ((1,), (1,)))


def gram_of(blocks, rank):
    gram = None
    for i, j in ((2, 0), (0, 2), (1, 1), (1, 0), (0, 1), (0, 0)):
        term = blocks[i * rank:(i + 1) * rank, j * rank:(j + 1) * rank]
        gram = term if gram is None else gram + term
    return gram


def inverse_factor(gram):
    rank = gram.shape[0]
    row = lax.broadcasted_iota(jnp.int32, (rank, rank), 0)
    lane = lax.broadcasted_iota(jnp.int32, (rank, rank), 1)
    eye = jnp.where(row == lane, 1.0, 0.0).astype(F32)
    wide = jnp.concatenate([gram, eye], axis=1)
    index = lax.broadcasted_iota(jnp.int32, wide.shape, 0)
    scale = jnp.ones_like(wide)
    for base in range(0, rank, GROUP):
        columns = [
            jnp.broadcast_to(wide[:, k:k + 1], wide.shape) for k in range(base, base + GROUP)
        ]
        for j in range(GROUP):
            k = base + j
            pivot = columns[j][k:k + 1, :]
            factor = jnp.where(index > k, columns[j] * (1.0 / pivot), 0.0)
            for i in range(j + 1, GROUP):
                columns[i] = columns[i] - factor * columns[i][k:k + 1, :]
            wide = wide - factor * wide[k:k + 1, :]
            scale = jnp.where(index == k, lax.rsqrt(pivot), scale)
    return (wide * scale)[:, rank:]


def short_dot(left, right):
    a, b, c = parts_of(left, 3)
    d, e, f = parts_of(right, 3)
    lefts = jnp.concatenate([c, a, b, b, a, a], axis=1)
    rights = jnp.concatenate([d, f, e, d, e, d], axis=0)
    return dot(lefts, rights, ((1,), (0,)))


def first_sweep_kernel(near_ref, far_ref, got_near_ref, got_far_ref, rows_ref, step_ref, gram_ref):
    rank, piece = near_ref.shape
    blocks = None
    for i, (mine_ref, got_ref) in enumerate([(near_ref, got_near_ref), (far_ref, got_far_ref)]):
        for j in range(piece // CHUNK):
            part = slice(j * CHUNK, (j + 1) * CHUNK)
            rows = of_second(mine_ref[:, part], got_ref[:, part])
            rows_ref[:, half_of(side() ^ i, piece, j * CHUNK, CHUNK)] = rows
            term = gram_blocks(rows)
            blocks = term if blocks is None else blocks + term
    step = inverse_factor(gram_of(blocks, rank))
    step_ref[...] = step
    blocks = None
    for i in range(rows_ref.shape[1] // CHUNK):
        part = slice(i * CHUNK, (i + 1) * CHUNK)
        rows = short_dot(step, rows_ref[:, part])
        rows_ref[:, part] = rows
        term = gram_blocks(rows)
        blocks = term if blocks is None else blocks + term
    gram_ref[...] = gram_of(blocks, rank)


def first_sweep(near, far, got_near, got_far):
    rank, piece = near.shape
    width = 2 * piece
    return pl.pallas_call(
        first_sweep_kernel,
        out_shape=[
            jax.ShapeDtypeStruct((rank, width), F32),
            jax.ShapeDtypeStruct((rank, rank), F32),
            jax.ShapeDtypeStruct((rank, rank), F32),
        ],
        compiler_params=params(),
        cost_estimate=cost(10 ** 9, 7 * 10 ** 6),
        name="first_sweep",
    )(near, far, got_near, got_far)


def second_sweep_kernel(rows_ref, step_ref, gram_ref, basis_ref, inverse_ref, lefts_ref):
    last = inverse_factor(gram_ref[...])
    rank = last.shape[0]
    for i in range(rows_ref.shape[1] // CHUNK):
        part = slice(i * CHUNK, (i + 1) * CHUNK)
        basis = short_dot(last, rows_ref[:, part])
        basis_ref[:, part] = basis
        high, low = parts_of(basis, 2)
        zeros = jnp.zeros((lefts_ref.shape[1] - 3 * rank, CHUNK), BF16)
        lefts_ref[part, :] = jnp.concatenate([high, high, low, zeros], axis=0).T
    inverse_ref[...] = short_dot(last, step_ref[...])


def second_sweep(rows, step, gram):
    return pl.pallas_call(
        second_sweep_kernel,
        out_shape=[
            jax.ShapeDtypeStruct(rows.shape, F32),
            jax.ShapeDtypeStruct(step.shape, F32),
            jax.ShapeDtypeStruct((rows.shape[1], 128), BF16),
        ],
        compiler_params=params(),
        cost_estimate=cost(10 ** 9, 7 * 10 ** 6),
        name="second_sweep",
    )(rows, step, gram)


def error_kernel(workers, basis_ref, lefts_ref, inverse_ref, mine_ref, got_ref, *refs):
    merged_refs = refs[:PARTS]
    error_hbm, basis_hbm, second_ref, error_ref, error_sem, basis_sem = refs[PARTS:]
    size = merged_refs[0].shape[0]
    keep = pltpu.make_async_copy(basis_ref, basis_hbm, basis_sem)
    keep.start()
    product = of_second(mine_ref[...], got_ref[...])
    second = short_dot(inverse_ref[...], product) * (1.0 / workers)
    second_ref[...] = second
    high, low = parts_of(second, 2)
    zeros = jnp.zeros((lefts_ref.shape[1] - 3 * high.shape[0], high.shape[1]), BF16)
    rights = jnp.concatenate([high, low, high, zeros], axis=0)
    copies = []
    for i in range(lefts_ref.shape[0] // CHUNK):
        start = i * CHUNK
        part = pl.ds(start, CHUNK)
        approx = dot(lefts_ref[part, :], rights, ((1,), (0,)))
        merged = merged_refs[start // size][start % size:start % size + CHUNK, :]
        error_ref[part, :] = (merged - approx).astype(BF16)
        copies.append(pltpu.make_async_copy(
            error_ref.at[part, :], error_hbm.at[0, part, :], error_sem.at[i]))
        copies[i].start()
    for copy in copies + [keep]:
        copy.wait()


def error_of(merged, basis, lefts, inverse, mine, got, workers):
    rank, width = basis.shape
    out = mine.shape[1]
    return pl.pallas_call(
        functools.partial(error_kernel, workers),
        in_specs=[VMEM] * (5 + PARTS),
        out_specs=[HBM, HBM, VMEM],
        out_shape=[
            jax.ShapeDtypeStruct((1, width, out), BF16),
            jax.ShapeDtypeStruct((rank, width), F32),
            jax.ShapeDtypeStruct((rank, out), F32),
        ],
        scratch_shapes=[
            pltpu.VMEM((width, out), BF16),
            pltpu.SemaphoreType.DMA((width // CHUNK,)),
            pltpu.SemaphoreType.DMA,
        ],
        compiler_params=params(),
        cost_estimate=cost(2 * rank * width * out, 6 * width * out),
        name="error_next",
    )(basis, lefts, inverse, mine, got, *merged)


def local(sizes, *arguments):
    inputs, cotangent, error_prev, seed_q = (
        pltpu.with_memory_space_constraint(value, pltpu.HBM) for value in arguments)
    rounds = bits_of("sub", sizes["sub"]) + bits_of("dp", sizes["dp"])
    workers = 2 * sizes["sub"] * sizes["dp"]

    halves = term_halves(inputs, cotangent, error_prev, seed_q)
    halves = halves + to_second(halves)
    merged = merge(inputs, cotangent, error_prev, halves)
    merged_other = [to_second(rows) for rows in merged]
    near = halves[0] + swapped(halves[1], sizes, rounds[0])
    for way in rounds[1:]:
        near = near + swapped(near, sizes, way)
    far = swapped(near, sizes, rounds[0])
    got_near, got_far = to_first(near), to_first(far)

    product = product_of(near, far, merged, merged_other)
    product, got_near, got_far = lax.optimization_barrier((product, got_near, got_far))
    rows, step, gram = first_sweep(near, far, got_near, got_far)
    product = product + swapped(product, sizes, rounds[0])
    product, rows, step, gram = lax.optimization_barrier((product, rows, step, gram))
    basis, inverse, lefts = second_sweep(rows, step, gram)
    product = product + swapped(product, sizes, rounds[1])
    product, basis, inverse, lefts = lax.optimization_barrier((product, basis, inverse, lefts))
    for way in rounds[2:]:
        product = product + swapped(product, sizes, way)
    return error_of(merged, basis, lefts, inverse, product, to_first(product), workers)


def solution(mesh):
    sizes = {axis: mesh.shape[axis] for axis in AXES}
    assert sizes["pair"] == 2

    def run(*args):
        return tuple(local(sizes, *args))

    return jax.shard_map(
        run,
        mesh=mesh,
        in_specs=(P(EVERYONE, None), P(EVERYONE, None), P(EVERYONE, None, None), P()),
        out_specs=(P(EVERYONE, None, None), P("groups", None), P("groups", None)),
        check_vma=False,
    )
```

```python
import functools

import jax
import jax.numpy as jnp
from jax import lax
from jax.experimental import pallas as pl
from jax.experimental.pallas import tpu as pltpu
from jax.sharding import PartitionSpec as P

AXES = ("dp", "sub", "pair")
EVERYONE = ("groups",) + AXES
VMEM_BYTES = 24 * 1024 * 1024
CHUNK = 256
GROUP = 4
PARTS = 4
BF16, F32 = jnp.bfloat16, jnp.float32
HBM = pl.BlockSpec(memory_space=pltpu.HBM)
ANY = pl.BlockSpec(memory_space=pl.ANY)
VMEM = pl.BlockSpec(memory_space=pltpu.VMEM)


def swapped(value, sizes, bits):
    pairs = []
    for dp in range(sizes["dp"]):
        for sub in range(sizes["sub"]):
            for pair in range(2):
                pairs.append(tuple(
                    (z * sizes["sub"] + x) * 2 + pair
                    for z, x in ((dp, sub), (dp ^ bits["dp"], sub ^ bits["sub"]))))
    return lax.ppermute(value, AXES, pairs)


def across(value):
    return lax.ppermute(value, "pair", [(0, 1), (1, 0)])


def bits_of(axis, size):
    assert size > 1 and size & (size - 1) == 0
    return [{"dp": 0, "sub": 0, axis: 1 << i} for i in range(size.bit_length() - 1)]


def both_bits(a, b):
    return {axis: a[axis] ^ b[axis] for axis in a}


def summed(value, sizes, group):
    if len(group) == 1:
        return value + swapped(value, sizes, group[0])
    one, two, three = (
        swapped(value, sizes, bits) for bits in (group[0], group[1], both_bits(*group)))
    return (value + one) + (two + three)


def parts_of(value, count):
    parts = []
    for _ in range(count):
        part = value.astype(BF16)
        parts.append(part)
        value = value - part.astype(F32)
    return parts


def dot(a, b, dims):
    return lax.dot_general(a, b, (dims, ((), ())), preferred_element_type=F32)


def params():
    return pltpu.CompilerParams(vmem_limit_bytes=VMEM_BYTES)


def cost(flops, nbytes):
    return pl.CostEstimate(flops=flops, bytes_accessed=nbytes, transcendentals=0)


def whole_copies(pairs, sems):
    return [pltpu.make_async_copy(pair[0], pair[1], sems.at[i]) for i, pair in enumerate(pairs)]


def row_parts(source, target, parts):
    block = target.shape[0] // parts
    rows = [pl.ds(i * block, block) for i in range(parts)]
    return [(source.at[part, :], target.at[part, :]) for part in rows]


def term_kernel(x_hbm, c_hbm, e_hbm, seed_hbm, keep_ref, send_ref,
                x_ref, c_ref, e_ref, seed_ref, term_ref, sems):
    copies = whole_copies(
        [(seed_hbm, seed_ref), (c_hbm, c_ref)] + row_parts(e_hbm.at[0], e_ref, 2)
        + row_parts(x_hbm, x_ref, 2), sems)
    for copy in copies:
        copy.start()
    rank = seed_ref.shape[0]
    tokens, width = x_ref.shape
    half, piece = keep_ref.shape[1:]
    copies[0].wait()
    copies[1].wait()
    seed = jnp.concatenate(parts_of(seed_ref[...], 3), axis=0)
    mixed = added(dot(seed, c_ref[...], ((1,), (1,))), rank)
    mixed = jnp.concatenate(parts_of(mixed, 3), axis=0)
    blocks = width // CHUNK
    for i in range(blocks):
        if i % (blocks // 2) == 0:
            copies[2 + i // (blocks // 2)].wait()
        part = pl.ds(i * CHUNK, CHUNK)
        term_ref[:, part] = added(dot(seed, e_ref[part, :], ((1,), (1,))), rank)
    for t in range(2):
        copies[4 + t].wait()
        own = mixed[:, t * (tokens // 2):(t + 1) * (tokens // 2)]
        rows = pl.ds(t * (tokens // 2), tokens // 2)
        for i in range(blocks):
            part = pl.ds(i * CHUNK, CHUNK)
            term_ref[:, part] += added(dot(own, x_ref[rows, part], ((1,), (0,))), rank)
    low = lax.axis_index("pair") == 0
    for i in range(2):
        part = half_of(side() ^ i, piece)
        top, bottom = term_ref[:half, part], term_ref[half:, part]
        keep_ref[i] = jnp.where(low, top, bottom)
        send_ref[i] = jnp.where(low, bottom, top)


def side():
    return lax.axis_index("sub") & 1


def half_of(chosen, piece, start=0, size=None):
    return pl.ds(pl.multiple_of(chosen * piece + start, CHUNK), size or piece)


def added(stack, rank):
    total = stack[stack.shape[0] - rank:]
    for i in range(stack.shape[0] // rank - 2, -1, -1):
        total = total + stack[i * rank:(i + 1) * rank]
    return total


def term_halves(inputs, cotangent, error_prev, seed_q):
    tokens, width = inputs.shape
    out = cotangent.shape[1]
    rank = seed_q.shape[0]
    return pl.pallas_call(
        term_kernel,
        in_specs=[HBM] * 4,
        out_specs=[VMEM] * 2,
        out_shape=[jax.ShapeDtypeStruct((2, rank // 2, width // 2), F32)] * 2,
        scratch_shapes=[
            pltpu.VMEM((tokens, width), BF16),
            pltpu.VMEM((tokens, out), BF16),
            pltpu.VMEM((width, out), BF16),
            pltpu.VMEM((rank, out), F32),
            pltpu.VMEM((rank, width), F32),
            pltpu.SemaphoreType.DMA((6,)),
        ],
        compiler_params=params(),
        cost_estimate=cost(6 * tokens * rank * width, 2 * tokens * width + 2 * width * out),
        name="term",
    )(inputs, cotangent, error_prev, seed_q)


def merge_kernel(x_hbm, c_hbm, e_hbm, after_hbm, *refs):
    merged_refs = refs[:PARTS]
    x_ref, c_ref, e_ref, sems = refs[PARTS:]
    size = merged_refs[0].shape[0]
    copies = whole_copies([(c_hbm, c_ref), (x_hbm, x_ref), (e_hbm.at[0], e_ref)], sems)
    for copy in copies:
        copy.start()
    for copy in copies:
        copy.wait()
    for i in range(e_ref.shape[0] // CHUNK):
        start = i * CHUNK
        part = pl.ds(start, CHUNK)
        merged_refs[start // size][start % size:start % size + CHUNK, :] = (
            dot(x_ref[:, part], c_ref[...], ((0,), (0,))) + e_ref[part, :].astype(F32))


def merge(inputs, cotangent, error_prev, after):
    tokens, width = inputs.shape
    out = cotangent.shape[1]
    return pl.pallas_call(
        merge_kernel,
        in_specs=[HBM] * 3 + [ANY],
        out_specs=[VMEM] * PARTS,
        out_shape=[jax.ShapeDtypeStruct((width // PARTS, out), F32)] * PARTS,
        scratch_shapes=[
            pltpu.VMEM((tokens, width), BF16),
            pltpu.VMEM((tokens, out), BF16),
            pltpu.VMEM((width, out), BF16),
            pltpu.SemaphoreType.DMA((3,)),
        ],
        compiler_params=params(),
        cost_estimate=cost(10 ** 8, 10 ** 6),
        name="merge",
    )(inputs, cotangent, error_prev, after)


def product_kernel(near_ref, far_ref, *refs):
    mine_refs, other_hbms = refs[:PARTS], refs[PARTS:2 * PARTS]
    product_ref, other_ref, sems = refs[2 * PARTS:]
    rank, piece = near_ref.shape
    size = mine_refs[0].shape[0]
    copies = whole_copies(
        [(other, other_ref.at[pl.ds(i * size, size), :]) for i, other in enumerate(other_hbms)],
        sems)
    for copy in copies:
        copy.start()
    straight = side() == 0
    product = None
    for i in range(2 * piece // CHUNK):
        start = i * CHUNK
        part = slice(start % piece, start % piece + CHUNK)
        near, far = near_ref[:, part], far_ref[:, part]
        rows = jnp.where(straight, near, far) if start < piece else jnp.where(straight, far, near)
        f_high, f_low = parts_of(rows, 2)
        both = jnp.concatenate([f_high, f_low], axis=0)
        if start % size == 0:
            copies[start // size].wait()
        merged = (mine_refs[start // size][start % size:start % size + CHUNK, :]
                  + other_ref[start:start + CHUNK, :])
        m_high, m_low = parts_of(merged, 2)
        term = added(dot(both, m_high, ((1,), (0,))), rank) + dot(f_high, m_low, ((1,), (0,)))
        product = term if product is None else product + term
    product_ref[...] = product


def product_of(near, far, mine, other):
    rank, piece = near.shape
    out = mine[0].shape[1]
    width = 2 * piece
    return pl.pallas_call(
        product_kernel,
        in_specs=[VMEM] * (2 + PARTS) + [ANY] * PARTS,
        out_shape=jax.ShapeDtypeStruct((rank, out), F32),
        scratch_shapes=[pltpu.VMEM((width, out), F32), pltpu.SemaphoreType.DMA((PARTS,))],
        compiler_params=params(),
        cost_estimate=cost(2 * rank * width * out, 8 * width * out),
        name="product",
    )(near, far, *mine, *other)


def both_halves(mine, other):
    low = lax.axis_index("pair") == 0
    return jnp.concatenate([jnp.where(low, mine, other), jnp.where(low, other, mine)], axis=0)


def gram_blocks(rows):
    stack = jnp.concatenate(parts_of(rows, 3), axis=0)
    return dot(stack, stack, ((1,), (1,)))


def gram_of(blocks, rank):
    gram = None
    for i, j in ((2, 0), (0, 2), (1, 1), (1, 0), (0, 1), (0, 0)):
        term = blocks[i * rank:(i + 1) * rank, j * rank:(j + 1) * rank]
        gram = term if gram is None else gram + term
    return gram


def inverse_factor(gram):
    rank = gram.shape[0]
    row = lax.broadcasted_iota(jnp.int32, (rank, rank), 0)
    lane = lax.broadcasted_iota(jnp.int32, (rank, rank), 1)
    eye = jnp.where(row == lane, 1.0, 0.0).astype(F32)
    wide = jnp.concatenate([gram, eye], axis=1)
    index = lax.broadcasted_iota(jnp.int32, wide.shape, 0)
    scale = jnp.ones_like(wide)
    for base in range(0, rank, GROUP):
        columns = [
            jnp.broadcast_to(wide[:, k:k + 1], wide.shape) for k in range(base, base + GROUP)
        ]
        for j in range(GROUP):
            k = base + j
            pivot = columns[j][k:k + 1, :]
            factor = jnp.where(index > k, columns[j] * (1.0 / pivot), 0.0)
            for i in range(j + 1, GROUP):
                columns[i] = columns[i] - factor * columns[i][k:k + 1, :]
            wide = wide - factor * wide[k:k + 1, :]
            scale = jnp.where(index == k, lax.rsqrt(pivot), scale)
    return (wide * scale)[:, rank:]


def short_dot(left, right):
    a, b, c = parts_of(left, 3)
    d, e, f = parts_of(right, 3)
    lefts = jnp.concatenate([c, a, b, b, a, a], axis=1)
    rights = jnp.concatenate([d, f, e, d, e, d], axis=0)
    return dot(lefts, rights, ((1,), (0,)))


def first_sweep_kernel(mine_ref, other_ref, rows_ref, step_ref, gram_ref):
    half, piece = mine_ref.shape[1:]
    rank = 2 * half
    blocks = None
    for i in range(2):
        for j in range(piece // CHUNK):
            part = slice(j * CHUNK, (j + 1) * CHUNK)
            rows = both_halves(mine_ref[i, :, part], other_ref[i, :, part])
            rows_ref[:, half_of(side() ^ i, piece, j * CHUNK, CHUNK)] = rows
            term = gram_blocks(rows)
            blocks = term if blocks is None else blocks + term
    step = inverse_factor(gram_of(blocks, rank))
    step_ref[...] = step
    blocks = None
    for i in range(rows_ref.shape[1] // CHUNK):
        part = slice(i * CHUNK, (i + 1) * CHUNK)
        rows = short_dot(step, rows_ref[:, part])
        rows_ref[:, part] = rows
        term = gram_blocks(rows)
        blocks = term if blocks is None else blocks + term
    gram_ref[...] = gram_of(blocks, rank)


def first_sweep(mine, other):
    _, half, piece = mine.shape
    rank, width = 2 * half, 2 * piece
    return pl.pallas_call(
        first_sweep_kernel,
        out_shape=[
            jax.ShapeDtypeStruct((rank, width), F32),
            jax.ShapeDtypeStruct((rank, rank), F32),
            jax.ShapeDtypeStruct((rank, rank), F32),
        ],
        compiler_params=params(),
        cost_estimate=cost(10 ** 9, 7 * 10 ** 6),
        name="first_sweep",
    )(mine, other)


def second_sweep_kernel(rows_ref, step_ref, gram_ref, basis_ref, inverse_ref):
    last = inverse_factor(gram_ref[...])
    for i in range(rows_ref.shape[1] // CHUNK):
        part = slice(i * CHUNK, (i + 1) * CHUNK)
        basis_ref[:, part] = short_dot(last, rows_ref[:, part])
    inverse_ref[...] = short_dot(last, step_ref[...])


def second_sweep(rows, step, gram):
    return pl.pallas_call(
        second_sweep_kernel,
        out_shape=[
            jax.ShapeDtypeStruct(rows.shape, F32),
            jax.ShapeDtypeStruct(step.shape, F32),
        ],
        compiler_params=params(),
        cost_estimate=cost(10 ** 9, 7 * 10 ** 6),
        name="second_sweep",
    )(rows, step, gram)


def error_kernel(workers, basis_ref, inverse_ref, mine_ref, other_ref, *refs):
    merged_refs = refs[:PARTS]
    error_hbm, basis_hbm, second_ref, error_ref, error_sem, basis_sem = refs[PARTS:]
    size = merged_refs[0].shape[0]
    keep = pltpu.make_async_copy(basis_ref, basis_hbm, basis_sem)
    keep.start()
    product = both_halves(mine_ref[...], other_ref[...])
    second = short_dot(inverse_ref[...], product) * (1.0 / workers)
    second_ref[...] = second
    s_high, s_low = parts_of(second, 2)
    rights = jnp.concatenate([s_high, s_low, s_high], axis=0)
    copies = []
    for i in range(error_ref.shape[0] // CHUNK):
        start = i * CHUNK
        part = pl.ds(start, CHUNK)
        b_high, b_low = parts_of(basis_ref[:, part], 2)
        lefts = jnp.concatenate([b_high, b_high, b_low], axis=0)
        approx = dot(lefts, rights, ((0,), (0,)))
        merged = merged_refs[start // size][start % size:start % size + CHUNK, :]
        error_ref[part, :] = (merged - approx).astype(BF16)
        copies.append(pltpu.make_async_copy(
            error_ref.at[part, :], error_hbm.at[0, part, :], error_sem.at[i]))
        copies[i].start()
    for copy in copies + [keep]:
        copy.wait()


def error_of(merged, basis, inverse, mine, other, workers):
    rank, width = basis.shape
    out = mine.shape[1]
    return pl.pallas_call(
        functools.partial(error_kernel, workers),
        in_specs=[VMEM] * (4 + PARTS),
        out_specs=[HBM, HBM, VMEM],
        out_shape=[
            jax.ShapeDtypeStruct((1, width, out), BF16),
            jax.ShapeDtypeStruct((rank, width), F32),
            jax.ShapeDtypeStruct((rank, out), F32),
        ],
        scratch_shapes=[
            pltpu.VMEM((width, out), BF16),
            pltpu.SemaphoreType.DMA((width // CHUNK,)),
            pltpu.SemaphoreType.DMA,
        ],
        compiler_params=params(),
        cost_estimate=cost(2 * rank * width * out, 6 * width * out),
        name="error_next",
    )(basis, inverse, mine, other, *merged)


def local(sizes, *arguments):
    inputs, cotangent, error_prev, seed_q = (
        pltpu.with_memory_space_constraint(value, pltpu.HBM) for value in arguments)
    rounds = bits_of("sub", sizes["sub"]) + bits_of("dp", sizes["dp"])
    beside, others = rounds[0], rounds[1:]
    workers = 2 * sizes["sub"] * sizes["dp"]

    keep, send = term_halves(inputs, cotangent, error_prev, seed_q)
    part = keep + across(send)
    merged = merge(inputs, cotangent, error_prev, part)
    merged_other = [across(rows) for rows in merged]
    near = part[0] + swapped(part[1], sizes, beside)
    for bits in others:
        near = near + swapped(near, sizes, bits)
    far = swapped(near, sizes, beside)
    mine = jnp.stack([near, far])
    other = across(mine)

    product = product_of(near, far, merged, merged_other)
    rows, step, gram = first_sweep(mine, other)
    product = summed(product, sizes, [beside])
    product, rows, step, gram = lax.optimization_barrier((product, rows, step, gram))
    basis, inverse = second_sweep(rows, step, gram)
    for i in range(0, len(others), 2):
        product = summed(product, sizes, others[i:i + 2])
    product, basis, inverse = lax.optimization_barrier((product, basis, inverse))
    return error_of(merged, basis, inverse, product, across(product), workers)


def solution(mesh):
    sizes = {axis: mesh.shape[axis] for axis in AXES}
    assert sizes["pair"] == 2

    def run(*args):
        return tuple(local(sizes, *args))

    return jax.shard_map(
        run,
        mesh=mesh,
        in_specs=(P(EVERYONE, None), P(EVERYONE, None), P(EVERYONE, None, None), P()),
        out_specs=(P(EVERYONE, None, None), P("groups", None), P("groups", None)),
        check_vma=False,
    )
```

```python
import functools

import jax
import jax.numpy as jnp
from jax import lax
from jax.experimental import pallas as pl
from jax.experimental.pallas import tpu as pltpu
from jax.sharding import PartitionSpec as P

AXES = ("dp", "sub", "pair")
EVERYONE = ("groups",) + AXES
VMEM_BYTES = 24 * 1024 * 1024
CHUNK = 256
GROUP = 4
PARTS = 4
BF16, F32 = jnp.bfloat16, jnp.float32
HBM = pl.BlockSpec(memory_space=pltpu.HBM)
ANY = pl.BlockSpec(memory_space=pl.ANY)
VMEM = pl.BlockSpec(memory_space=pltpu.VMEM)


def swapped(value, sizes, bits):
    pairs = []
    for dp in range(sizes["dp"]):
        for sub in range(sizes["sub"]):
            for pair in range(2):
                pairs.append(tuple(
                    (z * sizes["sub"] + x) * 2 + pair
                    for z, x in ((dp, sub), (dp ^ bits["dp"], sub ^ bits["sub"]))))
    return lax.ppermute(value, AXES, pairs)


def across(value):
    return lax.ppermute(value, "pair", [(0, 1), (1, 0)])


def bits_of(axis, size):
    assert size > 1 and size & (size - 1) == 0
    return [{"dp": 0, "sub": 0, axis: 1 << i} for i in range(size.bit_length() - 1)]


def parts_of(value, count):
    parts = []
    for _ in range(count):
        part = value.astype(BF16)
        parts.append(part)
        value = value - part.astype(F32)
    return parts


def dot(a, b, dims):
    return lax.dot_general(a, b, (dims, ((), ())), preferred_element_type=F32)


def params():
    return pltpu.CompilerParams(vmem_limit_bytes=VMEM_BYTES)


def cost(flops, nbytes):
    return pl.CostEstimate(flops=flops, bytes_accessed=nbytes, transcendentals=0)


def whole_copies(pairs, sems):
    return [pltpu.make_async_copy(pair[0], pair[1], sems.at[i]) for i, pair in enumerate(pairs)]


def row_parts(source, target, parts):
    block = target.shape[0] // parts
    rows = [pl.ds(i * block, block) for i in range(parts)]
    return [(source.at[part, :], target.at[part, :]) for part in rows]


def term_kernel(x_hbm, c_hbm, e_hbm, seed_hbm, keep_ref, send_ref, x_ref, c_ref, e_ref,
                seed_ref, term_ref, sems):
    copies = whole_copies(
        [(seed_hbm, seed_ref), (c_hbm, c_ref)] + row_parts(e_hbm.at[0], e_ref, 2)
        + row_parts(x_hbm, x_ref, 2), sems)
    for copy in copies:
        copy.start()
    rank = seed_ref.shape[0]
    tokens, width = x_ref.shape
    half, piece = keep_ref.shape[1:]
    copies[0].wait()
    copies[1].wait()
    seed = jnp.concatenate(parts_of(seed_ref[...], 3), axis=0)
    mixed = added(dot(seed, c_ref[...], ((1,), (1,))), rank)
    mixed = jnp.concatenate(parts_of(mixed, 3), axis=0)
    blocks = width // CHUNK
    for i in range(blocks):
        if i % (blocks // 2) == 0:
            copies[2 + i // (blocks // 2)].wait()
        part = pl.ds(i * CHUNK, CHUNK)
        term_ref[:, part] = added(dot(seed, e_ref[part, :], ((1,), (1,))), rank)
    for t in range(2):
        copies[4 + t].wait()
        own = mixed[:, t * (tokens // 2):(t + 1) * (tokens // 2)]
        rows = pl.ds(t * (tokens // 2), tokens // 2)
        for i in range(blocks):
            part = pl.ds(i * CHUNK, CHUNK)
            term_ref[:, part] += added(dot(own, x_ref[rows, part], ((1,), (0,))), rank)
    low = lax.axis_index("pair") == 0
    for i in range(2):
        part = half_of(side() ^ i, piece)
        top, bottom = term_ref[:half, part], term_ref[half:, part]
        keep_ref[i] = jnp.where(low, top, bottom)
        send_ref[i] = jnp.where(low, bottom, top)


def side():
    return lax.axis_index("sub") & 1


def half_of(chosen, piece, start=0, size=None):
    return pl.ds(pl.multiple_of(chosen * piece + start, CHUNK), size or piece)


def added(stack, rank):
    total = stack[stack.shape[0] - rank:]
    for i in range(stack.shape[0] // rank - 2, -1, -1):
        total = total + stack[i * rank:(i + 1) * rank]
    return total


def term_halves(inputs, cotangent, error_prev, seed_q):
    tokens, width = inputs.shape
    out = cotangent.shape[1]
    rank = seed_q.shape[0]
    return pl.pallas_call(
        term_kernel,
        in_specs=[HBM] * 4,
        out_specs=[VMEM] * 5,
        out_shape=[
            jax.ShapeDtypeStruct((2, rank // 2, width // 2), F32),
            jax.ShapeDtypeStruct((2, rank // 2, width // 2), F32),
            jax.ShapeDtypeStruct((tokens, width), BF16),
            jax.ShapeDtypeStruct((tokens, out), BF16),
            jax.ShapeDtypeStruct((width, out), BF16),
        ],
        scratch_shapes=[
            pltpu.VMEM((rank, out), F32),
            pltpu.VMEM((rank, width), F32),
            pltpu.SemaphoreType.DMA((6,)),
        ],
        compiler_params=params(),
        cost_estimate=cost(6 * tokens * rank * width, 2 * tokens * width + 2 * width * out),
        name="term",
    )(inputs, cotangent, error_prev, seed_q)


def merge_kernel(x_ref, c_ref, e_ref, after_ref, *merged_refs):
    size = merged_refs[0].shape[0]
    for i in range(e_ref.shape[0] // CHUNK):
        start = i * CHUNK
        part = pl.ds(start, CHUNK)
        merged_refs[start // size][start % size:start % size + CHUNK, :] = (
            dot(x_ref[:, part], c_ref[...], ((0,), (0,))) + e_ref[part, :].astype(F32))


def merge(x, c, e, after):
    width, out = e.shape
    return pl.pallas_call(
        merge_kernel,
        in_specs=[VMEM] * 3 + [ANY],
        out_specs=[VMEM] * PARTS,
        out_shape=[jax.ShapeDtypeStruct((width // PARTS, out), F32)] * PARTS,
        compiler_params=params(),
        cost_estimate=cost(10 ** 8, 10 ** 6),
        name="merge",
    )(x, c, e, after)


def product_kernel(near_ref, far_ref, *refs):
    mine_refs, other_refs, product_ref = refs[:PARTS], refs[PARTS:2 * PARTS], refs[2 * PARTS]
    rank, piece = near_ref.shape
    size = mine_refs[0].shape[0]
    straight = side() == 0
    product = None
    for i in range(2 * piece // CHUNK):
        start = i * CHUNK
        part = slice(start % piece, start % piece + CHUNK)
        near, far = near_ref[:, part], far_ref[:, part]
        rows = jnp.where(straight, near, far) if start < piece else jnp.where(straight, far, near)
        f_high, f_low = parts_of(rows, 2)
        both = jnp.concatenate([f_high, f_low], axis=0)
        rows_here = slice(start % size, start % size + CHUNK)
        merged = mine_refs[start // size][rows_here, :] + other_refs[start // size][rows_here, :]
        m_high, m_low = parts_of(merged, 2)
        term = added(dot(both, m_high, ((1,), (0,))), rank) + dot(f_high, m_low, ((1,), (0,)))
        product = term if product is None else product + term
    product_ref[...] = product


def product_of(near, far, mine, other):
    rank, piece = near.shape
    size, out = mine[0].shape
    width = 2 * piece
    return pl.pallas_call(
        product_kernel,
        out_shape=jax.ShapeDtypeStruct((rank, out), F32),
        compiler_params=params(),
        cost_estimate=cost(2 * rank * width * out, 8 * width * out),
        name="product",
    )(near, far, *mine, *other)


def both_halves(mine, other):
    low = lax.axis_index("pair") == 0
    return jnp.concatenate([jnp.where(low, mine, other), jnp.where(low, other, mine)], axis=0)


def gram_blocks(rows):
    stack = jnp.concatenate(parts_of(rows, 3), axis=0)
    return dot(stack, stack, ((1,), (1,)))


def gram_of(blocks, rank):
    gram = None
    for i, j in ((2, 0), (0, 2), (1, 1), (1, 0), (0, 1), (0, 0)):
        term = blocks[i * rank:(i + 1) * rank, j * rank:(j + 1) * rank]
        gram = term if gram is None else gram + term
    return gram


def inverse_factor(gram):
    rank = gram.shape[0]
    row = lax.broadcasted_iota(jnp.int32, (rank, rank), 0)
    lane = lax.broadcasted_iota(jnp.int32, (rank, rank), 1)
    eye = jnp.where(row == lane, 1.0, 0.0).astype(F32)
    wide = jnp.concatenate([gram, eye], axis=1)
    index = lax.broadcasted_iota(jnp.int32, wide.shape, 0)
    scale = jnp.ones_like(wide)
    for base in range(0, rank, GROUP):
        columns = [
            jnp.broadcast_to(wide[:, k:k + 1], wide.shape) for k in range(base, base + GROUP)
        ]
        for j in range(GROUP):
            k = base + j
            pivot = columns[j][k:k + 1, :]
            factor = jnp.where(index > k, columns[j] * (1.0 / pivot), 0.0)
            for i in range(j + 1, GROUP):
                columns[i] = columns[i] - factor * columns[i][k:k + 1, :]
            wide = wide - factor * wide[k:k + 1, :]
            scale = jnp.where(index == k, lax.rsqrt(pivot), scale)
    return (wide * scale)[:, rank:]


def short_dot(left, right):
    a, b, c = parts_of(left, 3)
    d, e, f = parts_of(right, 3)
    lefts = jnp.concatenate([c, a, b, b, a, a], axis=1)
    rights = jnp.concatenate([d, f, e, d, e, d], axis=0)
    return dot(lefts, rights, ((1,), (0,)))


def first_sweep_kernel(mine_ref, other_ref, rows_ref, step_ref, gram_ref):
    half, piece = mine_ref.shape[1:]
    rank = 2 * half
    blocks = None
    for i in range(2):
        for j in range(piece // CHUNK):
            part = slice(j * CHUNK, (j + 1) * CHUNK)
            rows = both_halves(mine_ref[i, :, part], other_ref[i, :, part])
            rows_ref[:, half_of(side() ^ i, piece, j * CHUNK, CHUNK)] = rows
            term = gram_blocks(rows)
            blocks = term if blocks is None else blocks + term
    step = inverse_factor(gram_of(blocks, rank))
    step_ref[...] = step
    blocks = None
    for i in range(rows_ref.shape[1] // CHUNK):
        part = slice(i * CHUNK, (i + 1) * CHUNK)
        rows = short_dot(step, rows_ref[:, part])
        rows_ref[:, part] = rows
        term = gram_blocks(rows)
        blocks = term if blocks is None else blocks + term
    gram_ref[...] = gram_of(blocks, rank)


def first_sweep(mine, other):
    _, half, piece = mine.shape
    rank, width = 2 * half, 2 * piece
    return pl.pallas_call(
        first_sweep_kernel,
        out_shape=[
            jax.ShapeDtypeStruct((rank, width), F32),
            jax.ShapeDtypeStruct((rank, rank), F32),
            jax.ShapeDtypeStruct((rank, rank), F32),
        ],
        compiler_params=params(),
        cost_estimate=cost(10 ** 9, 7 * 10 ** 6),
        name="first_sweep",
    )(mine, other)


def second_sweep_kernel(rows_ref, step_ref, gram_ref, basis_ref, inverse_ref):
    last = inverse_factor(gram_ref[...])
    for i in range(rows_ref.shape[1] // CHUNK):
        part = slice(i * CHUNK, (i + 1) * CHUNK)
        basis_ref[:, part] = short_dot(last, rows_ref[:, part])
    inverse_ref[...] = short_dot(last, step_ref[...])


def second_sweep(rows, step, gram):
    return pl.pallas_call(
        second_sweep_kernel,
        out_shape=[
            jax.ShapeDtypeStruct(rows.shape, F32),
            jax.ShapeDtypeStruct(step.shape, F32),
        ],
        compiler_params=params(),
        cost_estimate=cost(10 ** 9, 7 * 10 ** 6),
        name="second_sweep",
    )(rows, step, gram)


def error_kernel(workers, basis_ref, inverse_ref, mine_ref, other_ref, *refs):
    merged_refs = refs[:PARTS]
    error_hbm, basis_hbm, second_ref, error_ref, error_sem, basis_sem = refs[PARTS:]
    size = merged_refs[0].shape[0]
    keep = pltpu.make_async_copy(basis_ref, basis_hbm, basis_sem)
    keep.start()
    product = both_halves(mine_ref[...], other_ref[...])
    second = short_dot(inverse_ref[...], product) * (1.0 / workers)
    second_ref[...] = second
    s_high, s_low = parts_of(second, 2)
    rights = jnp.concatenate([s_high, s_low, s_high], axis=0)
    copies = []
    for i in range(error_ref.shape[0] // CHUNK):
        start = i * CHUNK
        part = pl.ds(start, CHUNK)
        b_high, b_low = parts_of(basis_ref[:, part], 2)
        lefts = jnp.concatenate([b_high, b_high, b_low], axis=0)
        approx = dot(lefts, rights, ((0,), (0,)))
        merged = merged_refs[start // size][start % size:start % size + CHUNK, :]
        error_ref[part, :] = (merged - approx).astype(BF16)
        copies.append(pltpu.make_async_copy(
            error_ref.at[part, :], error_hbm.at[0, part, :], error_sem.at[i]))
        copies[i].start()
    for copy in copies + [keep]:
        copy.wait()


def error_of(merged, basis, inverse, mine, other, workers):
    rank, width = basis.shape
    out = mine.shape[1]
    return pl.pallas_call(
        functools.partial(error_kernel, workers),
        in_specs=[VMEM] * (4 + PARTS),
        out_specs=[HBM, HBM, VMEM],
        out_shape=[
            jax.ShapeDtypeStruct((1, width, out), BF16),
            jax.ShapeDtypeStruct((rank, width), F32),
            jax.ShapeDtypeStruct((rank, out), F32),
        ],
        scratch_shapes=[
            pltpu.VMEM((width, out), BF16),
            pltpu.SemaphoreType.DMA((width // CHUNK,)),
            pltpu.SemaphoreType.DMA,
        ],
        compiler_params=params(),
        cost_estimate=cost(2 * rank * width * out, 6 * width * out),
        name="error_next",
    )(basis, inverse, mine, other, *merged)


def local(sizes, *arguments):
    inputs, cotangent, error_prev, seed_q = (
        pltpu.with_memory_space_constraint(value, pltpu.HBM) for value in arguments)
    rounds = bits_of("sub", sizes["sub"]) + bits_of("dp", sizes["dp"])
    beside, others = rounds[0], rounds[1:]
    workers = 2 * sizes["sub"] * sizes["dp"]

    keep, send, x, c, e = term_halves(inputs, cotangent, error_prev, seed_q)
    part = keep + across(send)
    near = part[0] + swapped(part[1], sizes, beside)
    merged = merge(x, c, e, part)
    merged_other = [across(rows) for rows in merged]
    for bits in others:
        near = near + swapped(near, sizes, bits)
    far = swapped(near, sizes, beside)
    mine = jnp.stack([near, far])
    other = across(mine)

    product = product_of(near, far, merged, merged_other)
    rows, step, gram = first_sweep(mine, other)
    product = product + swapped(product, sizes, beside)
    product, rows, step, gram = lax.optimization_barrier((product, rows, step, gram))
    basis, inverse = second_sweep(rows, step, gram)
    product = product + swapped(product, sizes, others[0])
    product, basis, inverse = lax.optimization_barrier((product, basis, inverse))
    for bits in others[1:]:
        product = product + swapped(product, sizes, bits)
    return error_of(merged, basis, inverse, product, across(product), workers)


def solution(mesh):
    sizes = {axis: mesh.shape[axis] for axis in AXES}
    assert sizes["pair"] == 2

    def run(*args):
        return tuple(local(sizes, *args))

    return jax.shard_map(
        run,
        mesh=mesh,
        in_specs=(P(EVERYONE, None), P(EVERYONE, None), P(EVERYONE, None, None), P()),
        out_specs=(P(EVERYONE, None, None), P("groups", None), P("groups", None)),
        check_vma=False,
    )
```

```python
import functools

import jax
import jax.numpy as jnp
from jax import lax
from jax.experimental import pallas as pl
from jax.experimental.pallas import tpu as pltpu
from jax.sharding import PartitionSpec as P

AXES = ("dp", "sub", "pair")
EVERYONE = ("groups",) + AXES
VMEM_BYTES = 24 * 1024 * 1024
CHUNK = 256
GROUP = 4
PARTS = 4
BF16, F32 = jnp.bfloat16, jnp.float32
HBM = pl.BlockSpec(memory_space=pltpu.HBM)
ANY = pl.BlockSpec(memory_space=pl.ANY)
VMEM = pl.BlockSpec(memory_space=pltpu.VMEM)


def swapped(value, sizes, bits, cores=(0, 1)):
    pairs = []
    for dp in range(sizes["dp"]):
        for sub in range(sizes["sub"]):
            for pair in range(2):
                pairs.append(tuple(
                    (z * sizes["sub"] + x) * 2 + pair
                    for z, x in ((dp, sub), (dp ^ bits["dp"], sub ^ bits["sub"])
                                 if pair in cores else (dp, sub))))
    return lax.ppermute(value, AXES, pairs)


def across(value):
    return lax.ppermute(value, "pair", [(0, 1), (1, 0)])


def bits_of(axis, size):
    assert size > 1 and size & (size - 1) == 0
    return [{"dp": 0, "sub": 0, axis: 1 << i} for i in range(size.bit_length() - 1)]


def parts_of(value, count):
    parts = []
    for _ in range(count):
        part = value.astype(BF16)
        parts.append(part)
        value = value - part.astype(F32)
    return parts


def dot(a, b, dims):
    return lax.dot_general(a, b, (dims, ((), ())), preferred_element_type=F32)


def params():
    return pltpu.CompilerParams(vmem_limit_bytes=VMEM_BYTES)


def cost(flops, nbytes):
    return pl.CostEstimate(flops=flops, bytes_accessed=nbytes, transcendentals=0)


def whole_copies(pairs, sems):
    return [pltpu.make_async_copy(pair[0], pair[1], sems.at[i]) for i, pair in enumerate(pairs)]


def row_parts(source, target, parts):
    block = target.shape[0] // parts
    rows = [pl.ds(i * block, block) for i in range(parts)]
    return [(source.at[part, :], target.at[part, :]) for part in rows]


def term_kernel(x_hbm, c_hbm, e_hbm, seed_hbm, keep_ref, send_ref, x_ref, c_ref, e_ref,
                seed_ref, term_ref, sems):
    copies = whole_copies(
        [(seed_hbm, seed_ref), (c_hbm, c_ref)] + row_parts(e_hbm.at[0], e_ref, 2)
        + row_parts(x_hbm, x_ref, 2), sems)
    for copy in copies:
        copy.start()
    rank = seed_ref.shape[0]
    tokens, width = x_ref.shape
    half, piece = keep_ref.shape[1:]
    copies[0].wait()
    copies[1].wait()
    seed = jnp.concatenate(parts_of(seed_ref[...], 3), axis=0)
    mixed = added(dot(seed, c_ref[...], ((1,), (1,))), rank)
    mixed = jnp.concatenate(parts_of(mixed, 3), axis=0)
    blocks = width // CHUNK
    for i in range(blocks):
        if i % (blocks // 2) == 0:
            copies[2 + i // (blocks // 2)].wait()
        part = pl.ds(i * CHUNK, CHUNK)
        term_ref[:, part] = added(dot(seed, e_ref[part, :], ((1,), (1,))), rank)
    for t in range(2):
        copies[4 + t].wait()
        own = mixed[:, t * (tokens // 2):(t + 1) * (tokens // 2)]
        rows = pl.ds(t * (tokens // 2), tokens // 2)
        for i in range(blocks):
            part = pl.ds(i * CHUNK, CHUNK)
            term_ref[:, part] += added(dot(own, x_ref[rows, part], ((1,), (0,))), rank)
    low = lax.axis_index("pair") == 0
    for i in range(2):
        part = half_of(side() ^ i, piece)
        top, bottom = term_ref[:half, part], term_ref[half:, part]
        keep_ref[i] = jnp.where(low, top, bottom)
        send_ref[i] = jnp.where(low, bottom, top)


def side():
    return lax.axis_index("sub") & 1


def half_of(chosen, piece, start=0, size=None):
    return pl.ds(pl.multiple_of(chosen * piece + start, CHUNK), size or piece)


def added(stack, rank):
    total = stack[stack.shape[0] - rank:]
    for i in range(stack.shape[0] // rank - 2, -1, -1):
        total = total + stack[i * rank:(i + 1) * rank]
    return total


def term_halves(inputs, cotangent, error_prev, seed_q):
    tokens, width = inputs.shape
    out = cotangent.shape[1]
    rank = seed_q.shape[0]
    return pl.pallas_call(
        term_kernel,
        in_specs=[HBM] * 4,
        out_specs=[VMEM] * 5,
        out_shape=[
            jax.ShapeDtypeStruct((2, rank // 2, width // 2), F32),
            jax.ShapeDtypeStruct((2, rank // 2, width // 2), F32),
            jax.ShapeDtypeStruct((tokens, width), BF16),
            jax.ShapeDtypeStruct((tokens, out), BF16),
            jax.ShapeDtypeStruct((width, out), BF16),
        ],
        scratch_shapes=[
            pltpu.VMEM((rank, out), F32),
            pltpu.VMEM((rank, width), F32),
            pltpu.SemaphoreType.DMA((6,)),
        ],
        compiler_params=params(),
        cost_estimate=cost(6 * tokens * rank * width, 2 * tokens * width + 2 * width * out),
        name="term",
    )(inputs, cotangent, error_prev, seed_q)


def merge_kernel(x_ref, c_ref, e_ref, after_ref, *merged_refs):
    size = merged_refs[0].shape[0]
    for i in range(e_ref.shape[0] // CHUNK):
        start = i * CHUNK
        part = pl.ds(start, CHUNK)
        merged_refs[start // size][start % size:start % size + CHUNK, :] = (
            dot(x_ref[:, part], c_ref[...], ((0,), (0,))) + e_ref[part, :].astype(F32))


def merge(x, c, e, after):
    width, out = e.shape
    return pl.pallas_call(
        merge_kernel,
        in_specs=[VMEM] * 3 + [ANY],
        out_specs=[VMEM] * PARTS,
        out_shape=[jax.ShapeDtypeStruct((width // PARTS, out), F32)] * PARTS,
        compiler_params=params(),
        cost_estimate=cost(10 ** 8, 10 ** 6),
        name="merge",
    )(x, c, e, after)


def product_kernel(mine_ref, other_ref, *refs):
    mine_refs, other_refs, product_ref = refs[:PARTS], refs[PARTS:2 * PARTS], refs[2 * PARTS]
    half, piece = mine_ref.shape[1:]
    rank = 2 * half
    size = mine_refs[0].shape[0]
    straight = side() == 0
    product = None
    for i in range(2 * piece // CHUNK):
        start = i * CHUNK
        part = slice(start % piece, start % piece + CHUNK)
        near = both_halves(mine_ref[0, :, part], other_ref[0, :, part])
        far = both_halves(mine_ref[1, :, part], other_ref[1, :, part])
        rows = jnp.where(straight, near, far) if start < piece else jnp.where(straight, far, near)
        f_high, f_low = parts_of(rows, 2)
        both = jnp.concatenate([f_high, f_low], axis=0)
        rows_here = slice(start % size, start % size + CHUNK)
        merged = mine_refs[start // size][rows_here, :] + other_refs[start // size][rows_here, :]
        m_high, m_low = parts_of(merged, 2)
        term = added(dot(both, m_high, ((1,), (0,))), rank) + dot(f_high, m_low, ((1,), (0,)))
        product = term if product is None else product + term
    product_ref[...] = product


def product_of(mine, other, merged, merged_other):
    _, half, piece = mine.shape
    rank, width, out = 2 * half, 2 * piece, merged[0].shape[1]
    return pl.pallas_call(
        product_kernel,
        out_shape=jax.ShapeDtypeStruct((rank, out), F32),
        compiler_params=params(),
        cost_estimate=cost(2 * rank * width * out, 8 * width * out),
        name="product",
    )(mine, other, *merged, *merged_other)


def both_halves(mine, other):
    low = lax.axis_index("pair") == 0
    return jnp.concatenate([jnp.where(low, mine, other), jnp.where(low, other, mine)], axis=0)


def gram_blocks(rows):
    stack = jnp.concatenate(parts_of(rows, 3), axis=0)
    return dot(stack, stack, ((1,), (1,)))


def gram_of(blocks, rank):
    gram = None
    for i, j in ((2, 0), (0, 2), (1, 1), (1, 0), (0, 1), (0, 0)):
        term = blocks[i * rank:(i + 1) * rank, j * rank:(j + 1) * rank]
        gram = term if gram is None else gram + term
    return gram


def inverse_factor(gram):
    rank = gram.shape[0]
    row = lax.broadcasted_iota(jnp.int32, (rank, rank), 0)
    lane = lax.broadcasted_iota(jnp.int32, (rank, rank), 1)
    eye = jnp.where(row == lane, 1.0, 0.0).astype(F32)
    wide = jnp.concatenate([gram, eye], axis=1)
    index = lax.broadcasted_iota(jnp.int32, wide.shape, 0)
    scale = jnp.ones_like(wide)
    for base in range(0, rank, GROUP):
        columns = [
            jnp.broadcast_to(wide[:, k:k + 1], wide.shape) for k in range(base, base + GROUP)
        ]
        for j in range(GROUP):
            k = base + j
            pivot = columns[j][k:k + 1, :]
            factor = jnp.where(index > k, columns[j] * (1.0 / pivot), 0.0)
            for i in range(j + 1, GROUP):
                columns[i] = columns[i] - factor * columns[i][k:k + 1, :]
            wide = wide - factor * wide[k:k + 1, :]
            scale = jnp.where(index == k, lax.rsqrt(pivot), scale)
    return (wide * scale)[:, rank:]


def short_dot(left, right):
    a, b, c = parts_of(left, 3)
    d, e, f = parts_of(right, 3)
    lefts = jnp.concatenate([c, a, b, b, a, a], axis=1)
    rights = jnp.concatenate([d, f, e, d, e, d], axis=0)
    return dot(lefts, rights, ((1,), (0,)))


def first_sweep_kernel(mine_ref, other_ref, rows_ref, step_ref, gram_ref):
    half, piece = mine_ref.shape[1:]
    rank = 2 * half
    blocks = None
    for i in range(2):
        for j in range(piece // CHUNK):
            part = slice(j * CHUNK, (j + 1) * CHUNK)
            rows = both_halves(mine_ref[i, :, part], other_ref[i, :, part])
            rows_ref[:, half_of(side() ^ i, piece, j * CHUNK, CHUNK)] = rows
            term = gram_blocks(rows)
            blocks = term if blocks is None else blocks + term
    step = inverse_factor(gram_of(blocks, rank))
    step_ref[...] = step
    blocks = None
    for i in range(rows_ref.shape[1] // CHUNK):
        part = slice(i * CHUNK, (i + 1) * CHUNK)
        rows = short_dot(step, rows_ref[:, part])
        rows_ref[:, part] = rows
        term = gram_blocks(rows)
        blocks = term if blocks is None else blocks + term
    gram_ref[...] = gram_of(blocks, rank)


def first_sweep(mine, other):
    _, half, piece = mine.shape
    rank, width = 2 * half, 2 * piece
    return pl.pallas_call(
        first_sweep_kernel,
        out_shape=[
            jax.ShapeDtypeStruct((rank, width), F32),
            jax.ShapeDtypeStruct((rank, rank), F32),
            jax.ShapeDtypeStruct((rank, rank), F32),
        ],
        compiler_params=params(),
        cost_estimate=cost(10 ** 9, 7 * 10 ** 6),
        name="first_sweep",
    )(mine, other)


def second_sweep_kernel(rows_ref, step_ref, gram_ref, basis_ref, inverse_ref):
    last = inverse_factor(gram_ref[...])
    for i in range(rows_ref.shape[1] // CHUNK):
        part = slice(i * CHUNK, (i + 1) * CHUNK)
        basis_ref[:, part] = short_dot(last, rows_ref[:, part])
    inverse_ref[...] = short_dot(last, step_ref[...])


def second_sweep(rows, step, gram):
    return pl.pallas_call(
        second_sweep_kernel,
        out_shape=[
            jax.ShapeDtypeStruct(rows.shape, F32),
            jax.ShapeDtypeStruct(step.shape, F32),
        ],
        compiler_params=params(),
        cost_estimate=cost(10 ** 9, 7 * 10 ** 6),
        name="second_sweep",
    )(rows, step, gram)


def error_kernel(workers, basis_ref, inverse_ref, mine_ref, other_ref, *refs):
    merged_refs = refs[:PARTS]
    error_hbm, basis_hbm, second_ref, error_ref, error_sem, basis_sem = refs[PARTS:]
    size = merged_refs[0].shape[0]
    keep = pltpu.make_async_copy(basis_ref, basis_hbm, basis_sem)
    keep.start()
    product = jnp.where(lax.axis_index("pair") == 1, mine_ref[...], other_ref[...])
    second = short_dot(inverse_ref[...], product) * (1.0 / workers)
    second_ref[...] = second
    s_high, s_low = parts_of(second, 2)
    rights = jnp.concatenate([s_high, s_low, s_high], axis=0)
    copies = []
    for i in range(error_ref.shape[0] // CHUNK):
        start = i * CHUNK
        part = pl.ds(start, CHUNK)
        b_high, b_low = parts_of(basis_ref[:, part], 2)
        lefts = jnp.concatenate([b_high, b_high, b_low], axis=0)
        approx = dot(lefts, rights, ((0,), (0,)))
        merged = merged_refs[start // size][start % size:start % size + CHUNK, :]
        error_ref[part, :] = (merged - approx).astype(BF16)
        copies.append(pltpu.make_async_copy(
            error_ref.at[part, :], error_hbm.at[0, part, :], error_sem.at[i]))
        copies[i].start()
    for copy in copies + [keep]:
        copy.wait()


def error_of(merged, basis, inverse, mine, other, workers):
    rank, width = basis.shape
    out = mine.shape[1]
    return pl.pallas_call(
        functools.partial(error_kernel, workers),
        in_specs=[VMEM] * (4 + PARTS),
        out_specs=[HBM, HBM, VMEM],
        out_shape=[
            jax.ShapeDtypeStruct((1, width, out), BF16),
            jax.ShapeDtypeStruct((rank, width), F32),
            jax.ShapeDtypeStruct((rank, out), F32),
        ],
        scratch_shapes=[
            pltpu.VMEM((width, out), BF16),
            pltpu.SemaphoreType.DMA((width // CHUNK,)),
            pltpu.SemaphoreType.DMA,
        ],
        compiler_params=params(),
        cost_estimate=cost(2 * rank * width * out, 6 * width * out),
        name="error_next",
    )(basis, inverse, mine, other, *merged)


def local(sizes, *arguments):
    inputs, cotangent, error_prev, seed_q = (
        pltpu.with_memory_space_constraint(value, pltpu.HBM) for value in arguments)
    rounds = bits_of("sub", sizes["sub"]) + bits_of("dp", sizes["dp"])
    beside, others = rounds[0], rounds[1:]
    workers = 2 * sizes["sub"] * sizes["dp"]

    keep, send, x, c, e = term_halves(inputs, cotangent, error_prev, seed_q)
    part = keep + across(send)
    near = part[0] + swapped(part[1], sizes, beside)
    merged = merge(x, c, e, part)
    merged_other = [across(rows) for rows in merged]
    for bits in others:
        near = near + swapped(near, sizes, bits)
    far = swapped(near, sizes, beside)
    mine = jnp.stack([near, far])
    other = across(mine)

    product = product_of(mine, other, merged, merged_other)
    rows, step, gram = first_sweep(mine, other)
    product = product + swapped(product, sizes, beside, (1,))
    product, rows, step, gram = lax.optimization_barrier((product, rows, step, gram))
    basis, inverse = second_sweep(rows, step, gram)
    product = product + swapped(product, sizes, others[0], (1,))
    product, basis, inverse = lax.optimization_barrier((product, basis, inverse))
    for bits in others[1:]:
        product = product + swapped(product, sizes, bits, (1,))
    return error_of(merged, basis, inverse, product, across(product), workers)


def solution(mesh):
    sizes = {axis: mesh.shape[axis] for axis in AXES}
    assert sizes["pair"] == 2

    def run(*args):
        return tuple(local(sizes, *args))

    return jax.shard_map(
        run,
        mesh=mesh,
        in_specs=(P(EVERYONE, None), P(EVERYONE, None), P(EVERYONE, None, None), P()),
        out_specs=(P(EVERYONE, None, None), P("groups", None), P("groups", None)),
        check_vma=False,
    )
```

```python
import functools

import jax
import jax.numpy as jnp
from jax import lax
from jax.experimental import pallas as pl
from jax.experimental.pallas import tpu as pltpu
from jax.sharding import PartitionSpec as P

AXES = ("dp", "sub", "pair")
EVERYONE = ("groups",) + AXES
VMEM_BYTES = 24 * 1024 * 1024
CHUNK = 256
GROUP = 4
PARTS = 4
BF16, F32 = jnp.bfloat16, jnp.float32
HBM = pl.BlockSpec(memory_space=pltpu.HBM)
ANY = pl.BlockSpec(memory_space=pl.ANY)
VMEM = pl.BlockSpec(memory_space=pltpu.VMEM)


def swapped(value, sizes, bits):
    pairs = []
    for dp in range(sizes["dp"]):
        for sub in range(sizes["sub"]):
            for pair in range(2):
                pairs.append(tuple(
                    (z * sizes["sub"] + x) * 2 + pair
                    for z, x in ((dp, sub), (dp ^ bits["dp"], sub ^ bits["sub"]))))
    return lax.ppermute(value, AXES, pairs)


def across(value):
    return lax.ppermute(value, "pair", [(0, 1), (1, 0)])


def bits_of(axis, size):
    assert size > 1 and size & (size - 1) == 0
    return [{"dp": 0, "sub": 0, axis: 1 << i} for i in range(size.bit_length() - 1)]


def parts_of(value, count):
    parts = []
    for _ in range(count):
        part = value.astype(BF16)
        parts.append(part)
        value = value - part.astype(F32)
    return parts


def dot(a, b, dims):
    return lax.dot_general(a, b, (dims, ((), ())), preferred_element_type=F32)


def params():
    return pltpu.CompilerParams(vmem_limit_bytes=VMEM_BYTES)


def cost(flops, nbytes):
    return pl.CostEstimate(flops=flops, bytes_accessed=nbytes, transcendentals=0)


def whole_copies(pairs, sems):
    return [pltpu.make_async_copy(pair[0], pair[1], sems.at[i]) for i, pair in enumerate(pairs)]


def row_parts(source, target, parts):
    block = target.shape[0] // parts
    rows = [pl.ds(i * block, block) for i in range(parts)]
    return [(source.at[part, :], target.at[part, :]) for part in rows]


def term_kernel(x_hbm, c_hbm, e_hbm, seed_hbm, keep_ref, send_ref, x_ref, c_ref, e_ref,
                seed_ref, term_ref, sems):
    copies = whole_copies(
        [(seed_hbm, seed_ref), (c_hbm, c_ref)] + row_parts(x_hbm, x_ref, 2)
        + row_parts(e_hbm.at[0], e_ref, 2), sems)
    for copy in copies:
        copy.start()
    rank = seed_ref.shape[0]
    tokens, width = x_ref.shape
    half, piece = keep_ref.shape[1:]
    copies[0].wait()
    copies[1].wait()
    seed = jnp.concatenate(parts_of(seed_ref[...], 3), axis=0)
    mixed = added(dot(seed, c_ref[...], ((1,), (1,))), rank)
    mixed = jnp.concatenate(parts_of(mixed, 3), axis=0)
    blocks = width // CHUNK
    for t in range(2):
        copies[2 + t].wait()
        own = mixed[:, t * (tokens // 2):(t + 1) * (tokens // 2)]
        rows = pl.ds(t * (tokens // 2), tokens // 2)
        for i in range(blocks):
            part = pl.ds(i * CHUNK, CHUNK)
            term = added(dot(own, x_ref[rows, part], ((1,), (0,))), rank)
            term_ref[:, part] = term if t == 0 else term_ref[:, part] + term
    for i in range(blocks):
        if i % (blocks // 2) == 0:
            copies[4 + i // (blocks // 2)].wait()
        part = pl.ds(i * CHUNK, CHUNK)
        term_ref[:, part] += added(dot(seed, e_ref[part, :], ((1,), (1,))), rank)
    low = lax.axis_index("pair") == 0
    for i in range(2):
        part = half_of(side() ^ i, piece)
        top, bottom = term_ref[:half, part], term_ref[half:, part]
        keep_ref[i] = jnp.where(low, top, bottom)
        send_ref[i] = jnp.where(low, bottom, top)


def side():
    return lax.axis_index("sub") & 1


def half_of(chosen, piece, start=0, size=None):
    return pl.ds(pl.multiple_of(chosen * piece + start, CHUNK), size or piece)


def added(stack, rank):
    total = stack[stack.shape[0] - rank:]
    for i in range(stack.shape[0] // rank - 2, -1, -1):
        total = total + stack[i * rank:(i + 1) * rank]
    return total


def term_halves(inputs, cotangent, error_prev, seed_q):
    tokens, width = inputs.shape
    out = cotangent.shape[1]
    rank = seed_q.shape[0]
    return pl.pallas_call(
        term_kernel,
        in_specs=[HBM] * 4,
        out_specs=[VMEM] * 5,
        out_shape=[
            jax.ShapeDtypeStruct((2, rank // 2, width // 2), F32),
            jax.ShapeDtypeStruct((2, rank // 2, width // 2), F32),
            jax.ShapeDtypeStruct((tokens, width), BF16),
            jax.ShapeDtypeStruct((tokens, out), BF16),
            jax.ShapeDtypeStruct((width, out), BF16),
        ],
        scratch_shapes=[
            pltpu.VMEM((rank, out), F32),
            pltpu.VMEM((rank, width), F32),
            pltpu.SemaphoreType.DMA((6,)),
        ],
        compiler_params=params(),
        cost_estimate=cost(6 * tokens * rank * width, 2 * tokens * width + 2 * width * out),
        name="term",
    )(inputs, cotangent, error_prev, seed_q)


def merge_kernel(x_ref, c_ref, e_ref, after_ref, *merged_refs):
    size = merged_refs[0].shape[0]
    for i in range(e_ref.shape[0] // CHUNK):
        start = i * CHUNK
        part = pl.ds(start, CHUNK)
        merged_refs[start // size][start % size:start % size + CHUNK, :] = (
            dot(x_ref[:, part], c_ref[...], ((0,), (0,))) + e_ref[part, :].astype(F32))


def merge(x, c, e, after):
    width, out = e.shape
    return pl.pallas_call(
        merge_kernel,
        in_specs=[VMEM] * 3 + [ANY],
        out_specs=[VMEM] * PARTS,
        out_shape=[jax.ShapeDtypeStruct((width // PARTS, out), F32)] * PARTS,
        compiler_params=params(),
        cost_estimate=cost(10 ** 8, 10 ** 6),
        name="merge",
    )(x, c, e, after)


def product_kernel(near_ref, far_ref, *refs):
    mine_refs, other_refs, product_ref = refs[:PARTS], refs[PARTS:2 * PARTS], refs[2 * PARTS]
    rank, piece = near_ref.shape
    size = mine_refs[0].shape[0]
    straight = side() == 0
    product = None
    for i in range(2 * piece // CHUNK):
        start = i * CHUNK
        part = slice(start % piece, start % piece + CHUNK)
        near, far = near_ref[:, part], far_ref[:, part]
        rows = jnp.where(straight, near, far) if start < piece else jnp.where(straight, far, near)
        f_high, f_low = parts_of(rows, 2)
        both = jnp.concatenate([f_high, f_low], axis=0)
        rows_here = slice(start % size, start % size + CHUNK)
        merged = mine_refs[start // size][rows_here, :] + other_refs[start // size][rows_here, :]
        m_high, m_low = parts_of(merged, 2)
        term = added(dot(both, m_high, ((1,), (0,))), rank) + dot(f_high, m_low, ((1,), (0,)))
        product = term if product is None else product + term
    product_ref[...] = product


def product_of(near, far, mine, other):
    rank, piece = near.shape
    size, out = mine[0].shape
    width = 2 * piece
    return pl.pallas_call(
        product_kernel,
        out_shape=jax.ShapeDtypeStruct((rank, out), F32),
        compiler_params=params(),
        cost_estimate=cost(2 * rank * width * out, 8 * width * out),
        name="product",
    )(near, far, *mine, *other)


def both_halves(mine, other):
    low = lax.axis_index("pair") == 0
    return jnp.concatenate([jnp.where(low, mine, other), jnp.where(low, other, mine)], axis=0)


def gram_blocks(rows):
    stack = jnp.concatenate(parts_of(rows, 3), axis=0)
    return dot(stack, stack, ((1,), (1,)))


def gram_of(blocks, rank):
    gram = None
    for i, j in ((2, 0), (0, 2), (1, 1), (1, 0), (0, 1), (0, 0)):
        term = blocks[i * rank:(i + 1) * rank, j * rank:(j + 1) * rank]
        gram = term if gram is None else gram + term
    return gram


def inverse_factor(gram):
    rank = gram.shape[0]
    row = lax.broadcasted_iota(jnp.int32, (rank, rank), 0)
    lane = lax.broadcasted_iota(jnp.int32, (rank, rank), 1)
    eye = jnp.where(row == lane, 1.0, 0.0).astype(F32)
    wide = jnp.concatenate([gram, eye], axis=1)
    index = lax.broadcasted_iota(jnp.int32, wide.shape, 0)
    scale = jnp.ones_like(wide)
    for base in range(0, rank, GROUP):
        columns = [
            jnp.broadcast_to(wide[:, k:k + 1], wide.shape) for k in range(base, base + GROUP)
        ]
        for j in range(GROUP):
            k = base + j
            pivot = columns[j][k:k + 1, :]
            factor = jnp.where(index > k, columns[j] * (1.0 / pivot), 0.0)
            for i in range(j + 1, GROUP):
                columns[i] = columns[i] - factor * columns[i][k:k + 1, :]
            wide = wide - factor * wide[k:k + 1, :]
            scale = jnp.where(index == k, lax.rsqrt(pivot), scale)
    return (wide * scale)[:, rank:]


def short_dot(left, right):
    a, b, c = parts_of(left, 3)
    d, e, f = parts_of(right, 3)
    lefts = jnp.concatenate([c, a, b, b, a, a], axis=1)
    rights = jnp.concatenate([d, f, e, d, e, d], axis=0)
    return dot(lefts, rights, ((1,), (0,)))


def first_sweep_kernel(mine_ref, other_ref, rows_ref, step_ref):
    half, piece = mine_ref.shape[1:]
    rank = 2 * half
    blocks = None
    for i in range(2):
        for j in range(piece // CHUNK):
            part = slice(j * CHUNK, (j + 1) * CHUNK)
            rows = both_halves(mine_ref[i, :, part], other_ref[i, :, part])
            rows_ref[:, half_of(side() ^ i, piece, j * CHUNK, CHUNK)] = rows
            term = gram_blocks(rows)
            blocks = term if blocks is None else blocks + term
    step_ref[...] = inverse_factor(gram_of(blocks, rank))


def first_sweep(mine, other):
    _, half, piece = mine.shape
    rank, width = 2 * half, 2 * piece
    return pl.pallas_call(
        first_sweep_kernel,
        out_shape=[
            jax.ShapeDtypeStruct((rank, width), F32),
            jax.ShapeDtypeStruct((rank, rank), F32),
        ],
        compiler_params=params(),
        cost_estimate=cost(10 ** 9, 7 * 10 ** 6),
        name="first_sweep",
    )(mine, other)


def second_sweep_kernel(first_ref, step_ref, rows_ref, last_ref):
    rank, width = rows_ref.shape
    step = step_ref[...]
    blocks = None
    for i in range(width // CHUNK):
        part = slice(i * CHUNK, (i + 1) * CHUNK)
        rows = short_dot(step, first_ref[:, part])
        rows_ref[:, part] = rows
        term = gram_blocks(rows)
        blocks = term if blocks is None else blocks + term
    last_ref[...] = inverse_factor(gram_of(blocks, rank))


def second_sweep(rows, step):
    return pl.pallas_call(
        second_sweep_kernel,
        out_shape=[
            jax.ShapeDtypeStruct(rows.shape, F32),
            jax.ShapeDtypeStruct(step.shape, F32),
        ],
        compiler_params=params(),
        cost_estimate=cost(10 ** 9, 7 * 10 ** 6),
        name="second_sweep",
    )(rows, step)


def basis_kernel(rows_ref, step_ref, last_ref, basis_ref, inverse_ref):
    last = last_ref[...]
    for i in range(rows_ref.shape[1] // CHUNK):
        part = slice(i * CHUNK, (i + 1) * CHUNK)
        basis_ref[:, part] = short_dot(last, rows_ref[:, part])
    inverse_ref[...] = short_dot(last, step_ref[...])


def basis_of(rows, step, last):
    return pl.pallas_call(
        basis_kernel,
        out_shape=[
            jax.ShapeDtypeStruct(rows.shape, F32),
            jax.ShapeDtypeStruct(step.shape, F32),
        ],
        compiler_params=params(),
        cost_estimate=cost(10 ** 9, 7 * 10 ** 6),
        name="basis",
    )(rows, step, last)


def error_kernel(workers, basis_ref, inverse_ref, mine_ref, other_ref, *refs):
    merged_refs = refs[:PARTS]
    error_hbm, basis_hbm, second_hbm, error_ref, second_ref, error_sem, small_sem = refs[PARTS:]
    size = merged_refs[0].shape[0]
    small = whole_copies([(basis_ref, basis_hbm), (second_ref, second_hbm)], small_sem)
    small[0].start()
    product = both_halves(mine_ref[...], other_ref[...])
    second = short_dot(inverse_ref[...], product) * (1.0 / workers)
    second_ref[...] = second
    small[1].start()
    s_high, s_low = parts_of(second, 2)
    rights = jnp.concatenate([s_high, s_low, s_high], axis=0)
    copies = []
    for i in range(error_ref.shape[0] // CHUNK):
        start = i * CHUNK
        part = pl.ds(start, CHUNK)
        b_high, b_low = parts_of(basis_ref[:, part], 2)
        lefts = jnp.concatenate([b_high, b_high, b_low], axis=0)
        approx = dot(lefts, rights, ((0,), (0,)))
        merged = merged_refs[start // size][start % size:start % size + CHUNK, :]
        error_ref[part, :] = (merged - approx).astype(BF16)
        copies.append(pltpu.make_async_copy(
            error_ref.at[part, :], error_hbm.at[0, part, :], error_sem.at[i]))
        copies[i].start()
    for copy in copies + small:
        copy.wait()


def error_of(merged, basis, inverse, mine, other, workers):
    rank, width = basis.shape
    out = mine.shape[1]
    return pl.pallas_call(
        functools.partial(error_kernel, workers),
        in_specs=[VMEM] * (4 + PARTS),
        out_specs=[HBM] * 3,
        out_shape=[
            jax.ShapeDtypeStruct((1, width, out), BF16),
            jax.ShapeDtypeStruct((rank, width), F32),
            jax.ShapeDtypeStruct((rank, out), F32),
        ],
        scratch_shapes=[
            pltpu.VMEM((width, out), BF16),
            pltpu.VMEM((rank, out), F32),
            pltpu.SemaphoreType.DMA((width // CHUNK,)),
            pltpu.SemaphoreType.DMA((2,)),
        ],
        compiler_params=params(),
        cost_estimate=cost(2 * rank * width * out, 6 * width * out),
        name="error_next",
    )(basis, inverse, mine, other, *merged)


def local(sizes, *arguments):
    inputs, cotangent, error_prev, seed_q = (
        pltpu.with_memory_space_constraint(value, pltpu.HBM) for value in arguments)
    rounds = bits_of("sub", sizes["sub"]) + bits_of("dp", sizes["dp"])
    beside, others = rounds[0], rounds[1:]
    workers = 2 * sizes["sub"] * sizes["dp"]

    keep, send, x, c, e = term_halves(inputs, cotangent, error_prev, seed_q)
    part = keep + across(send)
    near = part[0] + swapped(part[1], sizes, beside)
    merged = merge(x, c, e, part)
    merged_other = [across(rows) for rows in merged]
    for bits in others:
        near = near + swapped(near, sizes, bits)
    far = swapped(near, sizes, beside)
    mine = jnp.stack([near, far])
    other = across(mine)

    product = product_of(near, far, merged, merged_other)
    rows, step = first_sweep(mine, other)
    product = product + swapped(product, sizes, beside)
    product, rows, step = lax.optimization_barrier((product, rows, step))
    rows, last = second_sweep(rows, step)
    product = product + swapped(product, sizes, others[0])
    product, rows, step, last = lax.optimization_barrier((product, rows, step, last))
    basis, inverse = basis_of(rows, step, last)
    for bits in others[1:]:
        product = product + swapped(product, sizes, bits)
    product, basis, inverse = lax.optimization_barrier((product, basis, inverse))
    return error_of(merged, basis, inverse, product, across(product), workers)


def solution(mesh):
    sizes = {axis: mesh.shape[axis] for axis in AXES}
    assert sizes["pair"] == 2

    def run(*args):
        return tuple(local(sizes, *args))

    return jax.shard_map(
        run,
        mesh=mesh,
        in_specs=(P(EVERYONE, None), P(EVERYONE, None), P(EVERYONE, None, None), P()),
        out_specs=(P(EVERYONE, None, None), P("groups", None), P("groups", None)),
        check_vma=False,
    )
```

```python
import functools

import jax
import jax.numpy as jnp
from jax import lax
from jax.experimental import pallas as pl
from jax.experimental.pallas import tpu as pltpu
from jax.sharding import PartitionSpec as P

AXES = ("dp", "sub", "pair")
EVERYONE = ("groups",) + AXES
VMEM_BYTES = 24 * 1024 * 1024
CHUNK = 256
GROUP = 4
PARTS = 4
BF16, F32 = jnp.bfloat16, jnp.float32
HBM = pl.BlockSpec(memory_space=pltpu.HBM)
ANY = pl.BlockSpec(memory_space=pl.ANY)
VMEM = pl.BlockSpec(memory_space=pltpu.VMEM)


def swapped(value, sizes, bits):
    pairs = []
    for dp in range(sizes["dp"]):
        for sub in range(sizes["sub"]):
            for pair in range(2):
                pairs.append(tuple(
                    (z * sizes["sub"] + x) * 2 + pair
                    for z, x in ((dp, sub), (dp ^ bits["dp"], sub ^ bits["sub"]))))
    return lax.ppermute(value, AXES, pairs)


def across(value):
    return lax.ppermute(value, "pair", [(0, 1), (1, 0)])


def bits_of(axis, size):
    assert size > 1 and size & (size - 1) == 0
    return [{"dp": 0, "sub": 0, axis: 1 << i} for i in range(size.bit_length() - 1)]


def parts_of(value, count):
    parts = []
    for _ in range(count):
        part = value.astype(BF16)
        parts.append(part)
        value = value - part.astype(F32)
    return parts


def dot(a, b, dims):
    return lax.dot_general(a, b, (dims, ((), ())), preferred_element_type=F32)


def params():
    return pltpu.CompilerParams(vmem_limit_bytes=VMEM_BYTES)


def cost(flops, nbytes):
    return pl.CostEstimate(flops=flops, bytes_accessed=nbytes, transcendentals=0)


def whole_copies(pairs, sems):
    return [pltpu.make_async_copy(pair[0], pair[1], sems.at[i]) for i, pair in enumerate(pairs)]


def row_parts(source, target, parts):
    block = target.shape[0] // parts
    rows = [pl.ds(i * block, block) for i in range(parts)]
    return [(source.at[part, :], target.at[part, :]) for part in rows]


def term_kernel(x_hbm, c_hbm, e_hbm, seed_hbm, keep_ref, send_ref, x_ref, c_ref, e_ref,
                seed_ref, term_ref, sems):
    copies = whole_copies(
        [(seed_hbm, seed_ref), (c_hbm, c_ref)] + row_parts(e_hbm.at[0], e_ref, 2)
        + row_parts(x_hbm, x_ref, 2), sems)
    for copy in copies:
        copy.start()
    rank = seed_ref.shape[0]
    tokens, width = x_ref.shape
    half, piece = keep_ref.shape[1:]
    copies[0].wait()
    copies[1].wait()
    seed = jnp.concatenate(parts_of(seed_ref[...], 3), axis=0)
    mixed = added(dot(seed, c_ref[...], ((1,), (1,))), rank)
    mixed = jnp.concatenate(parts_of(mixed, 3), axis=0)
    blocks = width // CHUNK
    for i in range(blocks):
        if i % (blocks // 2) == 0:
            copies[2 + i // (blocks // 2)].wait()
        part = pl.ds(i * CHUNK, CHUNK)
        term_ref[:, part] = added(dot(seed, e_ref[part, :], ((1,), (1,))), rank)
    for t in range(2):
        copies[4 + t].wait()
        own = mixed[:, t * (tokens // 2):(t + 1) * (tokens // 2)]
        rows = pl.ds(t * (tokens // 2), tokens // 2)
        for i in range(blocks):
            part = pl.ds(i * CHUNK, CHUNK)
            term_ref[:, part] += added(dot(own, x_ref[rows, part], ((1,), (0,))), rank)
    low = lax.axis_index("pair") == 0
    for i in range(2):
        part = half_of(side() ^ i, piece)
        top, bottom = term_ref[:half, part], term_ref[half:, part]
        keep_ref[i] = jnp.where(low, top, bottom)
        send_ref[i] = jnp.where(low, bottom, top)


def side():
    return lax.axis_index("sub") & 1


def half_of(chosen, piece, start=0, size=None):
    return pl.ds(pl.multiple_of(chosen * piece + start, CHUNK), size or piece)


def added(stack, rank):
    total = stack[stack.shape[0] - rank:]
    for i in range(stack.shape[0] // rank - 2, -1, -1):
        total = total + stack[i * rank:(i + 1) * rank]
    return total


def term_halves(inputs, cotangent, error_prev, seed_q):
    tokens, width = inputs.shape
    out = cotangent.shape[1]
    rank = seed_q.shape[0]
    return pl.pallas_call(
        term_kernel,
        in_specs=[HBM] * 4,
        out_specs=[VMEM] * 5,
        out_shape=[
            jax.ShapeDtypeStruct((2, rank // 2, width // 2), F32),
            jax.ShapeDtypeStruct((2, rank // 2, width // 2), F32),
            jax.ShapeDtypeStruct((tokens, width), BF16),
            jax.ShapeDtypeStruct((tokens, out), BF16),
            jax.ShapeDtypeStruct((width, out), BF16),
        ],
        scratch_shapes=[
            pltpu.VMEM((rank, out), F32),
            pltpu.VMEM((rank, width), F32),
            pltpu.SemaphoreType.DMA((6,)),
        ],
        compiler_params=params(),
        cost_estimate=cost(6 * tokens * rank * width, 2 * tokens * width + 2 * width * out),
        name="term",
    )(inputs, cotangent, error_prev, seed_q)


def merge_kernel(x_ref, c_ref, e_ref, after_ref, *merged_refs):
    size = merged_refs[0].shape[0]
    for i in range(e_ref.shape[0] // CHUNK):
        start = i * CHUNK
        part = pl.ds(start, CHUNK)
        merged_refs[start // size][start % size:start % size + CHUNK, :] = (
            dot(x_ref[:, part], c_ref[...], ((0,), (0,))) + e_ref[part, :].astype(F32))


def merge(x, c, e, after):
    width, out = e.shape
    return pl.pallas_call(
        merge_kernel,
        in_specs=[VMEM] * 3 + [ANY],
        out_specs=[VMEM] * PARTS,
        out_shape=[jax.ShapeDtypeStruct((width // PARTS, out), F32)] * PARTS,
        compiler_params=params(),
        cost_estimate=cost(10 ** 8, 10 ** 6),
        name="merge",
    )(x, c, e, after)


def product_kernel(near_ref, far_ref, *refs):
    mine_refs, other_refs, copies_ref = refs[:PARTS], refs[PARTS:2 * PARTS], refs[2 * PARTS]
    rank, piece = near_ref.shape
    size = mine_refs[0].shape[0]
    straight = side() == 0
    product = None
    for i in range(2 * piece // CHUNK):
        start = i * CHUNK
        part = slice(start % piece, start % piece + CHUNK)
        near, far = near_ref[:, part], far_ref[:, part]
        rows = jnp.where(straight, near, far) if start < piece else jnp.where(straight, far, near)
        f_high, f_low = parts_of(rows, 2)
        both = jnp.concatenate([f_high, f_low], axis=0)
        rows_here = slice(start % size, start % size + CHUNK)
        merged = mine_refs[start // size][rows_here, :] + other_refs[start // size][rows_here, :]
        m_high, m_low = parts_of(merged, 2)
        term = added(dot(both, m_high, ((1,), (0,))), rank) + dot(f_high, m_low, ((1,), (0,)))
        product = term if product is None else product + term
    for i in range(copies_ref.shape[0]):
        copies_ref[i] = product


def product_copies(count, near, far, mine, other):
    rank, piece = near.shape
    size, out = mine[0].shape
    width = 2 * piece
    return pl.pallas_call(
        product_kernel,
        out_shape=jax.ShapeDtypeStruct((count, rank, out), F32),
        compiler_params=params(),
        cost_estimate=cost(2 * rank * width * out, 8 * width * out),
        name="product",
    )(near, far, *mine, *other)


def both_halves(mine, other):
    low = lax.axis_index("pair") == 0
    return jnp.concatenate([jnp.where(low, mine, other), jnp.where(low, other, mine)], axis=0)


def gram_blocks(rows):
    stack = jnp.concatenate(parts_of(rows, 3), axis=0)
    return dot(stack, stack, ((1,), (1,)))


def gram_of(blocks, rank):
    gram = None
    for i, j in ((2, 0), (0, 2), (1, 1), (1, 0), (0, 1), (0, 0)):
        term = blocks[i * rank:(i + 1) * rank, j * rank:(j + 1) * rank]
        gram = term if gram is None else gram + term
    return gram


def inverse_factor(gram):
    rank = gram.shape[0]
    row = lax.broadcasted_iota(jnp.int32, (rank, rank), 0)
    lane = lax.broadcasted_iota(jnp.int32, (rank, rank), 1)
    eye = jnp.where(row == lane, 1.0, 0.0).astype(F32)
    wide = jnp.concatenate([gram, eye], axis=1)
    index = lax.broadcasted_iota(jnp.int32, wide.shape, 0)
    scale = jnp.ones_like(wide)
    for base in range(0, rank, GROUP):
        columns = [
            jnp.broadcast_to(wide[:, k:k + 1], wide.shape) for k in range(base, base + GROUP)
        ]
        for j in range(GROUP):
            k = base + j
            pivot = columns[j][k:k + 1, :]
            factor = jnp.where(index > k, columns[j] * (1.0 / pivot), 0.0)
            for i in range(j + 1, GROUP):
                columns[i] = columns[i] - factor * columns[i][k:k + 1, :]
            wide = wide - factor * wide[k:k + 1, :]
            scale = jnp.where(index == k, lax.rsqrt(pivot), scale)
    return (wide * scale)[:, rank:]


def short_dot(left, right):
    a, b, c = parts_of(left, 3)
    d, e, f = parts_of(right, 3)
    lefts = jnp.concatenate([c, a, b, b, a, a], axis=1)
    rights = jnp.concatenate([d, f, e, d, e, d], axis=0)
    return dot(lefts, rights, ((1,), (0,)))


def first_sweep_kernel(mine_ref, other_ref, rows_ref, step_ref):
    half, piece = mine_ref.shape[1:]
    rank = 2 * half
    blocks = None
    for i in range(2):
        for j in range(piece // CHUNK):
            part = slice(j * CHUNK, (j + 1) * CHUNK)
            rows = both_halves(mine_ref[i, :, part], other_ref[i, :, part])
            rows_ref[:, half_of(side() ^ i, piece, j * CHUNK, CHUNK)] = rows
            term = gram_blocks(rows)
            blocks = term if blocks is None else blocks + term
    step_ref[...] = inverse_factor(gram_of(blocks, rank))


def first_sweep(mine, other):
    _, half, piece = mine.shape
    rank, width = 2 * half, 2 * piece
    return pl.pallas_call(
        first_sweep_kernel,
        out_shape=[
            jax.ShapeDtypeStruct((rank, width), F32),
            jax.ShapeDtypeStruct((rank, rank), F32),
        ],
        compiler_params=params(),
        cost_estimate=cost(10 ** 9, 7 * 10 ** 6),
        name="first_sweep",
    )(mine, other)


def second_sweep_kernel(first_ref, step_ref, rows_ref, last_ref):
    rank, width = rows_ref.shape
    step = step_ref[...]
    blocks = None
    for i in range(width // CHUNK):
        part = slice(i * CHUNK, (i + 1) * CHUNK)
        rows = short_dot(step, first_ref[:, part])
        rows_ref[:, part] = rows
        term = gram_blocks(rows)
        blocks = term if blocks is None else blocks + term
    last_ref[...] = inverse_factor(gram_of(blocks, rank))


def second_sweep(rows, step):
    return pl.pallas_call(
        second_sweep_kernel,
        out_shape=[
            jax.ShapeDtypeStruct(rows.shape, F32),
            jax.ShapeDtypeStruct(step.shape, F32),
        ],
        compiler_params=params(),
        cost_estimate=cost(10 ** 9, 7 * 10 ** 6),
        name="second_sweep",
    )(rows, step)


def basis_kernel(rows_ref, step_ref, last_ref, basis_ref, inverse_ref):
    last = last_ref[...]
    for i in range(rows_ref.shape[1] // CHUNK):
        part = slice(i * CHUNK, (i + 1) * CHUNK)
        basis_ref[:, part] = short_dot(last, rows_ref[:, part])
    inverse_ref[...] = short_dot(last, step_ref[...])


def basis_of(rows, step, last):
    return pl.pallas_call(
        basis_kernel,
        out_shape=[
            jax.ShapeDtypeStruct(rows.shape, F32),
            jax.ShapeDtypeStruct(step.shape, F32),
        ],
        compiler_params=params(),
        cost_estimate=cost(10 ** 9, 7 * 10 ** 6),
        name="basis",
    )(rows, step, last)


def error_kernel(workers, basis_ref, inverse_ref, mine_ref, other_ref, *refs):
    merged_refs = refs[:PARTS]
    error_hbm, basis_hbm, second_hbm, error_ref, second_ref, error_sem, small_sem = refs[PARTS:]
    size = merged_refs[0].shape[0]
    small = whole_copies([(basis_ref, basis_hbm), (second_ref, second_hbm)], small_sem)
    small[0].start()
    product = both_halves(mine_ref[...], other_ref[...])
    second = short_dot(inverse_ref[...], product) * (1.0 / workers)
    second_ref[...] = second
    small[1].start()
    s_high, s_low = parts_of(second, 2)
    rights = jnp.concatenate([s_high, s_low, s_high], axis=0)
    copies = []
    for i in range(error_ref.shape[0] // CHUNK):
        start = i * CHUNK
        part = pl.ds(start, CHUNK)
        b_high, b_low = parts_of(basis_ref[:, part], 2)
        lefts = jnp.concatenate([b_high, b_high, b_low], axis=0)
        approx = dot(lefts, rights, ((0,), (0,)))
        merged = merged_refs[start // size][start % size:start % size + CHUNK, :]
        error_ref[part, :] = (merged - approx).astype(BF16)
        copies.append(pltpu.make_async_copy(
            error_ref.at[part, :], error_hbm.at[0, part, :], error_sem.at[i]))
        copies[i].start()
    for copy in copies + small:
        copy.wait()


def error_of(merged, basis, inverse, mine, other, workers):
    rank, width = basis.shape
    out = mine.shape[1]
    return pl.pallas_call(
        functools.partial(error_kernel, workers),
        in_specs=[VMEM] * (4 + PARTS),
        out_specs=[HBM] * 3,
        out_shape=[
            jax.ShapeDtypeStruct((1, width, out), BF16),
            jax.ShapeDtypeStruct((rank, width), F32),
            jax.ShapeDtypeStruct((rank, out), F32),
        ],
        scratch_shapes=[
            pltpu.VMEM((width, out), BF16),
            pltpu.VMEM((rank, out), F32),
            pltpu.SemaphoreType.DMA((width // CHUNK,)),
            pltpu.SemaphoreType.DMA((2,)),
        ],
        compiler_params=params(),
        cost_estimate=cost(2 * rank * width * out, 6 * width * out),
        name="error_next",
    )(basis, inverse, mine, other, *merged)


def local(sizes, *arguments):
    inputs, cotangent, error_prev, seed_q = (
        pltpu.with_memory_space_constraint(value, pltpu.HBM) for value in arguments)
    rounds = bits_of("sub", sizes["sub"]) + bits_of("dp", sizes["dp"])
    beside, others = rounds[0], rounds[1:]
    workers = 2 * sizes["sub"] * sizes["dp"]

    keep, send, x, c, e = term_halves(inputs, cotangent, error_prev, seed_q)
    part = keep + across(send)
    near = part[0] + swapped(part[1], sizes, beside)
    merged = merge(x, c, e, part)
    merged_other = [across(rows) for rows in merged]
    for bits in others:
        near = near + swapped(near, sizes, bits)
    far = swapped(near, sizes, beside)
    mine = jnp.stack([near, far])
    other = across(mine)

    copies = product_copies(workers // 2, near, far, merged, merged_other)
    rows, step = first_sweep(mine, other)
    rows, last = second_sweep(rows, step)
    basis, inverse = basis_of(rows, step, last)
    products = lax.all_to_all(copies, ("dp", "sub"), 0, 0, tiled=True)
    product = jnp.sum(products, axis=0)
    product, basis, inverse = lax.optimization_barrier((product, basis, inverse))
    return error_of(merged, basis, inverse, product, across(product), workers)


def solution(mesh):
    sizes = {axis: mesh.shape[axis] for axis in AXES}
    assert sizes["pair"] == 2

    def run(*args):
        return tuple(local(sizes, *args))

    return jax.shard_map(
        run,
        mesh=mesh,
        in_specs=(P(EVERYONE, None), P(EVERYONE, None), P(EVERYONE, None, None), P()),
        out_specs=(P(EVERYONE, None, None), P("groups", None), P("groups", None)),
        check_vma=False,
    )
```

```python
import functools

import jax
import jax.numpy as jnp
from jax import lax
from jax.experimental import pallas as pl
from jax.experimental.pallas import tpu as pltpu
from jax.sharding import PartitionSpec as P

AXES = ("dp", "sub", "pair")
EVERYONE = ("groups",) + AXES
VMEM_BYTES = 24 * 1024 * 1024
CHUNK = 256
GROUP = 4
PARTS = 8
BF16, F32 = jnp.bfloat16, jnp.float32
HBM = pl.BlockSpec(memory_space=pltpu.HBM)
ANY = pl.BlockSpec(memory_space=pl.ANY)
VMEM = pl.BlockSpec(memory_space=pltpu.VMEM)


def swapped(value, sizes, bits):
    pairs = []
    for dp in range(sizes["dp"]):
        for sub in range(sizes["sub"]):
            for pair in range(2):
                pairs.append(tuple(
                    (z * sizes["sub"] + x) * 2 + pair
                    for z, x in ((dp, sub), (dp ^ bits["dp"], sub ^ bits["sub"]))))
    return lax.ppermute(value, AXES, pairs)


def across(value):
    return lax.ppermute(value, "pair", [(0, 1), (1, 0)])


def bits_of(axis, size):
    assert size > 1 and size & (size - 1) == 0
    return [{"dp": 0, "sub": 0, axis: 1 << i} for i in range(size.bit_length() - 1)]


def parts_of(value, count):
    parts = []
    for _ in range(count):
        part = value.astype(BF16)
        parts.append(part)
        value = value - part.astype(F32)
    return parts


def dot(a, b, dims):
    return lax.dot_general(a, b, (dims, ((), ())), preferred_element_type=F32)


def params():
    return pltpu.CompilerParams(vmem_limit_bytes=VMEM_BYTES)


def cost(flops, nbytes):
    return pl.CostEstimate(flops=flops, bytes_accessed=nbytes, transcendentals=0)


def whole_copies(pairs, sems):
    return [pltpu.make_async_copy(pair[0], pair[1], sems.at[i]) for i, pair in enumerate(pairs)]


def row_parts(source, target, parts):
    block = target.shape[0] // parts
    rows = [pl.ds(i * block, block) for i in range(parts)]
    return [(source.at[part, :], target.at[part, :]) for part in rows]


def term_kernel(x_hbm, c_hbm, e_hbm, seed_hbm, keep_ref, send_ref, x_ref, c_ref, e_ref,
                seed_ref, term_ref, sems):
    copies = whole_copies(
        [(seed_hbm, seed_ref), (c_hbm, c_ref)] + row_parts(e_hbm.at[0], e_ref, 2)
        + row_parts(x_hbm, x_ref, 2), sems)
    for copy in copies:
        copy.start()
    rank = seed_ref.shape[0]
    tokens, width = x_ref.shape
    half = keep_ref.shape[0]
    copies[0].wait()
    copies[1].wait()
    seed = jnp.concatenate(parts_of(seed_ref[...], 3), axis=0)
    mixed = added(dot(seed, c_ref[...], ((1,), (1,))), rank)
    mixed = jnp.concatenate(parts_of(mixed, 3), axis=0)
    blocks = width // CHUNK
    for i in range(blocks):
        if i % (blocks // 2) == 0:
            copies[2 + i // (blocks // 2)].wait()
        part = pl.ds(i * CHUNK, CHUNK)
        term_ref[:, part] = added(dot(seed, e_ref[part, :], ((1,), (1,))), rank)
    for t in range(2):
        copies[4 + t].wait()
        own = mixed[:, t * (tokens // 2):(t + 1) * (tokens // 2)]
        rows = pl.ds(t * (tokens // 2), tokens // 2)
        for i in range(blocks):
            part = pl.ds(i * CHUNK, CHUNK)
            term_ref[:, part] += added(dot(own, x_ref[rows, part], ((1,), (0,))), rank)
    low = lax.axis_index("pair") == 0
    keep_ref[...] = jnp.where(low, term_ref[:half, :], term_ref[half:, :])
    send_ref[...] = jnp.where(low, term_ref[half:, :], term_ref[:half, :])


def added(stack, rank):
    total = stack[stack.shape[0] - rank:]
    for i in range(stack.shape[0] // rank - 2, -1, -1):
        total = total + stack[i * rank:(i + 1) * rank]
    return total


def term_halves(inputs, cotangent, error_prev, seed_q):
    tokens, width = inputs.shape
    out = cotangent.shape[1]
    rank = seed_q.shape[0]
    return pl.pallas_call(
        term_kernel,
        in_specs=[HBM] * 4,
        out_specs=[VMEM] * 5,
        out_shape=[
            jax.ShapeDtypeStruct((rank // 2, width), F32),
            jax.ShapeDtypeStruct((rank // 2, width), F32),
            jax.ShapeDtypeStruct((tokens, width), BF16),
            jax.ShapeDtypeStruct((tokens, out), BF16),
            jax.ShapeDtypeStruct((width, out), BF16),
        ],
        scratch_shapes=[
            pltpu.VMEM((rank, out), F32),
            pltpu.VMEM((rank, width), F32),
            pltpu.SemaphoreType.DMA((6,)),
        ],
        compiler_params=params(),
        cost_estimate=cost(6 * tokens * rank * width, 2 * tokens * width + 2 * width * out),
        name="term",
    )(inputs, cotangent, error_prev, seed_q)


def merge_kernel(x_ref, c_ref, e_ref, after_ref, *merged_refs):
    size = merged_refs[0].shape[0]
    for i in range(e_ref.shape[0] // CHUNK):
        start = i * CHUNK
        part = pl.ds(start, CHUNK)
        merged_refs[start // size][start % size:start % size + CHUNK, :] = (
            dot(x_ref[:, part], c_ref[...], ((0,), (0,))) + e_ref[part, :].astype(F32))


def merge(x, c, e, after):
    width, out = e.shape
    return pl.pallas_call(
        merge_kernel,
        in_specs=[VMEM] * 3 + [ANY],
        out_specs=[VMEM] * PARTS,
        out_shape=[jax.ShapeDtypeStruct((width // PARTS, out), F32)] * PARTS,
        compiler_params=params(),
        cost_estimate=cost(10 ** 8, 10 ** 6),
        name="merge",
    )(x, c, e, after)


def product_kernel(first_ref, *refs):
    mine_refs, other_refs, product_ref = refs[:PARTS], refs[PARTS:2 * PARTS], refs[2 * PARTS]
    rank, width = first_ref.shape
    size = mine_refs[0].shape[0]
    product = None
    for i in range(width // CHUNK):
        start = i * CHUNK
        rows = first_ref[:, start:start + CHUNK]
        f_high, f_low = parts_of(rows, 2)
        both = jnp.concatenate([f_high, f_low], axis=0)
        rows_here = slice(start % size, start % size + CHUNK)
        merged = mine_refs[start // size][rows_here, :] + other_refs[start // size][rows_here, :]
        m_high, m_low = parts_of(merged, 2)
        term = added(dot(both, m_high, ((1,), (0,))), rank) + dot(f_high, m_low, ((1,), (0,)))
        product = term if product is None else product + term
    product_ref[...] = product


def product_of(first, mine, other):
    rank, width = first.shape
    out = mine[0].shape[1]
    return pl.pallas_call(
        product_kernel,
        out_shape=jax.ShapeDtypeStruct((rank, out), F32),
        compiler_params=params(),
        cost_estimate=cost(2 * rank * width * out, 8 * width * out),
        name="product",
    )(first, *mine, *other)


def both_halves(mine, other):
    low = lax.axis_index("pair") == 0
    return jnp.concatenate([jnp.where(low, mine, other), jnp.where(low, other, mine)], axis=0)


def gram_blocks(rows):
    stack = jnp.concatenate(parts_of(rows, 3), axis=0)
    return dot(stack, stack, ((1,), (1,)))


def gram_of(blocks, rank):
    gram = None
    for i, j in ((2, 0), (0, 2), (1, 1), (1, 0), (0, 1), (0, 0)):
        term = blocks[i * rank:(i + 1) * rank, j * rank:(j + 1) * rank]
        gram = term if gram is None else gram + term
    return gram


def inverse_factor(gram):
    rank = gram.shape[0]
    row = lax.broadcasted_iota(jnp.int32, (rank, rank), 0)
    lane = lax.broadcasted_iota(jnp.int32, (rank, rank), 1)
    eye = jnp.where(row == lane, 1.0, 0.0).astype(F32)
    wide = jnp.concatenate([gram, eye], axis=1)
    index = lax.broadcasted_iota(jnp.int32, wide.shape, 0)
    scale = jnp.ones_like(wide)
    for base in range(0, rank, GROUP):
        columns = [
            jnp.broadcast_to(wide[:, k:k + 1], wide.shape) for k in range(base, base + GROUP)
        ]
        for j in range(GROUP):
            k = base + j
            pivot = columns[j][k:k + 1, :]
            factor = jnp.where(index > k, columns[j] * (1.0 / pivot), 0.0)
            for i in range(j + 1, GROUP):
                columns[i] = columns[i] - factor * columns[i][k:k + 1, :]
            wide = wide - factor * wide[k:k + 1, :]
            scale = jnp.where(index == k, lax.rsqrt(pivot), scale)
    return (wide * scale)[:, rank:]


def short_dot(left, right):
    a, b, c = parts_of(left, 3)
    d, e, f = parts_of(right, 3)
    lefts = jnp.concatenate([c, a, b, b, a, a], axis=1)
    rights = jnp.concatenate([d, f, e, d, e, d], axis=0)
    return dot(lefts, rights, ((1,), (0,)))


def first_sweep_kernel(mine_ref, other_ref, rows_ref, step_ref):
    rank, width = rows_ref.shape
    blocks = None
    for i in range(width // CHUNK):
        part = slice(i * CHUNK, (i + 1) * CHUNK)
        rows = both_halves(mine_ref[:, part], other_ref[:, part])
        rows_ref[:, part] = rows
        term = gram_blocks(rows)
        blocks = term if blocks is None else blocks + term
    step_ref[...] = inverse_factor(gram_of(blocks, rank))


def first_sweep(mine, other):
    half, width = mine.shape
    rank = 2 * half
    return pl.pallas_call(
        first_sweep_kernel,
        out_shape=[
            jax.ShapeDtypeStruct((rank, width), F32),
            jax.ShapeDtypeStruct((rank, rank), F32),
        ],
        compiler_params=params(),
        cost_estimate=cost(10 ** 9, 7 * 10 ** 6),
        name="first_sweep",
    )(mine, other)


def second_sweep_kernel(first_ref, step_ref, rows_ref, last_ref):
    rank, width = rows_ref.shape
    step = step_ref[...]
    blocks = None
    for i in range(width // CHUNK):
        part = slice(i * CHUNK, (i + 1) * CHUNK)
        rows = short_dot(step, first_ref[:, part])
        rows_ref[:, part] = rows
        term = gram_blocks(rows)
        blocks = term if blocks is None else blocks + term
    last_ref[...] = inverse_factor(gram_of(blocks, rank))


def second_sweep(rows, step):
    return pl.pallas_call(
        second_sweep_kernel,
        out_shape=[
            jax.ShapeDtypeStruct(rows.shape, F32),
            jax.ShapeDtypeStruct(step.shape, F32),
        ],
        compiler_params=params(),
        cost_estimate=cost(10 ** 9, 7 * 10 ** 6),
        name="second_sweep",
    )(rows, step)


def basis_kernel(rows_ref, step_ref, last_ref, basis_ref, inverse_ref):
    last = last_ref[...]
    for i in range(rows_ref.shape[1] // CHUNK):
        part = slice(i * CHUNK, (i + 1) * CHUNK)
        basis_ref[:, part] = short_dot(last, rows_ref[:, part])
    inverse_ref[...] = short_dot(last, step_ref[...])


def basis_of(rows, step, last):
    return pl.pallas_call(
        basis_kernel,
        out_shape=[
            jax.ShapeDtypeStruct(rows.shape, F32),
            jax.ShapeDtypeStruct(step.shape, F32),
        ],
        compiler_params=params(),
        cost_estimate=cost(10 ** 9, 7 * 10 ** 6),
        name="basis",
    )(rows, step, last)


def error_kernel(workers, basis_ref, inverse_ref, mine_ref, other_ref, *refs):
    merged_refs = refs[:PARTS]
    error_hbm, basis_hbm, second_hbm, error_ref, second_ref, error_sem, small_sem = refs[PARTS:]
    size = merged_refs[0].shape[0]
    small = whole_copies([(basis_ref, basis_hbm), (second_ref, second_hbm)], small_sem)
    small[0].start()
    product = both_halves(mine_ref[...], other_ref[...])
    second = short_dot(inverse_ref[...], product) * (1.0 / workers)
    second_ref[...] = second
    small[1].start()
    s_high, s_low = parts_of(second, 2)
    rights = jnp.concatenate([s_high, s_low, s_high], axis=0)
    copies = []
    for i in range(error_ref.shape[0] // CHUNK):
        start = i * CHUNK
        part = pl.ds(start, CHUNK)
        b_high, b_low = parts_of(basis_ref[:, part], 2)
        lefts = jnp.concatenate([b_high, b_high, b_low], axis=0)
        approx = dot(lefts, rights, ((0,), (0,)))
        merged = merged_refs[start // size][start % size:start % size + CHUNK, :]
        error_ref[part, :] = (merged - approx).astype(BF16)
        copies.append(pltpu.make_async_copy(
            error_ref.at[part, :], error_hbm.at[0, part, :], error_sem.at[i]))
        copies[i].start()
    for copy in copies + small:
        copy.wait()


def error_of(merged, basis, inverse, mine, other, workers):
    rank, width = basis.shape
    out = mine.shape[1]
    return pl.pallas_call(
        functools.partial(error_kernel, workers),
        in_specs=[VMEM] * (4 + PARTS),
        out_specs=[HBM] * 3,
        out_shape=[
            jax.ShapeDtypeStruct((1, width, out), BF16),
            jax.ShapeDtypeStruct((rank, width), F32),
            jax.ShapeDtypeStruct((rank, out), F32),
        ],
        scratch_shapes=[
            pltpu.VMEM((width, out), BF16),
            pltpu.VMEM((rank, out), F32),
            pltpu.SemaphoreType.DMA((width // CHUNK,)),
            pltpu.SemaphoreType.DMA((2,)),
        ],
        compiler_params=params(),
        cost_estimate=cost(2 * rank * width * out, 6 * width * out),
        name="error_next",
    )(basis, inverse, mine, other, *merged)


def local(sizes, *arguments):
    inputs, cotangent, error_prev, seed_q = (
        pltpu.with_memory_space_constraint(value, pltpu.HBM) for value in arguments)
    rounds = bits_of("sub", sizes["sub"]) + bits_of("dp", sizes["dp"])
    workers = 2 * sizes["sub"] * sizes["dp"]

    keep, send, x, c, e = term_halves(inputs, cotangent, error_prev, seed_q)
    first = keep + across(send)
    merged = merge(x, c, e, first)
    merged_other = [across(rows) for rows in merged]
    for bits in rounds:
        first = first + swapped(first, sizes, bits)
    other = across(first)

    product = product_of(first, merged, merged_other)
    rows, step = first_sweep(first, other)
    product = product + swapped(product, sizes, rounds[0])
    product, rows, step = lax.optimization_barrier((product, rows, step))
    rows, last = second_sweep(rows, step)
    product = product + swapped(product, sizes, rounds[1])
    product, rows, step, last = lax.optimization_barrier((product, rows, step, last))
    basis, inverse = basis_of(rows, step, last)
    for bits in rounds[2:]:
        product = product + swapped(product, sizes, bits)
    product, basis, inverse = lax.optimization_barrier((product, basis, inverse))
    return error_of(merged, basis, inverse, product, across(product), workers)


def solution(mesh):
    sizes = {axis: mesh.shape[axis] for axis in AXES}
    assert sizes["pair"] == 2

    def run(*args):
        return tuple(local(sizes, *args))

    return jax.shard_map(
        run,
        mesh=mesh,
        in_specs=(P(EVERYONE, None), P(EVERYONE, None), P(EVERYONE, None, None), P()),
        out_specs=(P(EVERYONE, None, None), P("groups", None), P("groups", None)),
        check_vma=False,
    )
```

```python
import functools

import jax
import jax.numpy as jnp
from jax import lax
from jax.experimental import pallas as pl
from jax.experimental.pallas import tpu as pltpu
from jax.sharding import PartitionSpec as P

AXES = ("dp", "sub", "pair")
EVERYONE = ("groups",) + AXES
VMEM_BYTES = 24 * 1024 * 1024
CHUNK = 256
GROUP = 4
PARTS = 8
BF16, F32 = jnp.bfloat16, jnp.float32
HBM = pl.BlockSpec(memory_space=pltpu.HBM)
ANY = pl.BlockSpec(memory_space=pl.ANY)
VMEM = pl.BlockSpec(memory_space=pltpu.VMEM)


def swapped(value, sizes, bits):
    pairs = []
    for dp in range(sizes["dp"]):
        for sub in range(sizes["sub"]):
            for pair in range(2):
                pairs.append(tuple(
                    (z * sizes["sub"] + x) * 2 + pair
                    for z, x in ((dp, sub), (dp ^ bits["dp"], sub ^ bits["sub"]))))
    return lax.ppermute(value, AXES, pairs)


def across(value):
    return lax.ppermute(value, "pair", [(0, 1), (1, 0)])


def bits_of(axis, size):
    assert size > 1 and size & (size - 1) == 0
    return [{"dp": 0, "sub": 0, axis: 1 << i} for i in range(size.bit_length() - 1)]


def parts_of(value, count):
    parts = []
    for _ in range(count):
        part = value.astype(BF16)
        parts.append(part)
        value = value - part.astype(F32)
    return parts


def dot(a, b, dims):
    return lax.dot_general(a, b, (dims, ((), ())), preferred_element_type=F32)


def params():
    return pltpu.CompilerParams(vmem_limit_bytes=VMEM_BYTES)


def cost(flops, nbytes):
    return pl.CostEstimate(flops=flops, bytes_accessed=nbytes, transcendentals=0)


def whole_copies(pairs, sems):
    return [pltpu.make_async_copy(pair[0], pair[1], sems.at[i]) for i, pair in enumerate(pairs)]


def row_parts(source, target, parts):
    block = target.shape[0] // parts
    rows = [pl.ds(i * block, block) for i in range(parts)]
    return [(source.at[part, :], target.at[part, :]) for part in rows]


def term_kernel(x_hbm, c_hbm, e_hbm, seed_hbm, keep_ref, send_ref, x_ref, c_ref, e_ref,
                seed_ref, term_ref, sems):
    copies = whole_copies(
        [(seed_hbm, seed_ref), (c_hbm, c_ref)] + row_parts(e_hbm.at[0], e_ref, 2)
        + row_parts(x_hbm, x_ref, 2), sems)
    for copy in copies:
        copy.start()
    rank = seed_ref.shape[0]
    tokens, width = x_ref.shape
    half = keep_ref.shape[0]
    copies[0].wait()
    copies[1].wait()
    seed = jnp.concatenate(parts_of(seed_ref[...], 3), axis=0)
    mixed = added(dot(seed, c_ref[...], ((1,), (1,))), rank)
    mixed = jnp.concatenate(parts_of(mixed, 3), axis=0)
    blocks = width // CHUNK
    for i in range(blocks):
        if i % (blocks // 2) == 0:
            copies[2 + i // (blocks // 2)].wait()
        part = pl.ds(i * CHUNK, CHUNK)
        term_ref[:, part] = added(dot(seed, e_ref[part, :], ((1,), (1,))), rank)
    for t in range(2):
        copies[4 + t].wait()
        own = mixed[:, t * (tokens // 2):(t + 1) * (tokens // 2)]
        rows = pl.ds(t * (tokens // 2), tokens // 2)
        for i in range(blocks):
            part = pl.ds(i * CHUNK, CHUNK)
            term_ref[:, part] += added(dot(own, x_ref[rows, part], ((1,), (0,))), rank)
    low = lax.axis_index("pair") == 0
    keep_ref[...] = jnp.where(low, term_ref[:half, :], term_ref[half:, :])
    send_ref[...] = jnp.where(low, term_ref[half:, :], term_ref[:half, :])


def added(stack, rank):
    total = stack[stack.shape[0] - rank:]
    for i in range(stack.shape[0] // rank - 2, -1, -1):
        total = total + stack[i * rank:(i + 1) * rank]
    return total


def term_halves(inputs, cotangent, error_prev, seed_q):
    tokens, width = inputs.shape
    out = cotangent.shape[1]
    rank = seed_q.shape[0]
    return pl.pallas_call(
        term_kernel,
        in_specs=[HBM] * 4,
        out_specs=[VMEM] * 5,
        out_shape=[
            jax.ShapeDtypeStruct((rank // 2, width), F32),
            jax.ShapeDtypeStruct((rank // 2, width), F32),
            jax.ShapeDtypeStruct((tokens, width), BF16),
            jax.ShapeDtypeStruct((tokens, out), BF16),
            jax.ShapeDtypeStruct((width, out), BF16),
        ],
        scratch_shapes=[
            pltpu.VMEM((rank, out), F32),
            pltpu.VMEM((rank, width), F32),
            pltpu.SemaphoreType.DMA((6,)),
        ],
        compiler_params=params(),
        cost_estimate=cost(6 * tokens * rank * width, 2 * tokens * width + 2 * width * out),
        name="term",
    )(inputs, cotangent, error_prev, seed_q)


def merge_kernel(x_ref, c_ref, e_ref, after_ref, *merged_refs):
    size = merged_refs[0].shape[0]
    for i in range(e_ref.shape[0] // CHUNK):
        start = i * CHUNK
        part = pl.ds(start, CHUNK)
        merged_refs[start // size][start % size:start % size + CHUNK, :] = (
            dot(x_ref[:, part], c_ref[...], ((0,), (0,))) + e_ref[part, :].astype(F32))


def merge(x, c, e, after):
    width, out = e.shape
    return pl.pallas_call(
        merge_kernel,
        in_specs=[VMEM] * 3 + [ANY],
        out_specs=[VMEM] * PARTS,
        out_shape=[jax.ShapeDtypeStruct((width // PARTS, out), F32)] * PARTS,
        compiler_params=params(),
        cost_estimate=cost(10 ** 8, 10 ** 6),
        name="merge",
    )(x, c, e, after)


def product_kernel(first_ref, *refs):
    mine_refs, other_refs, product_ref = refs[:PARTS], refs[PARTS:2 * PARTS], refs[2 * PARTS]
    rank, width = first_ref.shape
    size = mine_refs[0].shape[0]
    product = None
    for i in range(width // CHUNK):
        start = i * CHUNK
        rows = first_ref[:, start:start + CHUNK]
        f_high, f_low = parts_of(rows, 2)
        both = jnp.concatenate([f_high, f_low], axis=0)
        rows_here = slice(start % size, start % size + CHUNK)
        merged = mine_refs[start // size][rows_here, :] + other_refs[start // size][rows_here, :]
        m_high, m_low = parts_of(merged, 2)
        term = added(dot(both, m_high, ((1,), (0,))), rank) + dot(f_high, m_low, ((1,), (0,)))
        product = term if product is None else product + term
    product_ref[...] = product


def product_of(first, mine, other):
    rank, width = first.shape
    out = mine[0].shape[1]
    return pl.pallas_call(
        product_kernel,
        out_shape=jax.ShapeDtypeStruct((rank, out), F32),
        compiler_params=params(),
        cost_estimate=cost(2 * rank * width * out, 8 * width * out),
        name="product",
    )(first, *mine, *other)


def both_halves(mine, other):
    low = lax.axis_index("pair") == 0
    return jnp.concatenate([jnp.where(low, mine, other), jnp.where(low, other, mine)], axis=0)


def gram_blocks(rows):
    stack = jnp.concatenate(parts_of(rows, 3), axis=0)
    return dot(stack, stack, ((1,), (1,)))


def gram_of(blocks, rank):
    gram = None
    for i, j in ((2, 0), (0, 2), (1, 1), (1, 0), (0, 1), (0, 0)):
        term = blocks[i * rank:(i + 1) * rank, j * rank:(j + 1) * rank]
        gram = term if gram is None else gram + term
    return gram


def inverse_factor(gram):
    rank = gram.shape[0]
    row = lax.broadcasted_iota(jnp.int32, (rank, rank), 0)
    lane = lax.broadcasted_iota(jnp.int32, (rank, rank), 1)
    eye = jnp.where(row == lane, 1.0, 0.0).astype(F32)
    wide = jnp.concatenate([gram, eye], axis=1)
    index = lax.broadcasted_iota(jnp.int32, wide.shape, 0)
    scale = jnp.ones_like(wide)
    for base in range(0, rank, GROUP):
        columns = [
            jnp.broadcast_to(wide[:, k:k + 1], wide.shape) for k in range(base, base + GROUP)
        ]
        for j in range(GROUP):
            k = base + j
            pivot = columns[j][k:k + 1, :]
            factor = jnp.where(index > k, columns[j] * (1.0 / pivot), 0.0)
            for i in range(j + 1, GROUP):
                columns[i] = columns[i] - factor * columns[i][k:k + 1, :]
            wide = wide - factor * wide[k:k + 1, :]
            scale = jnp.where(index == k, lax.rsqrt(pivot), scale)
    return (wide * scale)[:, rank:]


def short_dot(left, right):
    a, b, c = parts_of(left, 3)
    d, e, f = parts_of(right, 3)
    lefts = jnp.concatenate([c, a, b, b, a, a], axis=1)
    rights = jnp.concatenate([d, f, e, d, e, d], axis=0)
    return dot(lefts, rights, ((1,), (0,)))


def first_sweep_kernel(mine_ref, other_ref, rows_ref, step_ref):
    rank, width = rows_ref.shape
    blocks = None
    for i in range(width // CHUNK):
        part = slice(i * CHUNK, (i + 1) * CHUNK)
        rows = both_halves(mine_ref[:, part], other_ref[:, part])
        rows_ref[:, part] = rows
        term = gram_blocks(rows)
        blocks = term if blocks is None else blocks + term
    step_ref[...] = inverse_factor(gram_of(blocks, rank))


def first_sweep(mine, other):
    half, width = mine.shape
    rank = 2 * half
    return pl.pallas_call(
        first_sweep_kernel,
        out_shape=[
            jax.ShapeDtypeStruct((rank, width), F32),
            jax.ShapeDtypeStruct((rank, rank), F32),
        ],
        compiler_params=params(),
        cost_estimate=cost(10 ** 9, 7 * 10 ** 6),
        name="first_sweep",
    )(mine, other)


def second_sweep_kernel(first_ref, step_ref, rows_ref, last_ref):
    rank, width = rows_ref.shape
    step = step_ref[...]
    blocks = None
    for i in range(width // CHUNK):
        part = slice(i * CHUNK, (i + 1) * CHUNK)
        rows = short_dot(step, first_ref[:, part])
        rows_ref[:, part] = rows
        term = gram_blocks(rows)
        blocks = term if blocks is None else blocks + term
    last_ref[...] = inverse_factor(gram_of(blocks, rank))


def second_sweep(rows, step):
    return pl.pallas_call(
        second_sweep_kernel,
        out_shape=[
            jax.ShapeDtypeStruct(rows.shape, F32),
            jax.ShapeDtypeStruct(step.shape, F32),
        ],
        compiler_params=params(),
        cost_estimate=cost(10 ** 9, 7 * 10 ** 6),
        name="second_sweep",
    )(rows, step)


def basis_kernel(rows_ref, step_ref, last_ref, basis_ref, inverse_ref):
    last = last_ref[...]
    for i in range(rows_ref.shape[1] // CHUNK):
        part = slice(i * CHUNK, (i + 1) * CHUNK)
        basis_ref[:, part] = short_dot(last, rows_ref[:, part])
    inverse_ref[...] = short_dot(last, step_ref[...])


def basis_of(rows, step, last):
    return pl.pallas_call(
        basis_kernel,
        out_shape=[
            jax.ShapeDtypeStruct(rows.shape, F32),
            jax.ShapeDtypeStruct(step.shape, F32),
        ],
        compiler_params=params(),
        cost_estimate=cost(10 ** 9, 7 * 10 ** 6),
        name="basis",
    )(rows, step, last)


def error_kernel(workers, basis_ref, inverse_ref, mine_ref, other_ref, *refs):
    merged_refs = refs[:PARTS]
    error_hbm, basis_hbm, second_hbm, error_ref, second_ref, error_sem, small_sem = refs[PARTS:]
    size = merged_refs[0].shape[0]
    small = whole_copies([(basis_ref, basis_hbm), (second_ref, second_hbm)], small_sem)
    small[0].start()
    product = both_halves(mine_ref[...], other_ref[...])
    second = short_dot(inverse_ref[...], product) * (1.0 / workers)
    second_ref[...] = second
    small[1].start()
    s_high, s_low = parts_of(second, 2)
    rights = jnp.concatenate([s_high, s_low, s_high], axis=0)
    copies = []
    for i in range(error_ref.shape[0] // CHUNK):
        start = i * CHUNK
        part = pl.ds(start, CHUNK)
        b_high, b_low = parts_of(basis_ref[:, part], 2)
        lefts = jnp.concatenate([b_high, b_high, b_low], axis=0)
        approx = dot(lefts, rights, ((0,), (0,)))
        merged = merged_refs[start // size][start % size:start % size + CHUNK, :]
        error_ref[part, :] = (merged - approx).astype(BF16)
        copies.append(pltpu.make_async_copy(
            error_ref.at[part, :], error_hbm.at[0, part, :], error_sem.at[i]))
        copies[i].start()
    for copy in copies + small:
        copy.wait()


def error_of(merged, basis, inverse, mine, other, workers):
    rank, width = basis.shape
    out = mine.shape[1]
    return pl.pallas_call(
        functools.partial(error_kernel, workers),
        in_specs=[VMEM] * (4 + PARTS),
        out_specs=[HBM] * 3,
        out_shape=[
            jax.ShapeDtypeStruct((1, width, out), BF16),
            jax.ShapeDtypeStruct((rank, width), F32),
            jax.ShapeDtypeStruct((rank, out), F32),
        ],
        scratch_shapes=[
            pltpu.VMEM((width, out), BF16),
            pltpu.VMEM((rank, out), F32),
            pltpu.SemaphoreType.DMA((width // CHUNK,)),
            pltpu.SemaphoreType.DMA((2,)),
        ],
        compiler_params=params(),
        cost_estimate=cost(2 * rank * width * out, 6 * width * out),
        name="error_next",
    )(basis, inverse, mine, other, *merged)


def local(sizes, *arguments):
    inputs, cotangent, error_prev, seed_q = (
        pltpu.with_memory_space_constraint(value, pltpu.HBM) for value in arguments)
    rounds = bits_of("sub", sizes["sub"]) + bits_of("dp", sizes["dp"])
    workers = 2 * sizes["sub"] * sizes["dp"]

    keep, send, x, c, e = term_halves(inputs, cotangent, error_prev, seed_q)
    first = keep + across(send)
    merged = merge(x, c, e, first)
    merged_other = [across(rows) for rows in merged]
    for bits in rounds:
        first = first + swapped(first, sizes, bits)
    other = across(first)

    product = product_of(first, merged, merged_other)
    product, other = lax.optimization_barrier((product, other))
    rows, step = first_sweep(first, other)
    product = product + swapped(product, sizes, rounds[0])
    product, rows, step = lax.optimization_barrier((product, rows, step))
    rows, last = second_sweep(rows, step)
    product = product + swapped(product, sizes, rounds[1])
    product, rows, step, last = lax.optimization_barrier((product, rows, step, last))
    basis, inverse = basis_of(rows, step, last)
    for bits in rounds[2:]:
        product = product + swapped(product, sizes, bits)
    product, basis, inverse = lax.optimization_barrier((product, basis, inverse))
    return error_of(merged, basis, inverse, product, across(product), workers)


def solution(mesh):
    sizes = {axis: mesh.shape[axis] for axis in AXES}
    assert sizes["pair"] == 2

    def run(*args):
        return tuple(local(sizes, *args))

    return jax.shard_map(
        run,
        mesh=mesh,
        in_specs=(P(EVERYONE, None), P(EVERYONE, None), P(EVERYONE, None, None), P()),
        out_specs=(P(EVERYONE, None, None), P("groups", None), P("groups", None)),
        check_vma=False,
    )
```
